32 devices in a mesh: storey: 8 (over z, x), plate: 4 (over y, core).
Axes of the slice: x: 2, y: 2, z: 4, core: 2. Of those that a mesh axis runs over, the one named last changes fastest.
Arguments:
- load: float32 [1024, 2048], P('storey', 'plate'), may hold values from -6 to 6
- disp: float32 [1024, 2048], P('storey', 'plate'), may hold values from -2 to 2
- mass: float32 [1024, 2048], P('storey', 'plate'), may hold values from 0.05 to 0.5
- wall_class: int32 [1024, 2048], P('storey', 'plate'), may hold values from 0 to 3
- class_stiff: float32 [4], replicated, may hold values from 0.5 to 2
- damper_map: int32 [1024, 2048], P('storey', 'plate'), may hold values from 0 to 63
- damper_coef: float32 [512], P('storey'), may hold values from 0.2 to 2
- band_tile: float32 [4096, 2048], P('storey', 'plate')
- panel_store: float32 [1024, 512], P('storey', 'plate')
- owner: int32 [8], P('storey'), may hold values from 0 to 3
- node_index: int32 [8, 128], P('storey', 'plate'), may hold values from 0 to 65535, as said below
Outputs:
- new_disp: float32 [1024, 2048], P('storey', 'plate')
- adjoint: float32 [1024, 2048], P('storey', 'plate')
- shear: float32 [1024], P('storey')
- grads: float32 [512], P('storey')
The draws below stay inside these ranges and needn't reach their ends.
Inputs may be any that keep to these rules, and one draw needn't show every extreme that they name: `node_index`: the 32 nodes of one plate block of a group lie in distinct rows of the block, each given as row * 512 + column within the block.
All inputs are finite; a program needn't handle non-finite values.
Results may differ from the reference program's by a relative error of at most 0.0003.
Values sent between devices are 32-bit elements; how exact they have to be, the bound alone decides.
A program may use at most 64 MiB of HBM per device.

```python
import math
import jax
import jax.numpy as jnp
from jax import lax

HC = 128
PC = 512
NODES_DEV = 32
DAMP_DEV = 64
CLASSES = 4
ITERS = 6
GROUPS = 8
NH = 1024
NP = 2048
DP = 128
DAMPERS = 512
N_PLATE = 4


def dominant_blocks(key, rows, cols, order, centre, spread):
    first, second = jax.random.split(key)
    local_row = lax.broadcasted_iota(jnp.int32, (rows, cols), 0) % order
    local_col = lax.broadcasted_iota(jnp.int32, (rows, cols), 1) % order
    off = jax.random.normal(first, (rows, cols), jnp.float32) * (spread / math.sqrt(order))
    main = centre * (1.0 + 0.2 * jax.random.uniform(second, (rows, cols), jnp.float32, -1.0, 1.0))
    return jnp.where(local_row == local_col, main, off)


def draw_band_tile(key, part):
    return dominant_blocks(jax.random.fold_in(key, 11), GROUPS * PC, NP, PC, 0.5, 0.25)


def draw_panel_store(key, part):
    return dominant_blocks(jax.random.fold_in(key, 23), GROUPS * DP, N_PLATE * DP, DP, 0.08, 0.12)


def draw_node_index(key, part):
    first, second = jax.random.split(jax.random.fold_in(key, 37))
    span = HC // NODES_DEV
    column = lax.broadcasted_iota(jnp.int32, (GROUPS, DP), 1)
    group = lax.broadcasted_iota(jnp.int32, (GROUPS, DP), 0)
    which = column % NODES_DEV
    row = which * span + jax.random.randint(first, (GROUPS, DP), 0, span, jnp.int32)
    col = jax.random.randint(second, (GROUPS, DP), 0, PC, jnp.int32)
    index = row * PC + col
    index = jnp.where((group == 0) & (column == 0), 0, index)
    index = jnp.where((group == 0) & (column == NODES_DEV - 1), HC * PC - 1, index)
    return index.astype(jnp.int32)


def set_ends(array, stream_key, least, top_value):
    dims = array.shape
    spot = [jax.random.randint(jax.random.fold_in(stream_key, axis), (), 0, dims[axis]) for axis in range(len(dims))]
    array = array.at[tuple(spot)].set(least)
    longest = dims.index(max(dims))
    spot[longest] = (spot[longest] + 1) % dims[longest]
    return array.at[tuple(spot)].set(top_value)


def block_scale(rng, extent, pieces, low, high):
    def one(axis_at, shards_of):
        heights = jax.random.uniform(jax.random.fold_in(jax.random.fold_in(rng, 6), axis_at), (shards_of,), jnp.float32, low / len(pieces), high / len(pieces))
        return jnp.repeat(jnp.exp(heights), extent[axis_at] // shards_of).reshape((-1,) + (1,) * (len(extent) - axis_at - 1))

    factor_of = one(*pieces[0])
    for cut in pieces[1:]:
        factor_of = factor_of * one(*cut)
    return factor_of


def bell_draw(rng, extent, scale, bound, shards=(), kind=jnp.bfloat16):
    array = jax.random.normal(rng, extent, jnp.float32) * scale
    if len(shards) > 0:
        array = block_scale(rng, extent, shards, -0.22, 0.18) * array
    return jnp.clip(array, min=-bound, max=bound).astype(kind)


def setup_inputs(seed: int = 0) -> dict:
    seeds = jax.random.split(jax.random.key(seed), 12)
    load = bell_draw(seeds[0], (NH, NP), 1.0, 6.0, ((0, 8), (1, 4)), jnp.float32)
    disp = bell_draw(seeds[1], (NH, NP), 0.3, 2.0, ((0, 8), (1, 4)), jnp.float32)
    mass = jnp.clip(jnp.exp(math.log(0.5) - 2.3025851 * jax.random.uniform(seeds[2], (NH, NP), jnp.float32) ** block_scale(seeds[2], (NH, NP), ((0, 8), (1, 4)), -0.2, 0.2)), 0.05, 0.5)
    wall_class = set_ends(jax.random.randint(seeds[3], (NH, NP), 0, CLASSES), jax.random.fold_in(seeds[3], 1), 0, CLASSES - 1).astype(jnp.int32)
    class_stiff = jnp.clip(jnp.exp(jax.random.uniform(seeds[4], (CLASSES,), jnp.float32, math.log(0.5), math.log(2.0))), 0.5, 2.0)
    damper_map = set_ends(jax.random.randint(seeds[5], (NH, NP), 0, DAMP_DEV), jax.random.fold_in(seeds[5], 1), 0, DAMP_DEV - 1).astype(jnp.int32)
    damper_coef = jnp.clip(jnp.exp(math.log(2.0) - 2.3025851 * jax.random.uniform(seeds[6], (DAMPERS,), jnp.float32) ** block_scale(seeds[6], (DAMPERS,), ((0, 8),), -0.2, 0.2)), 0.2, 2.0)
    band_tile = draw_band_tile(jax.random.fold_in(seeds[11], 71), 0)
    panel_store = draw_panel_store(jax.random.fold_in(seeds[11], 71), 0)
    owner = set_ends(jax.random.randint(seeds[9], (GROUPS,), 0, N_PLATE), jax.random.fold_in(seeds[9], 1), 0, N_PLATE - 1).astype(jnp.int32)
    node_index = draw_node_index(jax.random.fold_in(seeds[11], 71), 0)
    return {"load": load, "disp": disp, "mass": mass, "wall_class": wall_class, "class_stiff": class_stiff, "damper_map": damper_map, "damper_coef": damper_coef, "band_tile": band_tile, "panel_store": panel_store, "owner": owner, "node_index": node_index}


KF = 5.0 / 9.0
CM = 2.16
CD = 1.1
HIGH = lax.Precision.HIGHEST

def neighbours(field):
    padded = jnp.pad(field, 1)
    return padded[2:, 1:-1] + padded[:-2, 1:-1] + padded[1:-1, 2:] + padded[1:-1, :-2]

def reference(load, disp, mass, wall_class, class_stiff, damper_map, damper_coef, band_tile, panel_store, owner, node_index):
    row_ids = jnp.arange(NH, dtype=jnp.int32)
    group = row_ids // HC
    stiff = KF * class_stiff[wall_class]
    inertia = CM * mass
    damping = CD * damper_coef[group[:, None] * DAMP_DEV + damper_map]
    diag = 4.0 * stiff + inertia + damping
    tiles = band_tile.reshape(GROUPS, PC, N_PLATE, PC)
    panels = panel_store.reshape(GROUPS, DP, N_PLATE, DP)
    chosen = jnp.take_along_axis(panels, owner[:, None, None, None].astype(jnp.int32), axis=2)[:, :, 0, :]
    plate_of = jnp.arange(DP, dtype=jnp.int32) // NODES_DEV
    node_row = jnp.arange(GROUPS, dtype=jnp.int32)[:, None] * HC + node_index // PC
    node_col = plate_of[None, :] * PC + node_index % PC

    def correct(resid, transpose):
        scaled = (resid / diag).reshape(GROUPS, HC, N_PLATE, PC)
        form = 'shpc,sdpc->shpd' if transpose else 'shpc,scpd->shpd'
        result = jnp.einsum(form, scaled, tiles, precision=HIGH).reshape(NH, NP)
        values = resid[node_row, node_col]
        form_two = 'sji,sj->si' if transpose else 'sij,sj->si'
        coarse = jnp.einsum(form_two, chosen, values, precision=HIGH)
        return result.at[node_row, node_col].add(coarse)
    new_disp = disp
    resid = load - (diag * new_disp - stiff * neighbours(new_disp))
    for step in range(ITERS):
        new_disp = new_disp + correct(resid, False)
        if step < ITERS - 1:
            resid = load - (diag * new_disp - stiff * neighbours(new_disp))
    force = 8.0 / math.sqrt(NP * NH) * lax.optimization_barrier(jnp.sum(inertia * new_disp, axis=1))
    shear = jnp.cumsum(force[::-1])[::-1]
    drift = jnp.cumsum(shear) / NH
    target = inertia * drift[:, None]
    adjoint = jnp.zeros_like(load)
    resid = target
    for step in range(ITERS):
        adjoint = adjoint + correct(resid, True)
        if step < ITERS - 1:
            resid = target - (diag * adjoint - neighbours(stiff * adjoint))
    product = (adjoint * new_disp).reshape(-1)
    ids = (group[:, None] * DAMP_DEV + damper_map).reshape(-1)
    sums = jax.ops.segment_sum(product, ids, num_segments=DAMPERS)
    grads = -CD * 64.0 / math.sqrt(HC * NP / DAMP_DEV) * sums
    return (new_disp, adjoint, shear, grads)
```

```python
import functools
import math

import jax
import jax.numpy as jnp
from jax import lax
from jax.experimental import pallas as pl
from jax.experimental.pallas import tpu as pltpu
from jax.sharding import PartitionSpec as P

ITERS = 6
KF = 5.0 / 9.0
CM = 2.16
CD = 1.1
HIGH = lax.Precision.HIGHEST
MESH = pl.DeviceIdType.MESH
F32 = jnp.float32
BF16 = jnp.bfloat16
LANES = 128


def iota(shape, dim):
    return lax.broadcasted_iota(jnp.int32, shape, dim)


def to_row(col):
    n = col.shape[0]
    return jnp.sum(jnp.where(iota((n, n), 0) == iota((n, n), 1), col, 0.0), axis=0, keepdims=True)


def to_col(row):
    n = row.shape[1]
    return jnp.sum(jnp.where(iota((n, n), 0) == iota((n, n), 1), row, 0.0), axis=1, keepdims=True)


def split(value):
    hi = value.astype(BF16)
    return hi, (value - hi.astype(F32)).astype(BF16)


def wait_bytes(ref, sem):
    pltpu.make_async_copy(ref, ref, sem).wait()


def kernel(
    ns, np_,
    load, disp, mass, wall, cstiff, dmap, coef, tile, panel, owner, nidx,
    out_disp, out_adj, out_shear, out_grads,
    stiff, diag, rdiag, cm, place, x, r, q, z,
    t_hi, t_lo, tt_hi, tt_lo,
    pan_own, pan_left, pan_right, info_out, info_in,
    spk, sslots, snb, pslots,
    pk, slots, nbs,
    apk, fslots, tslots, gslots, seg,
    s_send, s_recv, n_send, n_recv, p_send, p_recv, i_send, i_recv,
    r_send, r_recv, rn_send, rn_recv, a_send, a_recv,
):
    rows, cols = load.shape
    nodes = nidx.shape[1]
    order = nodes * np_
    count = coef.shape[0]
    width = spk.shape[1]
    pieces = cols // LANES
    s = lax.axis_index("storey")
    b = lax.axis_index("plate")
    has = (s > 0, s < ns - 1)
    beside = (s - 1, s + 1)

    barrier = pltpu.get_barrier_semaphore()
    for d in range(1, np_):
        pl.semaphore_signal(barrier, inc=1, device_id=(s, (b + d) % np_), device_id_type=MESH)
    for d in range(1, ns):
        pl.semaphore_signal(barrier, inc=1, device_id=((s + d) % ns, b), device_id_type=MESH)
    for way in range(2):
        @pl.when(has[way])
        def _():
            for d in range(1, np_):
                pl.semaphore_signal(barrier, inc=1, device_id=(beside[way], (b + d) % np_), device_id_type=MESH)
    sides = jnp.minimum(s, 1) + jnp.minimum(ns - 1 - s, 1)
    pl.semaphore_wait(barrier, np_ - 1 + ns - 1 + sides * (np_ - 1))

    def push(src, dst, send, recv, where):
        pltpu.make_async_remote_copy(
            src_ref=src, dst_ref=dst, send_sem=send, recv_sem=recv, device_id=where, device_id_type=MESH
        ).start()

    def to_plates(src, dst, send, recv):
        for d in range(1, np_):
            push(src, dst, send, recv, (s, (b + d) % np_))

    to_plates(panel, pslots.at[b], p_send, p_recv)

    level = jnp.zeros((rows, cols), F32)
    for c in range(cstiff.shape[0]):
        level = jnp.where(wall[...] == c, cstiff[c], level)
    stiff[...] = KF * level
    spk[...] = jnp.zeros(spk.shape, F32)
    spk[0:1, 0:cols] = disp[0:1, :]
    spk[1:2, 0:cols] = disp[rows - 1 : rows, :]
    tiled = (iota((nodes, order), 1) % nodes == iota((nodes, order), 0)).astype(F32)
    spk[2:3, 0:order] = jnp.dot(nidx[...].astype(F32), tiled, precision=HIGH, preferred_element_type=F32)
    spk[3:4, 0:rows] = to_row(disp[:, 0:1])
    spk[4:5, 0:rows] = to_row(disp[:, cols - 1 : cols])
    spk[5:6, 0:rows] = to_row(stiff[:, 0:1])
    spk[6:7, 0:rows] = to_row(stiff[:, cols - 1 : cols])
    to_plates(spk, sslots.at[b], s_send, s_recv)
    for way in range(2):
        @pl.when(has[way])
        def _():
            push(spk, snb.at[1 - way], n_send.at[way], n_recv.at[1 - way], (beside[way], b))

        @pl.when(jnp.logical_not(has[way]))
        def _():
            snb[way] = jnp.zeros(snb.shape[1:], F32)
            info_in[way] = jnp.zeros(info_in.shape[1:], F32)
            nbs[0, way] = jnp.zeros(nbs.shape[2:], F32)
            nbs[1, way] = jnp.zeros(nbs.shape[2:], F32)

    cm[...] = CM * mass[...]

    def lookup(i, carry):
        part = pl.ds(pl.multiple_of(i * 8, 8), 8)
        ids = dmap[part, :]
        value = jnp.zeros(ids.shape, F32)
        for d in range(count):
            value = jnp.where(ids == d, coef[d], value)
        total = 4.0 * stiff[part, :] + cm[part, :] + CD * value
        diag[part, :] = total
        rdiag[part, :] = 1.0 / total
        return carry

    lax.fori_loop(0, rows // 8, lookup, 0)
    t_hi[...], t_lo[...] = split(tile[...])
    tt_hi[...], tt_lo[...] = split(tile[...].T)

    pslots[b] = panel[...]
    sslots[b] = spk[...]
    wait_bytes(sslots.at[pl.ds(0, np_ - 1)], s_recv)
    wait_bytes(pslots.at[pl.ds(0, np_ - 1)], p_recv)
    for way in range(2):
        @pl.when(has[way])
        def _():
            wait_bytes(snb.at[way], n_recv.at[way])
            wait_bytes(spk, n_send.at[way])
    wait_bytes(sslots.at[pl.ds(0, np_ - 1)], s_send)
    wait_bytes(pslots.at[pl.ds(0, np_ - 1)], p_send)

    root = owner[0]
    used = jnp.zeros((order, order), F32)
    lane_node = iota((1, order), 1) // nodes
    where_all = jnp.zeros((1, order), F32)
    for j in range(np_):
        used = jnp.where(root == j, pslots[j], used)
        where_all = jnp.where(lane_node == j, sslots[j, 2:3, 0:order], where_all)
    at = where_all.astype(jnp.int32)
    shift = cols.bit_length() - 1
    at_row = jnp.right_shift(at, shift)
    at_col = jnp.bitwise_and(at, cols - 1)
    at_row_col = to_col(at_row.astype(F32)).astype(jnp.int32)
    wide = (order, np_ * rows)
    spread = (
        (iota(wide, 1) % rows == at_row_col) & (iota(wide, 1) // rows == iota(wide, 0) // nodes)
    ).astype(F32)
    tall = (rows, order)
    at_h = iota(tall, 0) == at_row
    pick_own = (at_h & (lane_node == b)).astype(F32)
    pick_left = (at_h & (lane_node == b - 1) & (at_col == cols - 1)).astype(F32)
    pick_right = (at_h & (lane_node == b + 1) & (at_col == 0)).astype(F32)
    col_of = jnp.sum(pick_own * (at_col + 1).astype(F32), axis=1, keepdims=True).astype(jnp.int32) - 1
    place[...] = (iota((rows, cols), 1) == col_of).astype(F32)
    left_slot = jnp.maximum(b - 1, 0)
    right_slot = jnp.minimum(b + 1, np_ - 1)
    stiff_left = to_col(sslots[left_slot][6:7, 0:rows])
    stiff_right = to_col(sslots[right_slot][5:6, 0:rows])
    stiff_own = jnp.sum(place[...] * stiff[...], axis=1, keepdims=True)
    info_out[...] = jnp.zeros(info_out.shape, F32)
    info_out[4:5, 0:cols] = place[0:1, :]
    info_out[5:6, 0:cols] = place[rows - 1 : rows, :]
    for mode in range(2):
        grown = jnp.dot(used.T if mode else used, spread, precision=HIGH, preferred_element_type=F32)
        own = jnp.dot(pick_own, grown, precision=HIGH, preferred_element_type=F32)
        left = jnp.dot(pick_left, grown, precision=HIGH, preferred_element_type=F32)
        right = jnp.dot(pick_right, grown, precision=HIGH, preferred_element_type=F32)
        pan_own[mode] = own
        pan_left[mode] = left * stiff_left if mode else left
        pan_right[mode] = right * stiff_right if mode else right
        edge = own * stiff_own if mode else own
        info_out[2 * mode : 2 * mode + 1, 0 : np_ * rows] = edge[0:1, :]
        info_out[2 * mode + 1 : 2 * mode + 2, 0 : np_ * rows] = edge[rows - 1 : rows, :]
    for way in range(2):
        @pl.when(has[way])
        def _():
            push(info_out, info_in.at[1 - way], i_send.at[way], i_recv.at[1 - way], (beside[way], b))

    eye = (iota((rows, rows), 0) == iota((rows, rows), 1)).astype(F32)
    lane = iota((rows, cols), 1)
    line = iota((rows, cols), 0)

    def neighbours(v, top, bottom, left, right):
        above = jnp.where(line == 0, top, pltpu.roll(v, 1, 0))
        below = jnp.where(line == rows - 1, bottom, pltpu.roll(v, rows - 1, 0))
        west = jnp.where(lane == 0, left, pltpu.roll(v, 1, 1))
        east = jnp.where(lane == cols - 1, right, pltpu.roll(v, cols - 1, 1))
        return above + below + west + east

    def send_round(mode, par):
        resid = r[...]
        hi, lo = split(resid * rdiag[...])
        wh, wl = (tt_hi, tt_lo) if mode else (t_hi, t_lo)
        both = jnp.dot(jnp.concatenate([hi, lo], axis=0), wh[...], preferred_element_type=F32)
        band = both[:rows] + both[rows:] + jnp.dot(hi, wl[...], preferred_element_type=F32)
        z[...] = x[...] + band
        here = pk.at[par]
        edge = (lambda *at: z[at] * stiff[at]) if mode else (lambda *at: z[at])
        first, last = edge(slice(0, 1), slice(None)), edge(slice(rows - 1, rows), slice(None))
        for t in range(pieces):
            here[1, t : t + 1, :] = first[:, t * LANES : (t + 1) * LANES]
            here[1, pieces + t : pieces + t + 1, :] = last[:, t * LANES : (t + 1) * LANES]
        here[0, 0:1, :] = to_row(jnp.sum(resid * place[...], axis=1, keepdims=True))
        here[0, 1:2, :] = to_row(edge(slice(None), slice(0, 1)))
        here[0, 2:3, :] = to_row(edge(slice(None), slice(cols - 1, cols)))
        to_plates(here.at[0], slots.at[par, b], r_send.at[par], r_recv.at[par])
        for way in range(2):
            @pl.when(has[way])
            def _():
                for d in range(np_):
                    push(
                        here.at[0], nbs.at[par, 1 - way, b], rn_send.at[par, way],
                        rn_recv.at[par, 1 - way], (beside[way], (b + d) % np_),
                    )
                push(
                    here.at[1], nbs.at[par, 1 - way, np_], rn_send.at[par, way],
                    rn_recv.at[par, 1 - way], (beside[way], b),
                )
        slots[par, b] = here[0]

    def wait_round(par):
        wait_bytes(slots.at[par, pl.ds(0, np_ - 1)], r_recv.at[par])
        wait_bytes(slots.at[par, pl.ds(0, np_ - 1)], r_send.at[par])
        for way in range(2):
            @pl.when(has[way])
            def _():
                wait_bytes(nbs.at[par, way], rn_recv.at[par, way])
                wait_bytes(nbs.at[par, way], rn_send.at[par, way])

    def applied(mat, mode, par, extra=None):
        total = extra
        for j in range(np_):
            term = mat[mode, :, j * rows : (j + 1) * rows] * slots[par, j, 0:1, :]
            total = term if total is None else total + term
        return jnp.sum(total, axis=1, keepdims=True)

    def finish(mode, par):
        x[...] = z[...] + applied(pan_own, mode, par) * place[...]

    def side_row(mode, par, way):
        pan_row = 2 * mode + (1 - way)
        total = jnp.zeros((1, rows), F32)
        for j in range(np_):
            total = total + info_in[way, pan_row : pan_row + 1, j * rows : (j + 1) * rows] * nbs[par, way, j, 0:1, :]
        value = jnp.sum(total, axis=1, keepdims=True)
        base = pieces * (1 - way)
        got = jnp.concatenate([nbs[par, way, np_, base + t : base + t + 1, :] for t in range(pieces)], axis=1)
        return got + value * info_in[way, 4 + (1 - way) : 5 + (1 - way), 0:cols]

    def halos(mode, par):
        west = jnp.where(b > 0, eye * slots[par, left_slot, 2:3, :], 0.0)
        east = jnp.where(b < np_ - 1, eye * slots[par, right_slot, 1:2, :], 0.0)
        return (
            side_row(mode, par, 0),
            side_row(mode, par, 1),
            applied(pan_left, mode, par, west),
            applied(pan_right, mode, par, east),
        )

    x[...] = disp[...]
    west = jnp.where(b > 0, to_col(sslots[left_slot][4:5, 0:rows]), 0.0)
    east = jnp.where(b < np_ - 1, to_col(sslots[right_slot][3:4, 0:rows]), 0.0)
    around = neighbours(disp[...], snb[0, 1:2, 0:cols], snb[1, 0:1, 0:cols], west, east)
    r[...] = load[...] - (diag[...] * disp[...] - stiff[...] * around)

    def primal(k, carry):
        par = lax.rem(k, 2)
        send_round(0, par)

        @pl.when(k == 0)
        def _():
            for way in range(2):
                @pl.when(has[way])
                def _():
                    wait_bytes(info_in.at[way], i_recv.at[way])
                    wait_bytes(info_out, i_send.at[way])

        wait_round(par)
        finish(0, par)
        v = x[...]
        r[...] = load[...] - (diag[...] * v - stiff[...] * neighbours(v, *halos(0, par)))
        return carry

    lax.fori_loop(0, ITERS - 1, primal, 0)
    par = (ITERS - 1) % 2
    send_round(0, par)
    wait_round(par)
    finish(0, par)
    out_disp[...] = x[...]

    apk[...] = jnp.zeros(apk.shape, F32)
    apk[0, 0:1, :] = to_row(jnp.sum(cm[...] * x[...], axis=1, keepdims=True))
    to_plates(apk.at[0], fslots.at[b], a_send.at[0], a_recv.at[0])
    fslots[b] = apk[0]
    wait_bytes(fslots.at[pl.ds(0, np_ - 1)], a_recv.at[0])
    wait_bytes(fslots.at[pl.ds(0, np_ - 1)], a_send.at[0])
    force = fslots[0, 0:1, :]
    for j in range(1, np_):
        force = force + fslots[j, 0:1, :]
    force = force * (8.0 / math.sqrt(cols * np_ * rows * ns))
    apk[1, 0:1, :] = force
    for d in range(1, ns):
        push(apk.at[1], tslots.at[s], a_send.at[1], a_recv.at[1], ((s + d) % ns, b))
    tslots[s] = apk[1]
    wait_bytes(tslots.at[pl.ds(0, ns - 1)], a_recv.at[1])
    wait_bytes(tslots.at[pl.ds(0, ns - 1)], a_send.at[1])
    over = jnp.zeros((1, rows), F32)
    under = jnp.zeros((1, rows), F32)
    weight = (iota((1, rows), 1) + 1).astype(F32)
    for j in range(ns):
        line_j = tslots[j, 0:1, :]
        over = over + jnp.where(s < j, line_j, 0.0)
        under = under + line_j * (jnp.where(s > j, weight, 0.0) + (rows * jnp.minimum(s, j)).astype(F32))
    over = jnp.sum(over, axis=1, keepdims=True)
    under = jnp.sum(under, axis=1, keepdims=True)
    hh, ll = iota((rows, rows), 0), iota((rows, rows), 1)
    shear = jnp.sum(jnp.where(ll >= hh, force, 0.0), axis=1, keepdims=True) + over
    out_shear[...] = to_row(shear)
    local = jnp.sum(force * (jnp.minimum(hh, ll) + 1).astype(F32), axis=1, keepdims=True)
    step = (iota((rows, 1), 0) + 1).astype(F32)
    drift = (local + step * over + under) * (1.0 / (rows * ns))
    q[...] = cm[...] * drift
    r[...] = q[...]
    x[...] = jnp.zeros((rows, cols), F32)

    def adjoint(k, carry):
        par = lax.rem(k, 2)
        send_round(1, par)
        wait_round(par)
        finish(1, par)
        v = x[...]
        r[...] = q[...] - (diag[...] * v - neighbours(stiff[...] * v, *halos(1, par)))
        return carry

    lax.fori_loop(0, ITERS - 1, adjoint, 0)
    send_round(1, par)
    wait_round(par)
    finish(1, par)
    out_adj[...] = x[...]

    z[...] = x[...] * out_disp[...]
    group = 8
    for first in range(0, count, group):
        def gather(i, accs):
            part = pl.ds(pl.multiple_of(i * 8, 8), 8)
            ids, vals = dmap[part, :], z[part, :]
            res = []
            for d in range(group):
                kept = jnp.where(ids == first + d, vals, 0.0)
                acc = accs[d]
                for t in range(pieces):
                    acc = acc + kept[:, t * LANES : (t + 1) * LANES]
                res.append(acc)
            return tuple(res)

        accs = lax.fori_loop(0, rows // 8, gather, tuple(jnp.zeros((8, LANES), F32) for _ in range(group)))
        for d in range(group):
            seg[first + d : first + d + 1, :] = jnp.sum(accs[d], axis=0, keepdims=True)
    apk[2, 0:1, 0:count] = to_row(jnp.sum(seg[...], axis=1, keepdims=True))
    to_plates(apk.at[2], gslots.at[b], a_send.at[2], a_recv.at[2])
    gslots[b] = apk[2]
    wait_bytes(gslots.at[pl.ds(0, np_ - 1)], a_recv.at[2])
    wait_bytes(gslots.at[pl.ds(0, np_ - 1)], a_send.at[2])
    sums = gslots[0, 0:1, 0:count]
    for j in range(1, np_):
        sums = sums + gslots[j, 0:1, 0:count]
    out_grads[...] = sums * (-CD * 64.0 / math.sqrt(rows * cols * np_ / count))


def on_device(load, disp, mass, wall_class, class_stiff, damper_map, damper_coef, band_tile, panel_store, owner, node_index):
    rows, cols = load.shape
    ns = lax.axis_size("storey")
    np_ = lax.axis_size("plate")
    nodes = node_index.shape[1]
    order = nodes * np_
    count = damper_coef.shape[0]
    width = max(cols, order, rows)
    wide = max(cols, np_ * rows)
    field = pltpu.VMEM((rows, cols), F32)
    square = pltpu.VMEM((cols, cols), BF16)
    grown = pltpu.VMEM((2, rows, np_ * rows), F32)
    dma = pltpu.SemaphoreType.DMA
    vmem = pl.BlockSpec(memory_space=pltpu.VMEM)
    smem = pl.BlockSpec(memory_space=pltpu.SMEM)
    new_disp, adj, shear, grads = pl.pallas_call(
        functools.partial(kernel, ns, np_),
        out_shape=(
            jax.ShapeDtypeStruct((rows, cols), F32),
            jax.ShapeDtypeStruct((rows, cols), F32),
            jax.ShapeDtypeStruct((1, rows), F32),
            jax.ShapeDtypeStruct((1, count), F32),
        ),
        in_specs=[vmem, vmem, vmem, vmem, smem, vmem, smem, vmem, vmem, smem, vmem],
        out_specs=(vmem, vmem, vmem, vmem),
        scratch_shapes=[field] * 9
        + [square] * 4
        + [grown] * 3
        + [
            pltpu.VMEM((8, wide), F32),
            pltpu.VMEM((2, 8, wide), F32),
            pltpu.VMEM((8, width), F32),
            pltpu.VMEM((np_, 8, width), F32),
            pltpu.VMEM((2, 8, width), F32),
            pltpu.VMEM((np_, order, order), F32),
            pltpu.VMEM((2, 2, 8, LANES), F32),
            pltpu.VMEM((2, np_, 8, LANES), F32),
            pltpu.VMEM((2, 2, np_ + 1, 8, LANES), F32),
            pltpu.VMEM((3, 8, LANES), F32),
            pltpu.VMEM((np_, 8, LANES), F32),
            pltpu.VMEM((ns, 8, LANES), F32),
            pltpu.VMEM((np_, 8, LANES), F32),
            pltpu.VMEM((count, LANES), F32),
            dma, dma, dma((2,)), dma((2,)), dma, dma, dma((2,)), dma((2,)),
            dma((2,)), dma((2,)), dma((2, 2)), dma((2, 2)), dma((3,)), dma((3,)),
        ],
        compiler_params=pltpu.CompilerParams(
            collective_id=0, has_side_effects=True, vmem_limit_bytes=48 * 1024 * 1024
        ),
    )(load, disp, mass, wall_class, class_stiff, damper_map, damper_coef, band_tile, panel_store, owner, node_index)
    return new_disp, adj, shear.reshape(rows), grads.reshape(count)


def solution(mesh):
    grid = P("storey", "plate")
    return jax.shard_map(
        on_device,
        mesh=mesh,
        in_specs=(grid, grid, grid, grid, P(), grid, P("storey"), grid, grid, P("storey"), grid),
        out_specs=(grid, grid, P("storey"), P("storey")),
        check_vma=False,
    )
```

```python
import functools
import math

import jax
import jax.numpy as jnp
from jax import lax
from jax.experimental import pallas as pl
from jax.experimental.pallas import tpu as pltpu
from jax.sharding import PartitionSpec as P

ITERS = 6
KF = 5.0 / 9.0
CM = 2.16
CD = 1.1
HIGH = lax.Precision.HIGHEST
MESH = pl.DeviceIdType.MESH
F32 = jnp.float32
BF16 = jnp.bfloat16
LANES = 128
FULL = 63 * 1024 * 1024


def iota(shape, dim):
    return lax.broadcasted_iota(jnp.int32, shape, dim)


def to_row(col):
    n = col.shape[0]
    return jnp.sum(jnp.where(iota((n, n), 0) == iota((n, n), 1), col, 0.0), axis=0, keepdims=True)


def to_col(row):
    n = row.shape[1]
    return jnp.sum(jnp.where(iota((n, n), 0) == iota((n, n), 1), row, 0.0), axis=1, keepdims=True)


def split(value):
    hi = value.astype(BF16)
    return hi, (value - hi.astype(F32)).astype(BF16)


def wait_bytes(ref, sem):
    pltpu.make_async_copy(ref, ref, sem).wait()


def kernel(
    ns, np_,
    load_in, disp_in, mass_in, wall_in, cstiff, dmap_in, coef, tile_in, panel, owner, nidx,
    out_disp, out_adj, out_shear, out_grads,
    load, disp, mass, wall, dmap, tile, in_sem, out_sem, found,
    stiff, diag, rdiag, cm, place, x, r, q, z,
    k_own, k_up, k_down,
    t_hi, t_lo, tt_hi, tt_lo,
    pan_own, pan_left, pan_right, info_out, info_in,
    spk, sslots, snb, pslots,
    gpk, cpk, rpk, slots, nbs, cols_in, rows_in,
    apk, fslots, tslots, gslots, seg,
    s_send, s_recv, n_send, n_recv, p_send, p_recv, i_send, i_recv,
    r_send, r_recv, rn_send, rn_recv, c_send, c_recv, e_send, e_recv, a_send, a_recv,
):
    rows, cols = load.shape
    nodes = nidx.shape[1]
    order = nodes * np_
    count = coef.shape[0]
    width = spk.shape[1]
    pieces = cols // LANES
    s = lax.axis_index("storey")
    b = lax.axis_index("plate")
    has = (s > 0, s < ns - 1)
    beside = (s - 1, s + 1)

    ways = ((wall_in, wall), (disp_in, disp), (mass_in, mass), (dmap_in, dmap), (tile_in, tile), (load_in, load))
    loads = [pltpu.make_async_copy(src, dst, in_sem.at[i]) for i, (src, dst) in enumerate(ways)]
    loads.append(pltpu.make_async_copy(panel, pslots.at[b], in_sem.at[len(ways)]))
    for copy in loads:
        copy.start()

    barrier = pltpu.get_barrier_semaphore()
    for d in range(1, np_):
        pl.semaphore_signal(barrier, inc=1, device_id=(s, (b + d) % np_), device_id_type=MESH)
    for d in range(1, ns):
        pl.semaphore_signal(barrier, inc=1, device_id=((s + d) % ns, b), device_id_type=MESH)
    for way in range(2):
        @pl.when(has[way])
        def _():
            for d in range(1, np_):
                pl.semaphore_signal(barrier, inc=1, device_id=(beside[way], (b + d) % np_), device_id_type=MESH)
    sides = jnp.minimum(s, 1) + jnp.minimum(ns - 1 - s, 1)
    pl.semaphore_wait(barrier, np_ - 1 + ns - 1 + sides * (np_ - 1))

    def push(src, dst, send, recv, where):
        pltpu.make_async_remote_copy(
            src_ref=src, dst_ref=dst, send_sem=send, recv_sem=recv, device_id=where, device_id_type=MESH
        ).start()

    def to_plates(src, dst, send, recv):
        for d in range(1, np_):
            push(src, dst, send, recv, (s, (b + d) % np_))

    to_plates(panel, pslots.at[b], p_send, p_recv)

    loads[0].wait()
    loads[1].wait()

    level = jnp.zeros((rows, cols), F32)
    for c in range(cstiff.shape[0]):
        level = jnp.where(wall[...] == c, cstiff[c], level)
    stiff[...] = KF * level
    spk[...] = jnp.zeros(spk.shape, F32)
    spk[0:1, 0:cols] = disp[0:1, :]
    spk[1:2, 0:cols] = disp[rows - 1 : rows, :]
    tiled = (iota((nodes, order), 1) % nodes == iota((nodes, order), 0)).astype(F32)
    spk[2:3, 0:order] = jnp.dot(nidx[...].astype(F32), tiled, precision=HIGH, preferred_element_type=F32)
    spk[3:4, 0:rows] = to_row(disp[:, 0:1])
    spk[4:5, 0:rows] = to_row(disp[:, cols - 1 : cols])
    spk[5:6, 0:rows] = to_row(stiff[:, 0:1])
    spk[6:7, 0:rows] = to_row(stiff[:, cols - 1 : cols])
    to_plates(spk, sslots.at[b], s_send, s_recv)
    for way in range(2):
        @pl.when(has[way])
        def _():
            push(spk, snb.at[1 - way], n_send.at[way], n_recv.at[1 - way], (beside[way], b))

        @pl.when(jnp.logical_not(has[way]))
        def _():
            snb[way] = jnp.zeros(snb.shape[1:], F32)
            info_in[way] = jnp.zeros(info_in.shape[1:], F32)
            for i in range(2):
                nbs[i, way] = jnp.zeros(nbs.shape[2:], F32)
                rows_in[i, way] = jnp.zeros(rows_in.shape[2:], F32)

    flank = (b > 0, b < np_ - 1)
    flanking = (b - 1, b + 1)
    for side in range(2):
        @pl.when(jnp.logical_not(flank[side]))
        def _():
            for i in range(2):
                cols_in[i, side] = jnp.zeros(cols_in.shape[2:], F32)

    loads[2].wait()
    loads[3].wait()
    cm[...] = CM * mass[...]

    def lookup(i, carry):
        part = pl.ds(pl.multiple_of(i * 8, 8), 8)
        ids = dmap[part, :]
        value = jnp.zeros(ids.shape, F32)
        for d in range(count):
            value = jnp.where(ids == d, coef[d], value)
        total = 4.0 * stiff[part, :] + cm[part, :] + CD * value
        diag[part, :] = total
        rdiag[part, :] = 1.0 / total
        return carry

    lax.fori_loop(0, rows // 8, lookup, 0)
    loads[4].wait()
    t_hi[...], t_lo[...] = split(tile[...])
    tt_hi[...], tt_lo[...] = split(tile[...].T)

    loads[5].wait()
    loads[6].wait()
    sslots[b] = spk[...]
    wait_bytes(sslots.at[pl.ds(0, np_ - 1)], s_recv)
    wait_bytes(pslots.at[pl.ds(0, np_ - 1)], p_recv)
    for way in range(2):
        @pl.when(has[way])
        def _():
            wait_bytes(snb.at[way], n_recv.at[way])
            wait_bytes(spk, n_send.at[way])
    wait_bytes(sslots.at[pl.ds(0, np_ - 1)], s_send)
    wait_bytes(pslots.at[pl.ds(0, np_ - 1)], p_send)

    root = owner[0]
    used = jnp.zeros((order, order), F32)
    lane_node = iota((1, order), 1) // nodes
    where_all = jnp.zeros((1, order), F32)
    for j in range(np_):
        used = jnp.where(root == j, pslots[j], used)
        where_all = jnp.where(lane_node == j, sslots[j, 2:3, 0:order], where_all)
    at = where_all.astype(jnp.int32)
    shift = cols.bit_length() - 1
    at_row = jnp.right_shift(at, shift)
    at_col = jnp.bitwise_and(at, cols - 1)
    at_row_col = to_col(at_row.astype(F32)).astype(jnp.int32)
    wide = (order, np_ * rows)
    spread = (
        (iota(wide, 1) % rows == at_row_col) & (iota(wide, 1) // rows == iota(wide, 0) // nodes)
    ).astype(F32)
    tall = (rows, order)
    at_h = iota(tall, 0) == at_row
    pick_own = (at_h & (lane_node == b)).astype(F32)
    pick_left = (at_h & (lane_node == b - 1) & (at_col == cols - 1)).astype(F32)
    pick_right = (at_h & (lane_node == b + 1) & (at_col == 0)).astype(F32)
    col_of = jnp.sum(pick_own * (at_col + 1).astype(F32), axis=1, keepdims=True).astype(jnp.int32) - 1
    place[...] = (iota((rows, cols), 1) == col_of).astype(F32)
    left_slot = jnp.maximum(b - 1, 0)
    right_slot = jnp.minimum(b + 1, np_ - 1)
    stiff_left = to_col(sslots[left_slot][6:7, 0:rows])
    stiff_right = to_col(sslots[right_slot][5:6, 0:rows])
    stiff_own = jnp.sum(place[...] * stiff[...], axis=1, keepdims=True)
    info_out[...] = jnp.zeros(info_out.shape, F32)
    info_out[4:5, 0:cols] = place[0:1, :]
    info_out[5:6, 0:cols] = place[rows - 1 : rows, :]
    for mode in range(2):
        grown = jnp.dot(used.T if mode else used, spread, precision=HIGH, preferred_element_type=F32)
        own = jnp.dot(pick_own, grown, precision=HIGH, preferred_element_type=F32)
        left = jnp.dot(pick_left, grown, precision=HIGH, preferred_element_type=F32)
        right = jnp.dot(pick_right, grown, precision=HIGH, preferred_element_type=F32)
        pan_own[mode] = own
        pan_left[mode] = left * stiff_left if mode else left
        pan_right[mode] = right * stiff_right if mode else right
        edge = own * stiff_own if mode else own
        info_out[2 * mode : 2 * mode + 1, 0 : np_ * rows] = edge[0:1, :]
        info_out[2 * mode + 1 : 2 * mode + 2, 0 : np_ * rows] = edge[rows - 1 : rows, :]
    for way in range(2):
        @pl.when(has[way])
        def _():
            push(info_out, info_in.at[1 - way], i_send.at[way], i_recv.at[1 - way], (beside[way], b))

    eye = (iota((rows, rows), 0) == iota((rows, rows), 1)).astype(F32)
    lane = iota((rows, cols), 1)
    line = iota((rows, cols), 0)

    def sideways(v):
        return jnp.where(lane == 0, 0.0, pltpu.roll(v, 1, 1)) + jnp.where(
            lane == cols - 1, 0.0, pltpu.roll(v, cols - 1, 1)
        )

    def neighbours(v, top, bottom, left, right):
        above = jnp.where(line == 0, top, pltpu.roll(v, 1, 0))
        below = jnp.where(line == rows - 1, bottom, pltpu.roll(v, rows - 1, 0))
        west = jnp.where(lane == 0, left, pltpu.roll(v, 1, 1))
        east = jnp.where(lane == cols - 1, right, pltpu.roll(v, cols - 1, 1))
        return above + below + west + east

    spot = place[...]
    k_own[0] = stiff[...] * sideways(spot) - diag[...] * spot
    k_up[0] = jnp.where(line == 0, 0.0, stiff[...] * pltpu.roll(spot, 1, 0))
    k_down[0] = jnp.where(line == rows - 1, 0.0, stiff[...] * pltpu.roll(spot, rows - 1, 0))
    held = stiff[...] * spot
    k_own[1] = sideways(held) - diag[...] * spot
    k_up[1] = jnp.where(line == 0, 0.0, pltpu.roll(held, 1, 0))
    k_down[1] = jnp.where(line == rows - 1, 0.0, pltpu.roll(held, rows - 1, 0))

    def send_round(mode, par, edges):
        resid = r[...]
        gpk[par, 0:1, :] = to_row(jnp.sum(resid * place[...], axis=1, keepdims=True))
        for way in range(2):
            @pl.when(has[way])
            def _():
                for d in range(np_):
                    push(
                        gpk.at[par], nbs.at[par, 1 - way, b], rn_send.at[par, way],
                        rn_recv.at[par, 1 - way], (beside[way], (b + d) % np_),
                    )
        to_plates(gpk.at[par], slots.at[par, b], r_send.at[par], r_recv.at[par])
        slots[par, b] = gpk[par]
        hi, lo = split(resid * rdiag[...])
        wh, wl = (tt_hi, tt_lo) if mode else (t_hi, t_lo)
        both = jnp.dot(jnp.concatenate([hi, lo], axis=0), wh[...], preferred_element_type=F32)
        band = both[:rows] + both[rows:] + jnp.dot(hi, wl[...], preferred_element_type=F32)
        z[...] = x[...] + band
        if not edges:
            return
        edge = (lambda *at: z[at] * stiff[at]) if mode else (lambda *at: z[at])
        first, last = edge(slice(0, 1), slice(None)), edge(slice(rows - 1, rows), slice(None))
        for t in range(pieces):
            rpk[par, t : t + 1, :] = first[:, t * LANES : (t + 1) * LANES]
            rpk[par, pieces + t : pieces + t + 1, :] = last[:, t * LANES : (t + 1) * LANES]
        for way in range(2):
            @pl.when(has[way])
            def _():
                push(
                    rpk.at[par], rows_in.at[par, 1 - way], e_send.at[par, way],
                    e_recv.at[par, 1 - way], (beside[way], b),
                )
        cpk[par, 0:1, :] = to_row(edge(slice(None), slice(0, 1)))
        cpk[par, 1:2, :] = to_row(edge(slice(None), slice(cols - 1, cols)))
        for side in range(2):
            @pl.when(flank[side])
            def _():
                push(
                    cpk.at[par], cols_in.at[par, 1 - side], c_send.at[par, side],
                    c_recv.at[par, 1 - side], (s, flanking[side]),
                )

    def wait_round(par, edges):
        wait_bytes(slots.at[par, pl.ds(0, np_ - 1)], r_recv.at[par])
        wait_bytes(slots.at[par, pl.ds(0, np_ - 1)], r_send.at[par])
        for way in range(2):
            @pl.when(has[way])
            def _():
                wait_bytes(nbs.at[par, way], rn_recv.at[par, way])
                wait_bytes(nbs.at[par, way], rn_send.at[par, way])
                if edges:
                    wait_bytes(rpk.at[par], e_recv.at[par, way])
                    wait_bytes(rpk.at[par], e_send.at[par, way])
        if edges:
            for side in range(2):
                @pl.when(flank[side])
                def _():
                    wait_bytes(cpk.at[par], c_recv.at[par, side])
                    wait_bytes(cpk.at[par], c_send.at[par, side])

    def applied(mat, mode, par, extra=None):
        total = extra
        for j in range(np_):
            term = mat[mode, :, j * rows : (j + 1) * rows] * slots[par, j, 0:1, :]
            total = term if total is None else total + term
        return jnp.sum(total, axis=1, keepdims=True)

    def finish(mode, par):
        coarse = jnp.broadcast_to(applied(pan_own, mode, par), (rows, LANES))
        for t in range(pieces):
            part = slice(t * LANES, (t + 1) * LANES)
            x[:, part] = z[:, part] + coarse * place[:, part]
        return coarse

    def side_row(mode, par, way):
        pan_row = 2 * mode + (1 - way)
        total = jnp.zeros((1, rows), F32)
        for j in range(np_):
            total = total + info_in[way, pan_row : pan_row + 1, j * rows : (j + 1) * rows] * nbs[par, way, j, 0:1, :]
        value = jnp.sum(total, axis=1, keepdims=True)
        base = pieces * (1 - way)
        got = jnp.concatenate([rows_in[par, way, base + t : base + t + 1, :] for t in range(pieces)], axis=1)
        return got + value * info_in[way, 4 + (1 - way) : 5 + (1 - way), 0:cols]

    def inner_resid(mode, base):
        v = z[...]
        zero = jnp.zeros((), F32)
        if mode:
            r[...] = base[...] - diag[...] * v + neighbours(stiff[...] * v, zero, zero, zero, zero)
        else:
            r[...] = base[...] - diag[...] * v + stiff[...] * neighbours(v, zero, zero, zero, zero)

    def outer_resid(mode, par, coarse):
        up, down = pltpu.roll(coarse, 1, 0), pltpu.roll(coarse, rows - 1, 0)
        west = applied(pan_left, mode, par, eye * cols_in[par, 0, 1:2, :])
        east = applied(pan_right, mode, par, eye * cols_in[par, 1, 0:1, :])
        thin = iota((rows, LANES), 1)
        for t in range(pieces):
            part = slice(t * LANES, (t + 1) * LANES)
            total = r[:, part] + coarse * k_own[mode, :, part]
            total = total + up * k_up[mode, :, part] + down * k_down[mode, :, part]
            if t == 0:
                total = total + jnp.where(thin == 0, west if mode else west * stiff[:, part], 0.0)
            if t == pieces - 1:
                total = total + jnp.where(thin == LANES - 1, east if mode else east * stiff[:, part], 0.0)
            r[:, part] = total
        top, bottom = side_row(mode, par, 0), side_row(mode, par, 1)
        if mode == 0:
            top, bottom = top * stiff[0:1, :], bottom * stiff[rows - 1 : rows, :]
        r[0:1, :] = r[0:1, :] + top
        r[rows - 1 : rows, :] = r[rows - 1 : rows, :] + bottom

    x[...] = disp[...]
    west = jnp.where(b > 0, to_col(sslots[left_slot][4:5, 0:rows]), 0.0)
    east = jnp.where(b < np_ - 1, to_col(sslots[right_slot][3:4, 0:rows]), 0.0)
    around = neighbours(disp[...], snb[0, 1:2, 0:cols], snb[1, 0:1, 0:cols], west, east)
    r[...] = load[...] - (diag[...] * disp[...] - stiff[...] * around)

    def primal(k, carry):
        par = lax.rem(k, 2)
        send_round(0, par, True)
        inner_resid(0, load)

        @pl.when(k == 0)
        def _():
            for way in range(2):
                @pl.when(has[way])
                def _():
                    wait_bytes(info_in.at[way], i_recv.at[way])
                    wait_bytes(info_out, i_send.at[way])

        wait_round(par, True)
        outer_resid(0, par, finish(0, par))
        return carry

    lax.fori_loop(0, ITERS - 1, primal, 0)
    par = (ITERS - 1) % 2
    send_round(0, par, False)
    wait_round(par, False)
    finish(0, par)
    found[...] = x[...]
    give_disp = pltpu.make_async_copy(found, out_disp, out_sem.at[0])
    give_disp.start()

    apk[...] = jnp.zeros(apk.shape, F32)
    apk[0, 0:1, :] = to_row(jnp.sum(cm[...] * x[...], axis=1, keepdims=True))
    to_plates(apk.at[0], fslots.at[b], a_send.at[0], a_recv.at[0])
    fslots[b] = apk[0]
    wait_bytes(fslots.at[pl.ds(0, np_ - 1)], a_recv.at[0])
    wait_bytes(fslots.at[pl.ds(0, np_ - 1)], a_send.at[0])
    force = fslots[0, 0:1, :]
    for j in range(1, np_):
        force = force + fslots[j, 0:1, :]
    force = force * (8.0 / math.sqrt(cols * np_ * rows * ns))
    apk[1, 0:1, :] = force
    for d in range(1, ns):
        push(apk.at[1], tslots.at[s], a_send.at[1], a_recv.at[1], ((s + d) % ns, b))
    tslots[s] = apk[1]
    wait_bytes(tslots.at[pl.ds(0, ns - 1)], a_recv.at[1])
    wait_bytes(tslots.at[pl.ds(0, ns - 1)], a_send.at[1])
    over = jnp.zeros((1, rows), F32)
    under = jnp.zeros((1, rows), F32)
    weight = (iota((1, rows), 1) + 1).astype(F32)
    for j in range(ns):
        line_j = tslots[j, 0:1, :]
        over = over + jnp.where(s < j, line_j, 0.0)
        under = under + line_j * (jnp.where(s > j, weight, 0.0) + (rows * jnp.minimum(s, j)).astype(F32))
    over = jnp.sum(over, axis=1, keepdims=True)
    under = jnp.sum(under, axis=1, keepdims=True)
    hh, ll = iota((rows, rows), 0), iota((rows, rows), 1)
    shear = jnp.sum(jnp.where(ll >= hh, force, 0.0), axis=1, keepdims=True) + over
    out_shear[...] = to_row(shear)
    local = jnp.sum(force * (jnp.minimum(hh, ll) + 1).astype(F32), axis=1, keepdims=True)
    step = (iota((rows, 1), 0) + 1).astype(F32)
    drift = (local + step * over + under) * (1.0 / (rows * ns))
    q[...] = cm[...] * drift
    r[...] = q[...]
    x[...] = jnp.zeros((rows, cols), F32)

    def adjoint(k, carry):
        par = lax.rem(k, 2)
        send_round(1, par, True)
        inner_resid(1, q)
        wait_round(par, True)
        outer_resid(1, par, finish(1, par))
        return carry

    lax.fori_loop(0, ITERS - 1, adjoint, 0)
    send_round(1, par, False)
    wait_round(par, False)
    finish(1, par)
    give_adj = pltpu.make_async_copy(x, out_adj, out_sem.at[1])
    give_adj.start()

    z[...] = x[...] * found[...]
    group = 8
    for first in range(0, count, group):
        def gather(i, accs):
            part = pl.ds(pl.multiple_of(i * 8, 8), 8)
            ids, vals = dmap[part, :], z[part, :]
            res = []
            for d in range(group):
                kept = jnp.where(ids == first + d, vals, 0.0)
                acc = accs[d]
                for t in range(pieces):
                    acc = acc + kept[:, t * LANES : (t + 1) * LANES]
                res.append(acc)
            return tuple(res)

        accs = lax.fori_loop(0, rows // 8, gather, tuple(jnp.zeros((8, LANES), F32) for _ in range(group)))
        for d in range(group):
            seg[first + d : first + d + 1, :] = jnp.sum(accs[d], axis=0, keepdims=True)
    apk[2, 0:1, 0:count] = to_row(jnp.sum(seg[...], axis=1, keepdims=True))
    to_plates(apk.at[2], gslots.at[b], a_send.at[2], a_recv.at[2])
    gslots[b] = apk[2]
    wait_bytes(gslots.at[pl.ds(0, np_ - 1)], a_recv.at[2])
    wait_bytes(gslots.at[pl.ds(0, np_ - 1)], a_send.at[2])
    sums = gslots[0, 0:1, 0:count]
    for j in range(1, np_):
        sums = sums + gslots[j, 0:1, 0:count]
    out_grads[...] = sums * (-CD * 64.0 / math.sqrt(rows * cols * np_ / count))
    give_disp.wait()
    give_adj.wait()


def deliver(*refs):
    copies = [pltpu.make_async_copy(refs[i], refs[4 + i], refs[8].at[i]) for i in range(4)]
    for copy in copies:
        copy.start()
    for copy in copies:
        copy.wait()


def on_device(load, disp, mass, wall_class, class_stiff, damper_map, damper_coef, band_tile, panel_store, owner, node_index):
    rows, cols = load.shape
    ns = lax.axis_size("storey")
    np_ = lax.axis_size("plate")
    nodes = node_index.shape[1]
    order = nodes * np_
    count = damper_coef.shape[0]
    width = max(cols, order, rows)
    wide = max(cols, np_ * rows)
    field = pltpu.VMEM((rows, cols), F32)
    square = pltpu.VMEM((cols, cols), BF16)
    grown = pltpu.VMEM((2, rows, np_ * rows), F32)
    dma = pltpu.SemaphoreType.DMA
    vmem = pl.BlockSpec(memory_space=pltpu.VMEM)
    smem = pl.BlockSpec(memory_space=pltpu.SMEM)
    hbm = pl.BlockSpec(memory_space=pltpu.HBM)
    ids = pltpu.VMEM((rows, cols), jnp.int32)
    shapes = ((rows, cols), (rows, cols), (rows,), (count,))
    new_disp, adj, shear, grads = pl.pallas_call(
        functools.partial(kernel, ns, np_),
        out_shape=(
            jax.ShapeDtypeStruct((rows, cols), F32),
            jax.ShapeDtypeStruct((rows, cols), F32),
            jax.ShapeDtypeStruct((1, rows), F32),
            jax.ShapeDtypeStruct((1, count), F32),
        ),
        in_specs=[hbm, hbm, hbm, hbm, smem, hbm, smem, hbm, hbm, smem, vmem],
        out_specs=(hbm, hbm, vmem, vmem),
        scratch_shapes=[field] * 3
        + [ids] * 2
        + [pltpu.VMEM((cols, cols), F32), dma((7,)), dma((2,)), field]
        + [field] * 9
        + [pltpu.VMEM((2, rows, cols), F32)] * 3
        + [square] * 4
        + [grown] * 3
        + [
            pltpu.VMEM((8, wide), F32),
            pltpu.VMEM((2, 8, wide), F32),
            pltpu.VMEM((8, width), F32),
            pltpu.VMEM((np_, 8, width), F32),
            pltpu.VMEM((2, 8, width), F32),
            pltpu.VMEM((np_, order, order), F32),
            pltpu.VMEM((2, 8, LANES), F32),
            pltpu.VMEM((2, 8, LANES), F32),
            pltpu.VMEM((2, 8, LANES), F32),
            pltpu.VMEM((2, np_, 8, LANES), F32),
            pltpu.VMEM((2, 2, np_, 8, LANES), F32),
            pltpu.VMEM((2, 2, 8, LANES), F32),
            pltpu.VMEM((2, 2, 8, LANES), F32),
            pltpu.VMEM((3, 8, LANES), F32),
            pltpu.VMEM((np_, 8, LANES), F32),
            pltpu.VMEM((ns, 8, LANES), F32),
            pltpu.VMEM((np_, 8, LANES), F32),
            pltpu.VMEM((count, LANES), F32),
            dma, dma, dma((2,)), dma((2,)), dma, dma, dma((2,)), dma((2,)),
            dma((2,)), dma((2,)), *[dma((2, 2))] * 6, dma((3,)), dma((3,)),
        ],
        compiler_params=pltpu.CompilerParams(
            collective_id=0, has_side_effects=True, vmem_limit_bytes=FULL
        ),
    )(load, disp, mass, wall_class, class_stiff, damper_map, damper_coef, band_tile, panel_store, owner, node_index)
    return pl.pallas_call(
        deliver,
        out_shape=tuple(jax.ShapeDtypeStruct(shape, F32) for shape in shapes),
        in_specs=[hbm] * 4,
        out_specs=(hbm,) * 4,
        scratch_shapes=[dma((4,))],
        compiler_params=pltpu.CompilerParams(vmem_limit_bytes=FULL),
    )(new_disp, adj, shear.reshape(rows), grads.reshape(count))


def solution(mesh):
    grid = P("storey", "plate")
    return jax.shard_map(
        on_device,
        mesh=mesh,
        in_specs=(grid, grid, grid, grid, P(), grid, P("storey"), grid, grid, P("storey"), grid),
        out_specs=(grid, grid, P("storey"), P("storey")),
        check_vma=False,
    )
```

```python
import functools
import math

import jax
import jax.numpy as jnp
from jax import lax
from jax.experimental import pallas as pl
from jax.experimental.pallas import tpu as pltpu
from jax.sharding import PartitionSpec as P

ITERS = 6
KF = 5.0 / 9.0
CM = 2.16
CD = 1.1
HIGH = lax.Precision.HIGHEST
MESH = pl.DeviceIdType.MESH
F32 = jnp.float32
BF16 = jnp.bfloat16
LANES = 128
FULL = 63 * 1024 * 1024


def iota(shape, dim):
    return lax.broadcasted_iota(jnp.int32, shape, dim)


def to_row(col):
    n = col.shape[0]
    return jnp.sum(jnp.where(iota((n, n), 0) == iota((n, n), 1), col, 0.0), axis=0, keepdims=True)


def to_col(row):
    n = row.shape[1]
    return jnp.sum(jnp.where(iota((n, n), 0) == iota((n, n), 1), row, 0.0), axis=1, keepdims=True)


def split(value):
    hi = value.astype(BF16)
    return hi, (value - hi.astype(F32)).astype(BF16)


def wait_bytes(ref, sem):
    pltpu.make_async_copy(ref, ref, sem).wait()


def kernel(
    ns, np_,
    load_in, disp_in, mass_in, wall_in, cstiff, dmap_in, coef, tile_in, panel, owner, nidx,
    out_disp, out_adj, out_shear, out_grads,
    load, disp, mass, wall, dmap, tile, in_sem, out_sem, found,
    stiff, diag, rdiag, cm, place, x, r, q, z,
    k_own, k_up, k_down,
    t_hi, t_lo, tt_hi, tt_lo,
    pan_own, pan_left, pan_right, pan_force, grown, used, info_out, info_in,
    spk, sslots, snb, pslots, epk, extras, x_send, x_recv,
    gpk, cpk, rpk, slots, nbs, cols_in, rows_in,
    apk, fslots, tslots, gslots, seg,
    s_send, s_recv, n_send, n_recv, p_send, p_recv, i_send, i_recv,
    r_send, r_recv, rn_send, rn_recv, c_send, c_recv, e_send, e_recv, a_send, a_recv,
):
    rows, cols = load.shape
    nodes = nidx.shape[1]
    order = nodes * np_
    count = coef.shape[0]
    width = spk.shape[1]
    pieces = cols // LANES
    s = lax.axis_index("storey")
    b = lax.axis_index("plate")
    has = (s > 0, s < ns - 1)
    beside = (s - 1, s + 1)

    ways = ((disp_in, disp), (wall_in, wall), (mass_in, mass), (dmap_in, dmap), (tile_in, tile), (load_in, load))
    loads = [pltpu.make_async_copy(src, dst, in_sem.at[i]) for i, (src, dst) in enumerate(ways)]
    loads.append(pltpu.make_async_copy(panel, pslots.at[b], in_sem.at[len(ways)]))
    for copy in loads:
        copy.start()

    barrier = pltpu.get_barrier_semaphore()
    for d in range(1, np_):
        pl.semaphore_signal(barrier, inc=1, device_id=(s, (b + d) % np_), device_id_type=MESH)
    for d in range(1, ns):
        pl.semaphore_signal(barrier, inc=1, device_id=((s + d) % ns, b), device_id_type=MESH)
    for way in range(2):
        @pl.when(has[way])
        def _():
            for d in range(1, np_):
                pl.semaphore_signal(barrier, inc=1, device_id=(beside[way], (b + d) % np_), device_id_type=MESH)
    sides = jnp.minimum(s, 1) + jnp.minimum(ns - 1 - s, 1)
    pl.semaphore_wait(barrier, np_ - 1 + ns - 1 + sides * (np_ - 1))

    def push(src, dst, send, recv, where):
        pltpu.make_async_remote_copy(
            src_ref=src, dst_ref=dst, send_sem=send, recv_sem=recv, device_id=where, device_id_type=MESH
        ).start()

    def to_plates(src, dst, send, recv):
        for d in range(1, np_):
            push(src, dst, send, recv, (s, (b + d) % np_))

    to_plates(panel, pslots.at[b], p_send, p_recv)

    at_own = nidx[...].astype(F32)
    tiled = (iota((nodes, order), 1) % nodes == iota((nodes, order), 0)).astype(F32)
    spk[2:3, 0:order] = jnp.dot(at_own, tiled, precision=HIGH, preferred_element_type=F32)
    loads[0].wait()
    spk[0:1, 0:cols] = disp[0:1, :]
    spk[1:2, 0:cols] = disp[rows - 1 : rows, :]
    spk[3:4, 0:rows] = to_row(disp[:, 0:1])
    spk[4:5, 0:rows] = to_row(disp[:, cols - 1 : cols])
    to_plates(spk, sslots.at[b], s_send, s_recv)
    flank = (b > 0, b < np_ - 1)
    flanking = (b - 1, b + 1)
    for way in range(2):
        @pl.when(has[way])
        def _():
            push(spk, snb.at[1 - way], n_send.at[way], n_recv.at[1 - way], (beside[way], b))

        @pl.when(jnp.logical_not(has[way]))
        def _():
            snb[way] = jnp.zeros(snb.shape[1:], F32)
            for i in range(2):
                info_in[i, way] = jnp.zeros(info_in.shape[2:], F32)
                nbs[i, way] = jnp.zeros(nbs.shape[2:], F32)
                rows_in[i, way] = jnp.zeros(rows_in.shape[2:], F32)

        @pl.when(jnp.logical_not(flank[way]))
        def _():
            for i in range(2):
                cols_in[i, way] = jnp.zeros(cols_in.shape[2:], F32)

    loads[1].wait()
    level = jnp.zeros((rows, cols), F32)
    for c in range(cstiff.shape[0]):
        level = jnp.where(wall[...] == c, cstiff[c], level)
    stiff[...] = KF * level
    loads[2].wait()
    cm[...] = CM * mass[...]
    loads[3].wait()

    def lookup(i, carry):
        part = pl.ds(pl.multiple_of(i * 8, 8), 8)
        ids = dmap[part, :]
        value = jnp.zeros(ids.shape, F32)
        for d in range(count):
            value = jnp.where(ids == d, coef[d], value)
        total = 4.0 * stiff[part, :] + cm[part, :] + CD * value
        diag[part, :] = total
        rdiag[part, :] = 1.0 / total
        return carry

    lax.fori_loop(0, rows // 8, lookup, 0)
    loads[4].wait()
    t_hi[...], t_lo[...] = split(tile[...])

    loads[5].wait()
    loads[6].wait()
    sslots[b] = spk[...]
    wait_bytes(sslots.at[pl.ds(0, np_ - 1)], s_recv)
    wait_bytes(pslots.at[pl.ds(0, np_ - 1)], p_recv)
    for way in range(2):
        @pl.when(has[way])
        def _():
            wait_bytes(snb.at[way], n_recv.at[way])
            wait_bytes(spk, n_send.at[way])
    wait_bytes(sslots.at[pl.ds(0, np_ - 1)], s_send)
    wait_bytes(pslots.at[pl.ds(0, np_ - 1)], p_send)

    root = owner[0]
    used_now = jnp.zeros((order, order), F32)
    for j in range(np_):
        used_now = jnp.where(root == j, pslots[j], used_now)
    used[...] = used_now
    lane_node = iota((1, order), 1) // nodes
    shift = cols.bit_length() - 1
    tall = (rows, order)
    left_slot = jnp.maximum(b - 1, 0)
    right_slot = jnp.minimum(b + 1, np_ - 1)

    def places():
        where_all = jnp.zeros((1, order), F32)
        for j in range(np_):
            where_all = jnp.where(lane_node == j, sslots[j, 2:3, 0:order], where_all)
        at = where_all.astype(jnp.int32)
        return jnp.right_shift(at, shift), jnp.bitwise_and(at, cols - 1)

    def expand_columns(mode):
        at_row, _ = places()
        at_row_col = to_col(at_row.astype(F32)).astype(jnp.int32)
        wide = (order, np_ * rows)
        spread = (
            (iota(wide, 1) % rows == at_row_col) & (iota(wide, 1) // rows == iota(wide, 0) // nodes)
        ).astype(F32).astype(BF16)
        hi, lo = split(used[...].T if mode else used[...])
        both = jnp.dot(jnp.concatenate([hi, lo], axis=0), spread, preferred_element_type=F32)
        grown[...] = both[:order] + both[order:]

    def pick(mask):
        hi, lo = split(grown[...])
        ones = mask.astype(F32).astype(BF16)
        return jnp.dot(ones, hi, preferred_element_type=F32) + jnp.dot(ones, lo, preferred_element_type=F32)

    def expand_own(mode):
        at_row, at_col = places()
        mask = (iota(tall, 0) == at_row) & (lane_node == b)
        if mode == 0:
            col_of = jnp.sum(jnp.where(mask, (at_col + 1).astype(F32), 0.0), axis=1, keepdims=True)
            place[...] = (iota((rows, cols), 1) == col_of.astype(jnp.int32) - 1).astype(F32)
        own = pick(mask)
        pan_own[mode] = own
        if mode:
            own = own * jnp.sum(place[...] * stiff[...], axis=1, keepdims=True)
        info_out[mode, 0:1, 0 : np_ * rows] = own[0:1, :]
        info_out[mode, 1:2, 0 : np_ * rows] = own[rows - 1 : rows, :]
        info_out[mode, 2:3, 0:cols] = place[0:1, :]
        info_out[mode, 3:4, 0:cols] = place[rows - 1 : rows, :]
        for way in range(2):
            @pl.when(has[way])
            def _():
                push(
                    info_out.at[mode], info_in.at[mode, 1 - way], i_send.at[mode, way],
                    i_recv.at[mode, 1 - way], (beside[way], b),
                )

    def wait_info(mode):
        for way in range(2):
            @pl.when(has[way])
            def _():
                wait_bytes(info_in.at[mode, way], i_recv.at[mode, way])
                wait_bytes(info_out.at[mode], i_send.at[mode, way])

    def expand_sides(mode):
        at_row, at_col = places()
        at_h = iota(tall, 0) == at_row
        left = at_h & (lane_node == b - 1) & (at_col == cols - 1)
        right = at_h & (lane_node == b + 1) & (at_col == 0)
        if mode:
            pan_left[mode] = pick(left) * to_col(extras[left_slot][1:2, 0:rows])
            pan_right[mode] = pick(right) * to_col(extras[right_slot][0:1, 0:rows])
        else:
            pan_left[mode] = pick(left)
            pan_right[mode] = pick(right)

    expand_columns(0)
    expand_own(0)

    eye = (iota((rows, rows), 0) == iota((rows, rows), 1)).astype(F32)
    lane = iota((rows, cols), 1)
    line = iota((rows, cols), 0)

    def sideways(v):
        return jnp.where(lane == 0, 0.0, pltpu.roll(v, 1, 1)) + jnp.where(
            lane == cols - 1, 0.0, pltpu.roll(v, cols - 1, 1)
        )

    def neighbours(v, top, bottom, left, right):
        above = jnp.where(line == 0, top, pltpu.roll(v, 1, 0))
        below = jnp.where(line == rows - 1, bottom, pltpu.roll(v, rows - 1, 0))
        west = jnp.where(lane == 0, left, pltpu.roll(v, 1, 1))
        east = jnp.where(lane == cols - 1, right, pltpu.roll(v, cols - 1, 1))
        return above + below + west + east

    def reach(mode):
        spot = place[...]
        held = stiff[...] * spot if mode else spot
        scale = (lambda v: v) if mode else (lambda v: stiff[...] * v)
        k_own[mode] = scale(sideways(held)) - diag[...] * spot
        k_up[mode] = jnp.where(line == 0, 0.0, scale(pltpu.roll(held, 1, 0)))
        k_down[mode] = jnp.where(line == rows - 1, 0.0, scale(pltpu.roll(held, rows - 1, 0)))

    def force_panel():
        at_row, _ = places()
        at_h = iota(tall, 0) == at_row
        mix = jnp.zeros(tall, F32)
        for j in range(np_):
            mix = jnp.where(at_h & (lane_node == j), to_col(extras[j, 2:3, 0:rows]), mix)
        pan_force[0] = jnp.dot(mix, grown[...], precision=HIGH, preferred_element_type=F32)

    def send_round(mode, par, edges):
        resid = r[...]
        gpk[par, 0:1, :] = to_row(jnp.sum(resid * place[...], axis=1, keepdims=True))
        for way in range(2):
            @pl.when(has[way])
            def _():
                for d in range(np_):
                    push(
                        gpk.at[par], nbs.at[par, 1 - way, b], rn_send.at[par, way],
                        rn_recv.at[par, 1 - way], (beside[way], (b + d) % np_),
                    )
        to_plates(gpk.at[par], slots.at[par, b], r_send.at[par], r_recv.at[par])
        slots[par, b] = gpk[par]
        hi, lo = split(resid * rdiag[...])
        wh, wl = (tt_hi, tt_lo) if mode else (t_hi, t_lo)
        both = jnp.dot(jnp.concatenate([hi, lo], axis=0), wh[...], preferred_element_type=F32)
        band = both[:rows] + both[rows:] + jnp.dot(hi, wl[...], preferred_element_type=F32)
        z[...] = x[...] + band
        if not edges:
            return
        edge = (lambda *at: z[at] * stiff[at]) if mode else (lambda *at: z[at])
        first, last = edge(slice(0, 1), slice(None)), edge(slice(rows - 1, rows), slice(None))
        for t in range(pieces):
            rpk[par, t : t + 1, :] = first[:, t * LANES : (t + 1) * LANES]
            rpk[par, pieces + t : pieces + t + 1, :] = last[:, t * LANES : (t + 1) * LANES]
        for way in range(2):
            @pl.when(has[way])
            def _():
                push(
                    rpk.at[par], rows_in.at[par, 1 - way], e_send.at[par, way],
                    e_recv.at[par, 1 - way], (beside[way], b),
                )
        cpk[par, 0:1, :] = to_row(edge(slice(None), slice(0, 1)))
        cpk[par, 1:2, :] = to_row(edge(slice(None), slice(cols - 1, cols)))
        for side in range(2):
            @pl.when(flank[side])
            def _():
                push(
                    cpk.at[par], cols_in.at[par, 1 - side], c_send.at[par, side],
                    c_recv.at[par, 1 - side], (s, flanking[side]),
                )

    def wait_round(par, edges):
        wait_bytes(slots.at[par, pl.ds(0, np_ - 1)], r_recv.at[par])
        wait_bytes(slots.at[par, pl.ds(0, np_ - 1)], r_send.at[par])
        for way in range(2):
            @pl.when(has[way])
            def _():
                wait_bytes(nbs.at[par, way], rn_recv.at[par, way])
                wait_bytes(nbs.at[par, way], rn_send.at[par, way])
                if edges:
                    wait_bytes(rpk.at[par], e_recv.at[par, way])
                    wait_bytes(rpk.at[par], e_send.at[par, way])
        if edges:
            for side in range(2):
                @pl.when(flank[side])
                def _():
                    wait_bytes(cpk.at[par], c_recv.at[par, side])
                    wait_bytes(cpk.at[par], c_send.at[par, side])

    def applied(mat, mode, par, extra=None):
        total = extra
        for j in range(np_):
            term = mat[mode, :, j * rows : (j + 1) * rows] * slots[par, j, 0:1, :]
            total = term if total is None else total + term
        return jnp.sum(total, axis=1, keepdims=True)

    def finish(mode, par):
        coarse = jnp.broadcast_to(applied(pan_own, mode, par), (rows, LANES))
        for t in range(pieces):
            part = slice(t * LANES, (t + 1) * LANES)
            x[:, part] = z[:, part] + coarse * place[:, part]
        return coarse

    def side_row(mode, par, way):
        pan_row = 1 - way
        total = jnp.zeros((1, rows), F32)
        for j in range(np_):
            total = total + info_in[mode, way, pan_row : pan_row + 1, j * rows : (j + 1) * rows] * nbs[par, way, j, 0:1, :]
        value = jnp.sum(total, axis=1, keepdims=True)
        base = pieces * (1 - way)
        got = jnp.concatenate([rows_in[par, way, base + t : base + t + 1, :] for t in range(pieces)], axis=1)
        return got + value * info_in[mode, way, 2 + (1 - way) : 3 + (1 - way), 0:cols]

    def inner_resid(mode, base):
        v = z[...]
        zero = jnp.zeros((), F32)
        if mode:
            r[...] = base[...] - diag[...] * v + neighbours(stiff[...] * v, zero, zero, zero, zero)
        else:
            r[...] = base[...] - diag[...] * v + stiff[...] * neighbours(v, zero, zero, zero, zero)

    def outer_resid(mode, par, coarse):
        up, down = pltpu.roll(coarse, 1, 0), pltpu.roll(coarse, rows - 1, 0)
        west = applied(pan_left, mode, par, eye * cols_in[par, 0, 1:2, :])
        east = applied(pan_right, mode, par, eye * cols_in[par, 1, 0:1, :])
        thin = iota((rows, LANES), 1)
        for t in range(pieces):
            part = slice(t * LANES, (t + 1) * LANES)
            total = r[:, part] + coarse * k_own[mode, :, part]
            total = total + up * k_up[mode, :, part] + down * k_down[mode, :, part]
            if t == 0:
                total = total + jnp.where(thin == 0, west if mode else west * stiff[:, part], 0.0)
            if t == pieces - 1:
                total = total + jnp.where(thin == LANES - 1, east if mode else east * stiff[:, part], 0.0)
            r[:, part] = total
        top, bottom = side_row(mode, par, 0), side_row(mode, par, 1)
        if mode == 0:
            top, bottom = top * stiff[0:1, :], bottom * stiff[rows - 1 : rows, :]
        r[0:1, :] = r[0:1, :] + top
        r[rows - 1 : rows, :] = r[rows - 1 : rows, :] + bottom

    x[...] = disp[...]
    west = jnp.where(b > 0, to_col(sslots[left_slot][4:5, 0:rows]), 0.0)
    east = jnp.where(b < np_ - 1, to_col(sslots[right_slot][3:4, 0:rows]), 0.0)
    around = neighbours(disp[...], snb[0, 1:2, 0:cols], snb[1, 0:1, 0:cols], west, east)
    r[...] = load[...] - (diag[...] * disp[...] - stiff[...] * around)

    def primal(k, carry):
        par = lax.rem(k, 2)
        send_round(0, par, True)

        @pl.when(k == 0)
        def _():
            expand_sides(0)
            reach(0)
            epk[0:1, :] = to_row(stiff[:, 0:1])
            epk[1:2, :] = to_row(stiff[:, cols - 1 : cols])
            epk[2:3, :] = to_row(jnp.sum(place[...] * cm[...], axis=1, keepdims=True))
            to_plates(epk, extras.at[b], x_send, x_recv)
            extras[b] = epk[...]

        @pl.when(k == 1)
        def _():
            wait_bytes(extras.at[pl.ds(0, np_ - 1)], x_recv)
            wait_bytes(extras.at[pl.ds(0, np_ - 1)], x_send)
            force_panel()
            expand_columns(1)
            expand_own(1)

        @pl.when(k == 2)
        def _():
            expand_sides(1)
            reach(1)

        @pl.when(k == 3)
        def _():
            tt_hi[...], tt_lo[...] = split(tile[...].T)

        inner_resid(0, load)

        @pl.when(k == 0)
        def _():
            wait_info(0)

        wait_round(par, True)
        outer_resid(0, par, finish(0, par))
        return carry

    lax.fori_loop(0, ITERS - 1, primal, 0)
    par = (ITERS - 1) % 2
    send_round(0, par, False)
    apk[0, 0:1, :] = to_row(jnp.sum(cm[...] * z[...], axis=1, keepdims=True))
    to_plates(apk.at[0], fslots.at[b], a_send.at[0], a_recv.at[0])
    fslots[b] = apk[0]
    wait_info(1)
    wait_round(par, False)
    wait_bytes(fslots.at[pl.ds(0, np_ - 1)], a_recv.at[0])
    wait_bytes(fslots.at[pl.ds(0, np_ - 1)], a_send.at[0])

    force = fslots[0, 0:1, :]
    for j in range(1, np_):
        force = force + fslots[j, 0:1, :]
    force = to_row(applied(pan_force, 0, par, eye * force))
    force = force * (8.0 / math.sqrt(cols * np_ * rows * ns))
    apk[1, 0:1, :] = force
    for d in range(1, ns):
        push(apk.at[1], tslots.at[s], a_send.at[1], a_recv.at[1], ((s + d) % ns, b))
    tslots[s] = apk[1]
    finish(0, par)
    found[...] = x[...]
    give_disp = pltpu.make_async_copy(found, out_disp, out_sem.at[0])
    give_disp.start()
    wait_bytes(tslots.at[pl.ds(0, ns - 1)], a_recv.at[1])
    wait_bytes(tslots.at[pl.ds(0, ns - 1)], a_send.at[1])
    over = jnp.zeros((1, rows), F32)
    under = jnp.zeros((1, rows), F32)
    weight = (iota((1, rows), 1) + 1).astype(F32)
    for j in range(ns):
        line_j = tslots[j, 0:1, :]
        over = over + jnp.where(s < j, line_j, 0.0)
        under = under + line_j * (jnp.where(s > j, weight, 0.0) + (rows * jnp.minimum(s, j)).astype(F32))
    over = jnp.sum(over, axis=1, keepdims=True)
    under = jnp.sum(under, axis=1, keepdims=True)
    hh, ll = iota((rows, rows), 0), iota((rows, rows), 1)
    shear = jnp.sum(jnp.where(ll >= hh, force, 0.0), axis=1, keepdims=True) + over
    out_shear[...] = to_row(shear)
    local = jnp.sum(force * (jnp.minimum(hh, ll) + 1).astype(F32), axis=1, keepdims=True)
    step = (iota((rows, 1), 0) + 1).astype(F32)
    drift = (local + step * over + under) * (1.0 / (rows * ns))
    q[...] = cm[...] * drift
    r[...] = q[...]
    x[...] = jnp.zeros((rows, cols), F32)

    def adjoint(k, carry):
        par = lax.rem(k, 2)
        send_round(1, par, True)
        inner_resid(1, q)
        wait_round(par, True)
        outer_resid(1, par, finish(1, par))
        return carry

    lax.fori_loop(0, ITERS - 1, adjoint, 0)
    send_round(1, par, False)
    wait_round(par, False)
    finish(1, par)
    give_adj = pltpu.make_async_copy(x, out_adj, out_sem.at[1])
    give_adj.start()

    z[...] = x[...] * found[...]
    group = 8
    for first in range(0, count, group):
        def gather(i, accs):
            part = pl.ds(pl.multiple_of(i * 8, 8), 8)
            ids, vals = dmap[part, :], z[part, :]
            res = []
            for d in range(group):
                kept = jnp.where(ids == first + d, vals, 0.0)
                acc = accs[d]
                for t in range(pieces):
                    acc = acc + kept[:, t * LANES : (t + 1) * LANES]
                res.append(acc)
            return tuple(res)

        accs = lax.fori_loop(0, rows // 8, gather, tuple(jnp.zeros((8, LANES), F32) for _ in range(group)))
        for d in range(group):
            seg[first + d : first + d + 1, :] = jnp.sum(accs[d], axis=0, keepdims=True)
    apk[2, 0:1, 0:count] = to_row(jnp.sum(seg[...], axis=1, keepdims=True))
    to_plates(apk.at[2], gslots.at[b], a_send.at[2], a_recv.at[2])
    gslots[b] = apk[2]
    wait_bytes(gslots.at[pl.ds(0, np_ - 1)], a_recv.at[2])
    wait_bytes(gslots.at[pl.ds(0, np_ - 1)], a_send.at[2])
    sums = gslots[0, 0:1, 0:count]
    for j in range(1, np_):
        sums = sums + gslots[j, 0:1, 0:count]
    out_grads[...] = sums * (-CD * 64.0 / math.sqrt(rows * cols * np_ / count))
    give_disp.wait()
    give_adj.wait()


def deliver(*refs):
    source, target, room, sems = refs[:4], refs[4:8], refs[8:12], refs[12]
    ins = [pltpu.make_async_copy(source[i], room[i], sems.at[0, i]) for i in range(4)]
    outs = [pltpu.make_async_copy(room[i], target[i], sems.at[1, i]) for i in range(4)]
    for copy in ins:
        copy.start()
    for i in range(4):
        ins[i].wait()
        outs[i].start()
    for copy in outs:
        copy.wait()


def on_device(load, disp, mass, wall_class, class_stiff, damper_map, damper_coef, band_tile, panel_store, owner, node_index):
    rows, cols = load.shape
    ns = lax.axis_size("storey")
    np_ = lax.axis_size("plate")
    nodes = node_index.shape[1]
    order = nodes * np_
    count = damper_coef.shape[0]
    width = max(cols, order, rows)
    wide = max(cols, np_ * rows)
    field = pltpu.VMEM((rows, cols), F32)
    square = pltpu.VMEM((cols, cols), BF16)
    grown = pltpu.VMEM((2, rows, np_ * rows), F32)
    dma = pltpu.SemaphoreType.DMA
    vmem = pl.BlockSpec(memory_space=pltpu.VMEM)
    smem = pl.BlockSpec(memory_space=pltpu.SMEM)
    hbm = pl.BlockSpec(memory_space=pltpu.HBM)
    ids = pltpu.VMEM((rows, cols), jnp.int32)
    shapes = ((rows, cols), (rows, cols), (rows,), (count,))
    new_disp, adj, shear, grads = pl.pallas_call(
        functools.partial(kernel, ns, np_),
        out_shape=(
            jax.ShapeDtypeStruct((rows, cols), F32),
            jax.ShapeDtypeStruct((rows, cols), F32),
            jax.ShapeDtypeStruct((1, rows), F32),
            jax.ShapeDtypeStruct((1, count), F32),
        ),
        in_specs=[hbm, hbm, hbm, hbm, smem, hbm, smem, hbm, hbm, smem, vmem],
        out_specs=(hbm, hbm, vmem, vmem),
        scratch_shapes=[field] * 3
        + [ids] * 2
        + [pltpu.VMEM((cols, cols), F32), dma((7,)), dma((2,)), field]
        + [field] * 9
        + [pltpu.VMEM((2, rows, cols), F32)] * 3
        + [square] * 4
        + [grown] * 3
        + [
            pltpu.VMEM((1, rows, np_ * rows), F32),
            pltpu.VMEM((order, np_ * rows), F32),
            pltpu.VMEM((order, order), F32),
            pltpu.VMEM((2, 8, wide), F32),
            pltpu.VMEM((2, 2, 8, wide), F32),
            pltpu.VMEM((8, width), F32),
            pltpu.VMEM((np_, 8, width), F32),
            pltpu.VMEM((2, 8, width), F32),
            pltpu.VMEM((np_, order, order), F32),
            pltpu.VMEM((8, LANES), F32),
            pltpu.VMEM((np_, 8, LANES), F32),
            dma,
            dma,
            pltpu.VMEM((2, 8, LANES), F32),
            pltpu.VMEM((2, 8, LANES), F32),
            pltpu.VMEM((2, 8, LANES), F32),
            pltpu.VMEM((2, np_, 8, LANES), F32),
            pltpu.VMEM((2, 2, np_, 8, LANES), F32),
            pltpu.VMEM((2, 2, 8, LANES), F32),
            pltpu.VMEM((2, 2, 8, LANES), F32),
            pltpu.VMEM((3, 8, LANES), F32),
            pltpu.VMEM((np_, 8, LANES), F32),
            pltpu.VMEM((ns, 8, LANES), F32),
            pltpu.VMEM((np_, 8, LANES), F32),
            pltpu.VMEM((count, LANES), F32),
            dma, dma, dma((2,)), dma((2,)), dma, dma, dma((2, 2)), dma((2, 2)),
            dma((2,)), dma((2,)), *[dma((2, 2))] * 6, dma((3,)), dma((3,)),
        ],
        compiler_params=pltpu.CompilerParams(
            collective_id=0, has_side_effects=True, vmem_limit_bytes=FULL
        ),
    )(load, disp, mass, wall_class, class_stiff, damper_map, damper_coef, band_tile, panel_store, owner, node_index)
    return pl.pallas_call(
        deliver,
        out_shape=tuple(jax.ShapeDtypeStruct(shape, F32) for shape in shapes),
        in_specs=[hbm] * 4,
        out_specs=(hbm,) * 4,
        scratch_shapes=[pltpu.VMEM(shape, F32) for shape in shapes] + [dma((2, 4))],
        compiler_params=pltpu.CompilerParams(vmem_limit_bytes=FULL),
    )(new_disp, adj, shear.reshape(rows), grads.reshape(count))


def solution(mesh):
    grid = P("storey", "plate")
    return jax.shard_map(
        on_device,
        mesh=mesh,
        in_specs=(grid, grid, grid, grid, P(), grid, P("storey"), grid, grid, P("storey"), grid),
        out_specs=(grid, grid, P("storey"), P("storey")),
        check_vma=False,
    )
```

```python
import functools
import math

import jax
import jax.numpy as jnp
from jax import lax
from jax.experimental import pallas as pl
from jax.experimental.pallas import tpu as pltpu
from jax.sharding import PartitionSpec as P

ITERS = 6
KF = 5.0 / 9.0
CM = 2.16
CD = 1.1
HIGH = lax.Precision.HIGHEST
MESH = pl.DeviceIdType.MESH
F32 = jnp.float32
BF16 = jnp.bfloat16
LANES = 128
FULL = 63 * 1024 * 1024


def iota(shape, dim):
    return lax.broadcasted_iota(jnp.int32, shape, dim)


def to_row(col):
    n = col.shape[0]
    return jnp.sum(jnp.where(iota((n, n), 0) == iota((n, n), 1), col, 0.0), axis=0, keepdims=True)


def to_col(row):
    n = row.shape[1]
    return jnp.sum(jnp.where(iota((n, n), 0) == iota((n, n), 1), row, 0.0), axis=1, keepdims=True)


def split(value):
    hi = value.astype(BF16)
    return hi, (value - hi.astype(F32)).astype(BF16)


def wait_bytes(ref, sem):
    pltpu.make_async_copy(ref, ref, sem).wait()


def kernel(
    ns, np_,
    load_in, disp_in, mass_in, wall_in, cstiff, dmap_in, coef, tile_in, panel, owner, nidx,
    out_disp, out_adj, out_shear, out_grads,
    load, disp, mass, wall, dmap, tile, in_sem, out_sem, found,
    stiff, diag, rdiag, cm, place, x, r, q, z,
    k_own, k_up, k_down,
    t_hi, t_lo, tt_hi, tt_lo,
    pan_own, pan_left, pan_right, pan_force, grown, used, info_out, info_in,
    spk, sslots, snb, pslots, epk, extras, x_send, x_recv,
    gpk, rpk, slots, nbs, rows_in, edge_tile,
    apk, fslots, tslots, gslots, seg,
    s_send, s_recv, n_send, n_recv, p_send, p_recv, i_send, i_recv,
    r_send, r_recv, rn_send, rn_recv, e_send, e_recv, a_send, a_recv,
):
    rows, cols = load.shape
    nodes = nidx.shape[1]
    order = nodes * np_
    count = coef.shape[0]
    width = spk.shape[1]
    pieces = cols // LANES
    s = lax.axis_index("storey")
    b = lax.axis_index("plate")
    has = (s > 0, s < ns - 1)
    beside = (s - 1, s + 1)
    miss = (1 - jnp.minimum(s, 1), 1 - jnp.minimum(ns - 1 - s, 1))
    toward = (jnp.maximum(s - 1, 0), jnp.minimum(s + 1, ns - 1))
    lands = tuple((1 - way) * (1 - miss[way]) + way * miss[way] for way in range(2))
    same = tuple((b + miss[way]) % np_ for way in range(2))

    ways = ((disp_in, disp), (wall_in, wall), (mass_in, mass), (dmap_in, dmap), (tile_in, tile), (load_in, load))
    loads = [pltpu.make_async_copy(src, dst, in_sem.at[i]) for i, (src, dst) in enumerate(ways)]
    loads.append(pltpu.make_async_copy(panel, pslots.at[b], in_sem.at[len(ways)]))
    for copy in loads:
        copy.start()

    barrier = pltpu.get_barrier_semaphore()
    for d in range(1, np_):
        pl.semaphore_signal(barrier, inc=1, device_id=(s, (b + d) % np_), device_id_type=MESH)
    for d in range(1, ns):
        pl.semaphore_signal(barrier, inc=1, device_id=((s + d) % ns, b), device_id_type=MESH)
    for way in range(2):
        @pl.when(has[way])
        def _():
            for d in range(1, np_):
                pl.semaphore_signal(barrier, inc=1, device_id=(beside[way], (b + d) % np_), device_id_type=MESH)
    sides = jnp.minimum(s, 1) + jnp.minimum(ns - 1 - s, 1)
    pl.semaphore_wait(barrier, np_ - 1 + ns - 1 + sides * (np_ - 1))

    def push(src, dst, send, recv, where):
        pltpu.make_async_remote_copy(
            src_ref=src, dst_ref=dst, send_sem=send, recv_sem=recv, device_id=where, device_id_type=MESH
        ).start()

    def to_plates(src, dst, send, recv):
        for d in range(1, np_):
            push(src, dst, send, recv, (s, (b + d) % np_))

    to_plates(panel, pslots.at[b], p_send, p_recv)

    at_own = nidx[...].astype(F32)
    tiled = (iota((nodes, order), 1) % nodes == iota((nodes, order), 0)).astype(F32)
    spk[2:3, 0:order] = jnp.dot(at_own, tiled, precision=HIGH, preferred_element_type=F32)
    loads[0].wait()
    spk[0:1, 0:cols] = disp[0:1, :]
    spk[1:2, 0:cols] = disp[rows - 1 : rows, :]
    spk[3:4, 0:rows] = to_row(disp[:, 0:1])
    spk[4:5, 0:rows] = to_row(disp[:, cols - 1 : cols])
    to_plates(spk, sslots.at[b], s_send, s_recv)
    for way in range(2):
        @pl.when(has[way])
        def _():
            push(spk, snb.at[1 - way], n_send.at[way], n_recv.at[1 - way], (beside[way], b))

        @pl.when(jnp.logical_not(has[way]))
        def _():
            snb[way] = jnp.zeros(snb.shape[1:], F32)
            for i in range(2):
                info_in[i, way] = jnp.zeros(info_in.shape[2:], F32)

    loads[1].wait()
    level = jnp.zeros((rows, cols), F32)
    for c in range(cstiff.shape[0]):
        level = jnp.where(wall[...] == c, cstiff[c], level)
    stiff[...] = KF * level
    loads[2].wait()
    cm[...] = CM * mass[...]
    loads[3].wait()

    def lookup(i, carry):
        part = pl.ds(pl.multiple_of(i * 8, 8), 8)
        ids = dmap[part, :]
        value = jnp.zeros(ids.shape, F32)
        for d in range(count):
            value = jnp.where(ids == d, coef[d], value)
        total = 4.0 * stiff[part, :] + cm[part, :] + CD * value
        diag[part, :] = total
        rdiag[part, :] = 1.0 / total
        return carry

    lax.fori_loop(0, rows // 8, lookup, 0)
    loads[4].wait()
    t_hi[...], t_lo[...] = split(tile[...])
    for i, at in enumerate((0, cols - 1)):
        edge_tile[0, i : i + 1, :] = to_row(tile[:, at : at + 1])
        edge_tile[1, i : i + 1, :] = tile[at : at + 1, :]

    loads[5].wait()
    loads[6].wait()
    sslots[b] = spk[...]
    wait_bytes(sslots.at[pl.ds(0, np_ - 1)], s_recv)
    wait_bytes(pslots.at[pl.ds(0, np_ - 1)], p_recv)
    for way in range(2):
        @pl.when(has[way])
        def _():
            wait_bytes(snb.at[way], n_recv.at[way])
            wait_bytes(spk, n_send.at[way])
    wait_bytes(sslots.at[pl.ds(0, np_ - 1)], s_send)
    wait_bytes(pslots.at[pl.ds(0, np_ - 1)], p_send)

    root = owner[0]
    used_now = jnp.zeros((order, order), F32)
    for j in range(np_):
        used_now = jnp.where(root == j, pslots[j], used_now)
    used[...] = used_now
    lane_node = iota((1, order), 1) // nodes
    shift = cols.bit_length() - 1
    tall = (rows, order)
    left_slot = jnp.maximum(b - 1, 0)
    right_slot = jnp.minimum(b + 1, np_ - 1)

    def places():
        where_all = jnp.zeros((1, order), F32)
        for j in range(np_):
            where_all = jnp.where(lane_node == j, sslots[j, 2:3, 0:order], where_all)
        at = where_all.astype(jnp.int32)
        return jnp.right_shift(at, shift), jnp.bitwise_and(at, cols - 1)

    def expand_columns(mode):
        at_row, _ = places()
        at_row_col = to_col(at_row.astype(F32)).astype(jnp.int32)
        wide = (order, np_ * rows)
        spread = (
            (iota(wide, 1) % rows == at_row_col) & (iota(wide, 1) // rows == iota(wide, 0) // nodes)
        ).astype(F32).astype(BF16)
        hi, lo = split(used[...].T if mode else used[...])
        both = jnp.dot(jnp.concatenate([hi, lo], axis=0), spread, preferred_element_type=F32)
        grown[...] = both[:order] + both[order:]

    def pick(mask):
        hi, lo = split(grown[...])
        ones = mask.astype(F32).astype(BF16)
        return jnp.dot(ones, hi, preferred_element_type=F32) + jnp.dot(ones, lo, preferred_element_type=F32)

    def expand_own(mode):
        at_row, at_col = places()
        mask = (iota(tall, 0) == at_row) & (lane_node == b)
        if mode == 0:
            col_of = jnp.sum(jnp.where(mask, (at_col + 1).astype(F32), 0.0), axis=1, keepdims=True)
            place[...] = (iota((rows, cols), 1) == col_of.astype(jnp.int32) - 1).astype(F32)
        own = pick(mask)
        pan_own[mode] = own
        if mode:
            own = own * jnp.sum(place[...] * stiff[...], axis=1, keepdims=True)
        info_out[mode, 0:1, 0 : np_ * rows] = own[0:1, :]
        info_out[mode, 1:2, 0 : np_ * rows] = own[rows - 1 : rows, :]
        info_out[mode, 2:3, 0:cols] = place[0:1, :]
        info_out[mode, 3:4, 0:cols] = place[rows - 1 : rows, :]
        for way in range(2):
            @pl.when(has[way])
            def _():
                push(
                    info_out.at[mode], info_in.at[mode, 1 - way], i_send.at[mode, way],
                    i_recv.at[mode, 1 - way], (beside[way], b),
                )

    def wait_info(mode):
        for way in range(2):
            @pl.when(has[way])
            def _():
                wait_bytes(info_in.at[mode, way], i_recv.at[mode, way])
                wait_bytes(info_out.at[mode], i_send.at[mode, way])

    def expand_sides(mode):
        at_row, at_col = places()
        at_h = iota(tall, 0) == at_row
        left = at_h & (lane_node == b - 1) & (at_col == cols - 1)
        right = at_h & (lane_node == b + 1) & (at_col == 0)
        if mode:
            pan_left[mode] = pick(left) * to_col(extras[left_slot][1:2, 0:rows])
            pan_right[mode] = pick(right) * to_col(extras[right_slot][0:1, 0:rows])
        else:
            pan_left[mode] = pick(left)
            pan_right[mode] = pick(right)

    expand_columns(0)
    expand_own(0)

    eye = (iota((rows, rows), 0) == iota((rows, rows), 1)).astype(F32)
    lane = iota((rows, cols), 1)
    line = iota((rows, cols), 0)

    def sideways(v):
        return jnp.where(lane == 0, 0.0, pltpu.roll(v, 1, 1)) + jnp.where(
            lane == cols - 1, 0.0, pltpu.roll(v, cols - 1, 1)
        )

    def neighbours(v, top, bottom, left, right):
        above = jnp.where(line == 0, top, pltpu.roll(v, 1, 0))
        below = jnp.where(line == rows - 1, bottom, pltpu.roll(v, rows - 1, 0))
        west = jnp.where(lane == 0, left, pltpu.roll(v, 1, 1))
        east = jnp.where(lane == cols - 1, right, pltpu.roll(v, cols - 1, 1))
        return above + below + west + east

    def reach(mode):
        spot = place[...]
        held = stiff[...] * spot if mode else spot
        scale = (lambda v: v) if mode else (lambda v: stiff[...] * v)
        k_own[mode] = scale(sideways(held)) - diag[...] * spot
        k_up[mode] = jnp.where(line == 0, 0.0, scale(pltpu.roll(held, 1, 0)))
        k_down[mode] = jnp.where(line == rows - 1, 0.0, scale(pltpu.roll(held, rows - 1, 0)))

    def force_panel():
        at_row, _ = places()
        at_h = iota(tall, 0) == at_row
        mix = jnp.zeros(tall, F32)
        for j in range(np_):
            mix = jnp.where(at_h & (lane_node == j), to_col(extras[j, 2:3, 0:rows]), mix)
        pan_force[0] = jnp.dot(mix, grown[...], precision=HIGH, preferred_element_type=F32)

    def send_round(mode, par, edges):
        resid = r[...]
        scaled = resid * rdiag[...]
        gpk[par, 0:1, :] = to_row(jnp.sum(resid * place[...], axis=1, keepdims=True))
        if edges:
            for i, at in enumerate((0, cols - 1)):
                value = x[:, at : at + 1] + jnp.sum(scaled * edge_tile[mode, i : i + 1, :], axis=1, keepdims=True)
                gpk[par, 1 + i : 2 + i, :] = to_row(value * stiff[:, at : at + 1] if mode else value)
        for way in range(2):
            for d in range(np_):
                if d:
                    plate, slot = (b + d) % np_, b
                else:
                    plate, slot = same[way], same[way]
                push(gpk.at[par], nbs.at[par, lands[way], slot], rn_send.at[par], rn_recv.at[par], (toward[way], plate))
        to_plates(gpk.at[par], slots.at[par, b], r_send.at[par], r_recv.at[par])
        slots[par, b] = gpk[par]
        hi, lo = split(scaled)
        wh, wl = (tt_hi, tt_lo) if mode else (t_hi, t_lo)
        both = jnp.dot(jnp.concatenate([hi, lo], axis=0), wh[...], preferred_element_type=F32)
        band = both[:rows] + both[rows:] + jnp.dot(hi, wl[...], preferred_element_type=F32)
        total = x[...] + band
        z[...] = total
        if not edges:
            return
        first, last = total[0:1, :], total[rows - 1 : rows, :]
        if mode:
            first, last = first * stiff[0:1, :], last * stiff[rows - 1 : rows, :]
        for t in range(pieces):
            rpk[par, t : t + 1, :] = first[:, t * LANES : (t + 1) * LANES]
            rpk[par, pieces + t : pieces + t + 1, :] = last[:, t * LANES : (t + 1) * LANES]
        for way in range(2):
            push(rpk.at[par], rows_in.at[par, lands[way]], e_send.at[par], e_recv.at[par], (toward[way], same[way]))

    def wait_round(par, edges):
        wait_bytes(slots.at[par, pl.ds(0, np_ - 1)], r_recv.at[par])
        wait_bytes(nbs.at[par], rn_recv.at[par])
        if edges:
            wait_bytes(rows_in.at[par], e_recv.at[par])
            wait_bytes(rows_in.at[par], e_send.at[par])
        wait_bytes(slots.at[par, pl.ds(0, np_ - 1)], r_send.at[par])
        wait_bytes(nbs.at[par], rn_send.at[par])

    def applied(mat, mode, par, extra=None):
        total = extra
        for j in range(np_):
            term = mat[mode, :, j * rows : (j + 1) * rows] * slots[par, j, 0:1, :]
            total = term if total is None else total + term
        return jnp.sum(total, axis=1, keepdims=True)

    def finish(mode, par):
        coarse = jnp.broadcast_to(applied(pan_own, mode, par), (rows, LANES))
        for t in range(pieces):
            part = slice(t * LANES, (t + 1) * LANES)
            x[:, part] = z[:, part] + coarse * place[:, part]
        return coarse

    def side_row(mode, par, way):
        pan_row = 1 - way
        total = jnp.zeros((1, rows), F32)
        for j in range(np_):
            total = total + info_in[mode, way, pan_row : pan_row + 1, j * rows : (j + 1) * rows] * nbs[par, way, j, 0:1, :]
        value = jnp.sum(total, axis=1, keepdims=True)
        base = pieces * (1 - way)
        got = jnp.concatenate([rows_in[par, way, base + t : base + t + 1, :] for t in range(pieces)], axis=1)
        got = jnp.where(has[way], got, 0.0)
        return got + value * info_in[mode, way, 2 + (1 - way) : 3 + (1 - way), 0:cols]

    def inner_resid(mode, base):
        v = z[...]
        zero = jnp.zeros((), F32)
        if mode:
            r[...] = base[...] - diag[...] * v + neighbours(stiff[...] * v, zero, zero, zero, zero)
        else:
            r[...] = base[...] - diag[...] * v + stiff[...] * neighbours(v, zero, zero, zero, zero)

    def outer_resid(mode, par, coarse):
        up, down = pltpu.roll(coarse, 1, 0), pltpu.roll(coarse, rows - 1, 0)
        west = jnp.where(b > 0, slots[par, left_slot, 2:3, :], 0.0)
        east = jnp.where(b < np_ - 1, slots[par, right_slot, 1:2, :], 0.0)
        west = applied(pan_left, mode, par, eye * west)
        east = applied(pan_right, mode, par, eye * east)
        thin = iota((rows, LANES), 1)
        for t in range(pieces):
            part = slice(t * LANES, (t + 1) * LANES)
            total = r[:, part] + coarse * k_own[mode, :, part]
            total = total + up * k_up[mode, :, part] + down * k_down[mode, :, part]
            if t == 0:
                total = total + jnp.where(thin == 0, west if mode else west * stiff[:, part], 0.0)
            if t == pieces - 1:
                total = total + jnp.where(thin == LANES - 1, east if mode else east * stiff[:, part], 0.0)
            r[:, part] = total
        top, bottom = side_row(mode, par, 0), side_row(mode, par, 1)
        if mode == 0:
            top, bottom = top * stiff[0:1, :], bottom * stiff[rows - 1 : rows, :]
        r[0:1, :] = r[0:1, :] + top
        r[rows - 1 : rows, :] = r[rows - 1 : rows, :] + bottom

    x[...] = disp[...]
    west = jnp.where(b > 0, to_col(sslots[left_slot][4:5, 0:rows]), 0.0)
    east = jnp.where(b < np_ - 1, to_col(sslots[right_slot][3:4, 0:rows]), 0.0)
    around = neighbours(disp[...], snb[0, 1:2, 0:cols], snb[1, 0:1, 0:cols], west, east)
    r[...] = load[...] - (diag[...] * disp[...] - stiff[...] * around)

    def primal(k, carry):
        par = lax.rem(k, 2)
        send_round(0, par, True)

        @pl.when(k == 0)
        def _():
            expand_sides(0)
            reach(0)
            epk[0:1, :] = to_row(stiff[:, 0:1])
            epk[1:2, :] = to_row(stiff[:, cols - 1 : cols])
            epk[2:3, :] = to_row(jnp.sum(place[...] * cm[...], axis=1, keepdims=True))
            to_plates(epk, extras.at[b], x_send, x_recv)
            extras[b] = epk[...]

        @pl.when(k == 1)
        def _():
            wait_bytes(extras.at[pl.ds(0, np_ - 1)], x_recv)
            wait_bytes(extras.at[pl.ds(0, np_ - 1)], x_send)
            force_panel()
            expand_columns(1)
            expand_own(1)

        @pl.when(k == 2)
        def _():
            expand_sides(1)
            reach(1)

        @pl.when(k == 3)
        def _():
            tt_hi[...], tt_lo[...] = split(tile[...].T)

        inner_resid(0, load)

        @pl.when(k == 0)
        def _():
            wait_info(0)

        wait_round(par, True)
        outer_resid(0, par, finish(0, par))
        return carry

    lax.fori_loop(0, ITERS - 1, primal, 0)
    par = (ITERS - 1) % 2
    send_round(0, par, False)
    apk[0, 0:1, :] = to_row(jnp.sum(cm[...] * z[...], axis=1, keepdims=True))
    to_plates(apk.at[0], fslots.at[b], a_send.at[0], a_recv.at[0])
    fslots[b] = apk[0]
    wait_info(1)
    wait_round(par, False)
    wait_bytes(fslots.at[pl.ds(0, np_ - 1)], a_recv.at[0])
    wait_bytes(fslots.at[pl.ds(0, np_ - 1)], a_send.at[0])

    force = fslots[0, 0:1, :]
    for j in range(1, np_):
        force = force + fslots[j, 0:1, :]
    force = to_row(applied(pan_force, 0, par, eye * force))
    force = force * (8.0 / math.sqrt(cols * np_ * rows * ns))
    apk[1, 0:1, :] = force
    for d in range(1, ns):
        push(apk.at[1], tslots.at[s], a_send.at[1], a_recv.at[1], ((s + d) % ns, b))
    tslots[s] = apk[1]
    finish(0, par)
    found[...] = x[...]
    give_disp = pltpu.make_async_copy(found, out_disp, out_sem.at[0])
    give_disp.start()
    wait_bytes(tslots.at[pl.ds(0, ns - 1)], a_recv.at[1])
    wait_bytes(tslots.at[pl.ds(0, ns - 1)], a_send.at[1])
    over = jnp.zeros((1, rows), F32)
    under = jnp.zeros((1, rows), F32)
    weight = (iota((1, rows), 1) + 1).astype(F32)
    for j in range(ns):
        line_j = tslots[j, 0:1, :]
        over = over + jnp.where(s < j, line_j, 0.0)
        under = under + line_j * (jnp.where(s > j, weight, 0.0) + (rows * jnp.minimum(s, j)).astype(F32))
    over = jnp.sum(over, axis=1, keepdims=True)
    under = jnp.sum(under, axis=1, keepdims=True)
    hh, ll = iota((rows, rows), 0), iota((rows, rows), 1)
    shear = jnp.sum(jnp.where(ll >= hh, force, 0.0), axis=1, keepdims=True) + over
    out_shear[...] = to_row(shear)
    local = jnp.sum(force * (jnp.minimum(hh, ll) + 1).astype(F32), axis=1, keepdims=True)
    step = (iota((rows, 1), 0) + 1).astype(F32)
    drift = (local + step * over + under) * (1.0 / (rows * ns))
    q[...] = cm[...] * drift
    r[...] = q[...]
    x[...] = jnp.zeros((rows, cols), F32)

    def adjoint(k, carry):
        par = lax.rem(k, 2)
        send_round(1, par, True)
        inner_resid(1, q)
        wait_round(par, True)
        outer_resid(1, par, finish(1, par))
        return carry

    lax.fori_loop(0, ITERS - 1, adjoint, 0)
    send_round(1, par, False)

    q[...] = z[...] * found[...]
    group = 8
    for first in range(0, count, group):
        def gather(i, accs):
            part = pl.ds(pl.multiple_of(i * 8, 8), 8)
            ids, vals = dmap[part, :], q[part, :]
            res = []
            for d in range(group):
                kept = jnp.where(ids == first + d, vals, 0.0)
                acc = accs[d]
                for t in range(pieces):
                    acc = acc + kept[:, t * LANES : (t + 1) * LANES]
                res.append(acc)
            return tuple(res)

        accs = lax.fori_loop(0, rows // 8, gather, tuple(jnp.zeros((8, LANES), F32) for _ in range(group)))
        for d in range(group):
            seg[first + d : first + d + 1, :] = jnp.sum(accs[d], axis=0, keepdims=True)
    sums = to_row(jnp.sum(seg[...], axis=1, keepdims=True))
    damper = jnp.sum(place[...] * dmap[...].astype(F32), axis=1, keepdims=True)
    held = jnp.sum(place[...] * found[...], axis=1, keepdims=True)
    hits = jnp.where(damper == iota((rows, count), 1).astype(F32), held, 0.0)
    wait_round(par, False)
    coarse = finish(1, par)
    give_adj = pltpu.make_async_copy(x, out_adj, out_sem.at[1])
    give_adj.start()
    sums = sums + jnp.sum(hits * coarse[:, 0:count], axis=0, keepdims=True)
    apk[2, 0:1, 0:count] = sums
    to_plates(apk.at[2], gslots.at[b], a_send.at[2], a_recv.at[2])
    gslots[b] = apk[2]
    wait_bytes(gslots.at[pl.ds(0, np_ - 1)], a_recv.at[2])
    wait_bytes(gslots.at[pl.ds(0, np_ - 1)], a_send.at[2])
    sums = gslots[0, 0:1, 0:count]
    for j in range(1, np_):
        sums = sums + gslots[j, 0:1, 0:count]
    out_grads[...] = sums * (-CD * 64.0 / math.sqrt(rows * cols * np_ / count))
    give_disp.wait()
    give_adj.wait()


def deliver(*refs):
    source, target, room, sems = refs[:4], refs[4:8], refs[8:12], refs[12]
    ins = [pltpu.make_async_copy(source[i], room[i], sems.at[0, i]) for i in range(4)]
    outs = [pltpu.make_async_copy(room[i], target[i], sems.at[1, i]) for i in range(4)]
    for copy in ins:
        copy.start()
    for i in range(4):
        ins[i].wait()
        outs[i].start()
    for copy in outs:
        copy.wait()


def on_device(load, disp, mass, wall_class, class_stiff, damper_map, damper_coef, band_tile, panel_store, owner, node_index):
    rows, cols = load.shape
    ns = lax.axis_size("storey")
    np_ = lax.axis_size("plate")
    nodes = node_index.shape[1]
    order = nodes * np_
    count = damper_coef.shape[0]
    width = max(cols, order, rows)
    wide = max(cols, np_ * rows)
    field = pltpu.VMEM((rows, cols), F32)
    square = pltpu.VMEM((cols, cols), BF16)
    grown = pltpu.VMEM((2, rows, np_ * rows), F32)
    dma = pltpu.SemaphoreType.DMA
    vmem = pl.BlockSpec(memory_space=pltpu.VMEM)
    smem = pl.BlockSpec(memory_space=pltpu.SMEM)
    hbm = pl.BlockSpec(memory_space=pltpu.HBM)
    ids = pltpu.VMEM((rows, cols), jnp.int32)
    shapes = ((rows, cols), (rows, cols), (rows,), (count,))
    new_disp, adj, shear, grads = pl.pallas_call(
        functools.partial(kernel, ns, np_),
        out_shape=(
            jax.ShapeDtypeStruct((rows, cols), F32),
            jax.ShapeDtypeStruct((rows, cols), F32),
            jax.ShapeDtypeStruct((1, rows), F32),
            jax.ShapeDtypeStruct((1, count), F32),
        ),
        in_specs=[hbm, hbm, hbm, hbm, smem, hbm, smem, hbm, hbm, smem, vmem],
        out_specs=(hbm, hbm, vmem, vmem),
        scratch_shapes=[field] * 3
        + [ids] * 2
        + [pltpu.VMEM((cols, cols), F32), dma((7,)), dma((2,)), field]
        + [field] * 9
        + [pltpu.VMEM((2, rows, cols), F32)] * 3
        + [square] * 4
        + [grown] * 3
        + [
            pltpu.VMEM((1, rows, np_ * rows), F32),
            pltpu.VMEM((order, np_ * rows), F32),
            pltpu.VMEM((order, order), F32),
            pltpu.VMEM((2, 8, wide), F32),
            pltpu.VMEM((2, 2, 8, wide), F32),
            pltpu.VMEM((8, width), F32),
            pltpu.VMEM((np_, 8, width), F32),
            pltpu.VMEM((2, 8, width), F32),
            pltpu.VMEM((np_, order, order), F32),
            pltpu.VMEM((8, LANES), F32),
            pltpu.VMEM((np_, 8, LANES), F32),
            dma,
            dma,
            pltpu.VMEM((2, 8, LANES), F32),
            pltpu.VMEM((2, 8, LANES), F32),
            pltpu.VMEM((2, np_, 8, LANES), F32),
            pltpu.VMEM((2, 2, np_, 8, LANES), F32),
            pltpu.VMEM((2, 2, 8, LANES), F32),
            pltpu.VMEM((2, 8, cols), F32),
            pltpu.VMEM((3, 8, LANES), F32),
            pltpu.VMEM((np_, 8, LANES), F32),
            pltpu.VMEM((ns, 8, LANES), F32),
            pltpu.VMEM((np_, 8, LANES), F32),
            pltpu.VMEM((count, LANES), F32),
            dma, dma, dma((2,)), dma((2,)), dma, dma, dma((2, 2)), dma((2, 2)),
            *[dma((2,))] * 6, dma((3,)), dma((3,)),
        ],
        compiler_params=pltpu.CompilerParams(
            collective_id=0, has_side_effects=True, vmem_limit_bytes=FULL
        ),
    )(load, disp, mass, wall_class, class_stiff, damper_map, damper_coef, band_tile, panel_store, owner, node_index)
    return pl.pallas_call(
        deliver,
        out_shape=tuple(jax.ShapeDtypeStruct(shape, F32) for shape in shapes),
        in_specs=[hbm] * 4,
        out_specs=(hbm,) * 4,
        scratch_shapes=[pltpu.VMEM(shape, F32) for shape in shapes] + [dma((2, 4))],
        compiler_params=pltpu.CompilerParams(vmem_limit_bytes=FULL),
    )(new_disp, adj, shear.reshape(rows), grads.reshape(count))


def solution(mesh):
    grid = P("storey", "plate")
    return jax.shard_map(
        on_device,
        mesh=mesh,
        in_specs=(grid, grid, grid, grid, P(), grid, P("storey"), grid, grid, P("storey"), grid),
        out_specs=(grid, grid, P("storey"), P("storey")),
        check_vma=False,
    )
```

```python
import functools
import math

import jax
import jax.numpy as jnp
from jax import lax
from jax.experimental import pallas as pl
from jax.experimental.pallas import tpu as pltpu
from jax.sharding import PartitionSpec as P

ITERS = 6
KF = 5.0 / 9.0
CM = 2.16
CD = 1.1
HIGH = lax.Precision.HIGHEST
MESH = pl.DeviceIdType.MESH
F32 = jnp.float32
BF16 = jnp.bfloat16
LANES = 128
FULL = 63 * 1024 * 1024


def iota(shape, dim):
    return lax.broadcasted_iota(jnp.int32, shape, dim)


def to_row(col):
    n = col.shape[0]
    return jnp.sum(jnp.where(iota((n, n), 0) == iota((n, n), 1), col, 0.0), axis=0, keepdims=True)


def to_col(row):
    n = row.shape[1]
    return jnp.sum(jnp.where(iota((n, n), 0) == iota((n, n), 1), row, 0.0), axis=1, keepdims=True)


def split(value):
    hi = value.astype(BF16)
    return hi, (value - hi.astype(F32)).astype(BF16)


def wait_bytes(ref, sem):
    pltpu.make_async_copy(ref, ref, sem).wait()


def kernel(
    ns, np_,
    load_in, disp_in, mass_in, wall_in, cstiff, dmap_in, coef, tile_in, panel, owner, nidx,
    out_disp, out_adj, out_shear, out_grads,
    load, disp, mass, wall, dmap, tile, in_sem, out_sem, found,
    stiff, diag, rdiag, cm, place, x, r, q, z,
    k_own, k_up, k_down,
    t_hi, t_lo, tt_hi, tt_lo,
    pan_own, pan_left, pan_right, pan_force, grown, used, info_out, info_in,
    spk, sslots, snb, pslots, epk, extras, x_send, x_recv,
    g1, gpk, rpk, slots, nbs, rows_in, edge_tile,
    apk, fslots, tslots, gslots, seg,
    s_send, s_recv, n_send, n_recv, p_send, p_recv, i_send, i_recv,
    r_send, r_recv, rn_send, rn_recv, e_send, e_recv, a_send, a_recv,
):
    rows, cols = load.shape
    nodes = nidx.shape[1]
    order = nodes * np_
    count = coef.shape[0]
    width = spk.shape[1]
    pieces = cols // LANES
    s = lax.axis_index("storey")
    b = lax.axis_index("plate")
    has = (s > 0, s < ns - 1)
    beside = (s - 1, s + 1)
    miss = (1 - jnp.minimum(s, 1), 1 - jnp.minimum(ns - 1 - s, 1))
    toward = (jnp.maximum(s - 1, 0), jnp.minimum(s + 1, ns - 1))
    lands = tuple((1 - way) * (1 - miss[way]) + way * miss[way] for way in range(2))
    same = tuple((b + miss[way]) % np_ for way in range(2))

    ways = ((disp_in, disp), (wall_in, wall), (mass_in, mass), (dmap_in, dmap), (tile_in, tile), (load_in, load))
    loads = [pltpu.make_async_copy(src, dst, in_sem.at[i]) for i, (src, dst) in enumerate(ways)]
    loads.append(pltpu.make_async_copy(panel, pslots.at[b], in_sem.at[len(ways)]))
    for copy in loads:
        copy.start()

    barrier = pltpu.get_barrier_semaphore()
    for d in range(1, np_):
        pl.semaphore_signal(barrier, inc=1, device_id=(s, (b + d) % np_), device_id_type=MESH)
    for d in range(1, ns):
        pl.semaphore_signal(barrier, inc=1, device_id=((s + d) % ns, b), device_id_type=MESH)
    for way in range(2):
        @pl.when(has[way])
        def _():
            for d in range(1, np_):
                pl.semaphore_signal(barrier, inc=1, device_id=(beside[way], (b + d) % np_), device_id_type=MESH)
    sides = jnp.minimum(s, 1) + jnp.minimum(ns - 1 - s, 1)
    pl.semaphore_wait(barrier, np_ - 1 + ns - 1 + sides * (np_ - 1))

    def push(src, dst, send, recv, where):
        pltpu.make_async_remote_copy(
            src_ref=src, dst_ref=dst, send_sem=send, recv_sem=recv, device_id=where, device_id_type=MESH
        ).start()

    def to_plates(src, dst, send, recv):
        for d in range(1, np_):
            push(src, dst, send, recv, (s, (b + d) % np_))

    to_plates(panel, pslots.at[b], p_send, p_recv)

    at_own = nidx[...].astype(F32)
    tiled = (iota((nodes, order), 1) % nodes == iota((nodes, order), 0)).astype(F32)
    spk[2:3, 0:order] = jnp.dot(at_own, tiled, precision=HIGH, preferred_element_type=F32)
    loads[0].wait()
    spk[0:1, 0:cols] = disp[0:1, :]
    spk[1:2, 0:cols] = disp[rows - 1 : rows, :]
    spk[3:4, 0:rows] = to_row(disp[:, 0:1])
    spk[4:5, 0:rows] = to_row(disp[:, cols - 1 : cols])
    to_plates(spk, sslots.at[b], s_send, s_recv)
    for way in range(2):
        @pl.when(has[way])
        def _():
            push(spk, snb.at[1 - way], n_send.at[way], n_recv.at[1 - way], (beside[way], b))

        @pl.when(jnp.logical_not(has[way]))
        def _():
            snb[way] = jnp.zeros(snb.shape[1:], F32)
            for i in range(2):
                info_in[i, way] = jnp.zeros(info_in.shape[2:], F32)

    loads[1].wait()
    level = jnp.zeros((rows, cols), F32)
    for c in range(cstiff.shape[0]):
        level = jnp.where(wall[...] == c, cstiff[c], level)
    stiff[...] = KF * level
    loads[2].wait()
    cm[...] = CM * mass[...]
    loads[3].wait()

    def lookup(i, carry):
        part = pl.ds(pl.multiple_of(i * 8, 8), 8)
        ids = dmap[part, :]
        value = jnp.zeros(ids.shape, F32)
        for d in range(count):
            value = jnp.where(ids == d, coef[d], value)
        total = 4.0 * stiff[part, :] + cm[part, :] + CD * value
        diag[part, :] = total
        rdiag[part, :] = 1.0 / total
        return carry

    lax.fori_loop(0, rows // 8, lookup, 0)
    loads[4].wait()
    t_hi[...], t_lo[...] = split(tile[...])
    for i, at in enumerate((0, cols - 1)):
        edge_tile[0, i : i + 1, :] = to_row(tile[:, at : at + 1])
        edge_tile[1, i : i + 1, :] = tile[at : at + 1, :]

    loads[5].wait()
    loads[6].wait()
    sslots[b] = spk[...]
    wait_bytes(sslots.at[pl.ds(0, np_ - 1)], s_recv)
    wait_bytes(pslots.at[pl.ds(0, np_ - 1)], p_recv)
    for way in range(2):
        @pl.when(has[way])
        def _():
            wait_bytes(snb.at[way], n_recv.at[way])
            wait_bytes(spk, n_send.at[way])
    wait_bytes(sslots.at[pl.ds(0, np_ - 1)], s_send)
    wait_bytes(pslots.at[pl.ds(0, np_ - 1)], p_send)

    root = owner[0]
    used_now = jnp.zeros((order, order), F32)
    for j in range(np_):
        used_now = jnp.where(root == j, pslots[j], used_now)
    used[...] = used_now
    lane_node = iota((1, order), 1) // nodes
    shift = cols.bit_length() - 1
    tall = (rows, order)
    left_slot = jnp.maximum(b - 1, 0)
    right_slot = jnp.minimum(b + 1, np_ - 1)

    def places():
        where_all = jnp.zeros((1, order), F32)
        for j in range(np_):
            where_all = jnp.where(lane_node == j, sslots[j, 2:3, 0:order], where_all)
        at = where_all.astype(jnp.int32)
        return jnp.right_shift(at, shift), jnp.bitwise_and(at, cols - 1)

    def expand_columns(mode):
        at_row, _ = places()
        at_row_col = to_col(at_row.astype(F32)).astype(jnp.int32)
        wide = (order, np_ * rows)
        spread = (
            (iota(wide, 1) % rows == at_row_col) & (iota(wide, 1) // rows == iota(wide, 0) // nodes)
        ).astype(F32).astype(BF16)
        hi, lo = split(used[...].T if mode else used[...])
        both = jnp.dot(jnp.concatenate([hi, lo], axis=0), spread, preferred_element_type=F32)
        grown[...] = both[:order] + both[order:]

    def pick(mask):
        hi, lo = split(grown[...])
        ones = mask.astype(F32).astype(BF16)
        return jnp.dot(ones, hi, preferred_element_type=F32) + jnp.dot(ones, lo, preferred_element_type=F32)

    def expand_own(mode):
        at_row, at_col = places()
        mask = (iota(tall, 0) == at_row) & (lane_node == b)
        if mode == 0:
            col_of = jnp.sum(jnp.where(mask, (at_col + 1).astype(F32), 0.0), axis=1, keepdims=True)
            place[...] = (iota((rows, cols), 1) == col_of.astype(jnp.int32) - 1).astype(F32)
        own = pick(mask)
        pan_own[mode] = own
        if mode:
            own = own * jnp.sum(place[...] * stiff[...], axis=1, keepdims=True)
        info_out[mode, 0:1, 0 : np_ * rows] = own[0:1, :]
        info_out[mode, 1:2, 0 : np_ * rows] = own[rows - 1 : rows, :]
        info_out[mode, 2:3, 0:cols] = place[0:1, :]
        info_out[mode, 3:4, 0:cols] = place[rows - 1 : rows, :]
        for way in range(2):
            @pl.when(has[way])
            def _():
                push(
                    info_out.at[mode], info_in.at[mode, 1 - way], i_send.at[mode, way],
                    i_recv.at[mode, 1 - way], (beside[way], b),
                )

    def wait_info(mode):
        for way in range(2):
            @pl.when(has[way])
            def _():
                wait_bytes(info_in.at[mode, way], i_recv.at[mode, way])
                wait_bytes(info_out.at[mode], i_send.at[mode, way])

    def expand_sides(mode):
        at_row, at_col = places()
        at_h = iota(tall, 0) == at_row
        left = at_h & (lane_node == b - 1) & (at_col == cols - 1)
        right = at_h & (lane_node == b + 1) & (at_col == 0)
        if mode:
            pan_left[mode] = pick(left) * to_col(extras[left_slot][1:2, 0:rows])
            pan_right[mode] = pick(right) * to_col(extras[right_slot][0:1, 0:rows])
        else:
            pan_left[mode] = pick(left)
            pan_right[mode] = pick(right)

    expand_columns(0)
    expand_own(0)

    eye = (iota((rows, rows), 0) == iota((rows, rows), 1)).astype(F32)
    lane = iota((rows, cols), 1)
    line = iota((rows, cols), 0)

    def sideways(v):
        return jnp.where(lane == 0, 0.0, pltpu.roll(v, 1, 1)) + jnp.where(
            lane == cols - 1, 0.0, pltpu.roll(v, cols - 1, 1)
        )

    def neighbours(v, top, bottom, left, right):
        above = jnp.where(line == 0, top, pltpu.roll(v, 1, 0))
        below = jnp.where(line == rows - 1, bottom, pltpu.roll(v, rows - 1, 0))
        west = jnp.where(lane == 0, left, pltpu.roll(v, 1, 1))
        east = jnp.where(lane == cols - 1, right, pltpu.roll(v, cols - 1, 1))
        return above + below + west + east

    def reach(mode):
        spot = place[...]
        held = stiff[...] * spot if mode else spot
        scale = (lambda v: v) if mode else (lambda v: stiff[...] * v)
        k_own[mode] = scale(sideways(held)) - diag[...] * spot
        k_up[mode] = jnp.where(line == 0, 0.0, scale(pltpu.roll(held, 1, 0)))
        k_down[mode] = jnp.where(line == rows - 1, 0.0, scale(pltpu.roll(held, rows - 1, 0)))

    def force_panel():
        at_row, _ = places()
        at_h = iota(tall, 0) == at_row
        mix = jnp.zeros(tall, F32)
        for j in range(np_):
            mix = jnp.where(at_h & (lane_node == j), to_col(extras[j, 2:3, 0:rows]), mix)
        pan_force[0] = jnp.dot(mix, grown[...], precision=HIGH, preferred_element_type=F32)

    def send_round(mode, par, edges):
        resid = r[...]
        scaled = resid * rdiag[...]
        g1[par] = to_row(jnp.sum(resid * place[...], axis=1, keepdims=True))
        gpk[par, 0:1, :] = g1[par]
        if edges:
            for i, at in enumerate((0, cols - 1)):
                value = x[:, at : at + 1] + jnp.sum(scaled * edge_tile[mode, i : i + 1, :], axis=1, keepdims=True)
                gpk[par, 1 + i : 2 + i, :] = to_row(value * stiff[:, at : at + 1] if mode else value)
        for way in range(2):
            for d in range(np_):
                if d:
                    plate, slot = (b + d) % np_, b
                else:
                    plate, slot = same[way], same[way]
                push(g1.at[par], nbs.at[par, lands[way], slot], rn_send.at[par], rn_recv.at[par], (toward[way], plate))
        to_plates(gpk.at[par], slots.at[par, b], r_send.at[par], r_recv.at[par])
        slots[par, b] = gpk[par]
        hi, lo = split(scaled)
        wh, wl = (tt_hi, tt_lo) if mode else (t_hi, t_lo)
        both = jnp.dot(jnp.concatenate([hi, lo], axis=0), wh[...], preferred_element_type=F32)
        band = both[:rows] + both[rows:] + jnp.dot(hi, wl[...], preferred_element_type=F32)
        total = x[...] + band
        z[...] = total
        if not edges:
            return
        first, last = total[0:1, :], total[rows - 1 : rows, :]
        if mode:
            first, last = first * stiff[0:1, :], last * stiff[rows - 1 : rows, :]
        for t in range(pieces):
            rpk[par, 0, t : t + 1, :] = first[:, t * LANES : (t + 1) * LANES]
            rpk[par, 1, t : t + 1, :] = last[:, t * LANES : (t + 1) * LANES]
        for way in range(2):
            push(rpk.at[par, way], rows_in.at[par, lands[way]], e_send.at[par], e_recv.at[par], (toward[way], same[way]))

    def wait_round(par, edges):
        wait_bytes(slots.at[par, pl.ds(0, np_ - 1)], r_recv.at[par])
        wait_bytes(nbs.at[par], rn_recv.at[par])
        if edges:
            wait_bytes(rows_in.at[par], e_recv.at[par])
            wait_bytes(rows_in.at[par], e_send.at[par])
        wait_bytes(slots.at[par, pl.ds(0, np_ - 1)], r_send.at[par])
        wait_bytes(nbs.at[par], rn_send.at[par])

    def applied(mat, mode, par, extra=None):
        total = extra
        for j in range(np_):
            term = mat[mode, :, j * rows : (j + 1) * rows] * slots[par, j, 0:1, :]
            total = term if total is None else total + term
        return jnp.sum(total, axis=1, keepdims=True)

    def finish(mode, par):
        coarse = jnp.broadcast_to(applied(pan_own, mode, par), (rows, LANES))
        for t in range(pieces):
            part = slice(t * LANES, (t + 1) * LANES)
            x[:, part] = z[:, part] + coarse * place[:, part]
        return coarse

    def side_row(mode, par, way):
        pan_row = 1 - way
        total = jnp.zeros((1, rows), F32)
        for j in range(np_):
            total = total + info_in[mode, way, pan_row : pan_row + 1, j * rows : (j + 1) * rows] * nbs[par, way, j, 0:1, :]
        value = jnp.sum(total, axis=1, keepdims=True)
        got = jnp.concatenate([rows_in[par, way, t : t + 1, :] for t in range(pieces)], axis=1)
        got = jnp.where(has[way], got, 0.0)
        return got + value * info_in[mode, way, 2 + (1 - way) : 3 + (1 - way), 0:cols]

    def inner_resid(mode, base):
        v = z[...]
        zero = jnp.zeros((), F32)
        if mode:
            r[...] = base[...] - diag[...] * v + neighbours(stiff[...] * v, zero, zero, zero, zero)
        else:
            r[...] = base[...] - diag[...] * v + stiff[...] * neighbours(v, zero, zero, zero, zero)

    def outer_resid(mode, par, coarse):
        up, down = pltpu.roll(coarse, 1, 0), pltpu.roll(coarse, rows - 1, 0)
        west = jnp.where(b > 0, slots[par, left_slot, 2:3, :], 0.0)
        east = jnp.where(b < np_ - 1, slots[par, right_slot, 1:2, :], 0.0)
        west = applied(pan_left, mode, par, eye * west)
        east = applied(pan_right, mode, par, eye * east)
        thin = iota((rows, LANES), 1)
        for t in range(pieces):
            part = slice(t * LANES, (t + 1) * LANES)
            total = r[:, part] + coarse * k_own[mode, :, part]
            total = total + up * k_up[mode, :, part] + down * k_down[mode, :, part]
            if t == 0:
                total = total + jnp.where(thin == 0, west if mode else west * stiff[:, part], 0.0)
            if t == pieces - 1:
                total = total + jnp.where(thin == LANES - 1, east if mode else east * stiff[:, part], 0.0)
            r[:, part] = total
        top, bottom = side_row(mode, par, 0), side_row(mode, par, 1)
        if mode == 0:
            top, bottom = top * stiff[0:1, :], bottom * stiff[rows - 1 : rows, :]
        r[0:1, :] = r[0:1, :] + top
        r[rows - 1 : rows, :] = r[rows - 1 : rows, :] + bottom

    x[...] = disp[...]
    west = jnp.where(b > 0, to_col(sslots[left_slot][4:5, 0:rows]), 0.0)
    east = jnp.where(b < np_ - 1, to_col(sslots[right_slot][3:4, 0:rows]), 0.0)
    around = neighbours(disp[...], snb[0, 1:2, 0:cols], snb[1, 0:1, 0:cols], west, east)
    r[...] = load[...] - (diag[...] * disp[...] - stiff[...] * around)

    def primal(k, carry):
        par = lax.rem(k, 2)
        send_round(0, par, True)

        @pl.when(k == 0)
        def _():
            expand_sides(0)
            reach(0)
            epk[0:1, :] = to_row(stiff[:, 0:1])
            epk[1:2, :] = to_row(stiff[:, cols - 1 : cols])
            epk[2:3, :] = to_row(jnp.sum(place[...] * cm[...], axis=1, keepdims=True))
            to_plates(epk, extras.at[b], x_send, x_recv)
            extras[b] = epk[...]

        @pl.when(k == 1)
        def _():
            wait_bytes(extras.at[pl.ds(0, np_ - 1)], x_recv)
            wait_bytes(extras.at[pl.ds(0, np_ - 1)], x_send)
            force_panel()
            expand_columns(1)
            expand_own(1)

        @pl.when(k == 2)
        def _():
            expand_sides(1)
            reach(1)

        @pl.when(k == 3)
        def _():
            tt_hi[...], tt_lo[...] = split(tile[...].T)

        inner_resid(0, load)

        @pl.when(k == 0)
        def _():
            wait_info(0)

        wait_round(par, True)
        outer_resid(0, par, finish(0, par))
        return carry

    lax.fori_loop(0, ITERS - 1, primal, 0)
    par = (ITERS - 1) % 2
    send_round(0, par, False)
    apk[0, 0:1, :] = to_row(jnp.sum(cm[...] * z[...], axis=1, keepdims=True))
    to_plates(apk.at[0], fslots.at[b], a_send.at[0], a_recv.at[0])
    fslots[b] = apk[0]
    wait_info(1)
    wait_round(par, False)
    wait_bytes(fslots.at[pl.ds(0, np_ - 1)], a_recv.at[0])
    wait_bytes(fslots.at[pl.ds(0, np_ - 1)], a_send.at[0])

    force = fslots[0, 0:1, :]
    for j in range(1, np_):
        force = force + fslots[j, 0:1, :]
    force = to_row(applied(pan_force, 0, par, eye * force))
    force = force * (8.0 / math.sqrt(cols * np_ * rows * ns))
    apk[1, 0:1, :] = force
    for d in range(1, ns):
        push(apk.at[1], tslots.at[s], a_send.at[1], a_recv.at[1], ((s + d) % ns, b))
    tslots[s] = apk[1]
    finish(0, par)
    found[...] = x[...]
    give_disp = pltpu.make_async_copy(found, out_disp, out_sem.at[0])
    give_disp.start()
    wait_bytes(tslots.at[pl.ds(0, ns - 1)], a_recv.at[1])
    wait_bytes(tslots.at[pl.ds(0, ns - 1)], a_send.at[1])
    over = jnp.zeros((1, rows), F32)
    under = jnp.zeros((1, rows), F32)
    weight = (iota((1, rows), 1) + 1).astype(F32)
    for j in range(ns):
        line_j = tslots[j, 0:1, :]
        over = over + jnp.where(s < j, line_j, 0.0)
        under = under + line_j * (jnp.where(s > j, weight, 0.0) + (rows * jnp.minimum(s, j)).astype(F32))
    over = jnp.sum(over, axis=1, keepdims=True)
    under = jnp.sum(under, axis=1, keepdims=True)
    hh, ll = iota((rows, rows), 0), iota((rows, rows), 1)
    shear = jnp.sum(jnp.where(ll >= hh, force, 0.0), axis=1, keepdims=True) + over
    out_shear[...] = to_row(shear)
    local = jnp.sum(force * (jnp.minimum(hh, ll) + 1).astype(F32), axis=1, keepdims=True)
    step = (iota((rows, 1), 0) + 1).astype(F32)
    drift = (local + step * over + under) * (1.0 / (rows * ns))
    q[...] = cm[...] * drift
    r[...] = q[...]
    x[...] = jnp.zeros((rows, cols), F32)

    def adjoint(k, carry):
        par = lax.rem(k, 2)
        send_round(1, par, True)
        inner_resid(1, q)
        wait_round(par, True)
        outer_resid(1, par, finish(1, par))
        return carry

    lax.fori_loop(0, ITERS - 1, adjoint, 0)
    send_round(1, par, False)

    q[...] = z[...] * found[...]
    group = 8
    for first in range(0, count, group):
        def gather(i, accs):
            part = pl.ds(pl.multiple_of(i * 8, 8), 8)
            ids, vals = dmap[part, :], q[part, :]
            res = []
            for d in range(group):
                kept = jnp.where(ids == first + d, vals, 0.0)
                acc = accs[d]
                for t in range(pieces):
                    acc = acc + kept[:, t * LANES : (t + 1) * LANES]
                res.append(acc)
            return tuple(res)

        accs = lax.fori_loop(0, rows // 8, gather, tuple(jnp.zeros((8, LANES), F32) for _ in range(group)))
        for d in range(group):
            seg[first + d : first + d + 1, :] = jnp.sum(accs[d], axis=0, keepdims=True)
    sums = to_row(jnp.sum(seg[...], axis=1, keepdims=True))
    damper = jnp.sum(place[...] * dmap[...].astype(F32), axis=1, keepdims=True)
    held = jnp.sum(place[...] * found[...], axis=1, keepdims=True)
    hits = jnp.where(damper == iota((rows, count), 1).astype(F32), held, 0.0)
    wait_round(par, False)
    coarse = finish(1, par)
    give_adj = pltpu.make_async_copy(x, out_adj, out_sem.at[1])
    give_adj.start()
    sums = sums + jnp.sum(hits * coarse[:, 0:count], axis=0, keepdims=True)
    apk[2, 0:1, 0:count] = sums
    to_plates(apk.at[2], gslots.at[b], a_send.at[2], a_recv.at[2])
    gslots[b] = apk[2]
    wait_bytes(gslots.at[pl.ds(0, np_ - 1)], a_recv.at[2])
    wait_bytes(gslots.at[pl.ds(0, np_ - 1)], a_send.at[2])
    sums = gslots[0, 0:1, 0:count]
    for j in range(1, np_):
        sums = sums + gslots[j, 0:1, 0:count]
    out_grads[...] = sums * (-CD * 64.0 / math.sqrt(rows * cols * np_ / count))
    give_disp.wait()
    give_adj.wait()


def deliver(*refs):
    source, target, room, sems = refs[:4], refs[4:8], refs[8:12], refs[12]
    ins = [pltpu.make_async_copy(source[i], room[i], sems.at[0, i]) for i in range(4)]
    outs = [pltpu.make_async_copy(room[i], target[i], sems.at[1, i]) for i in range(4)]
    for copy in ins:
        copy.start()
    for i in range(4):
        ins[i].wait()
        outs[i].start()
    for copy in outs:
        copy.wait()


def on_device(load, disp, mass, wall_class, class_stiff, damper_map, damper_coef, band_tile, panel_store, owner, node_index):
    rows, cols = load.shape
    ns = lax.axis_size("storey")
    np_ = lax.axis_size("plate")
    nodes = node_index.shape[1]
    order = nodes * np_
    count = damper_coef.shape[0]
    width = max(cols, order, rows)
    wide = max(cols, np_ * rows)
    field = pltpu.VMEM((rows, cols), F32)
    square = pltpu.VMEM((cols, cols), BF16)
    grown = pltpu.VMEM((2, rows, np_ * rows), F32)
    dma = pltpu.SemaphoreType.DMA
    vmem = pl.BlockSpec(memory_space=pltpu.VMEM)
    smem = pl.BlockSpec(memory_space=pltpu.SMEM)
    hbm = pl.BlockSpec(memory_space=pltpu.HBM)
    ids = pltpu.VMEM((rows, cols), jnp.int32)
    shapes = ((rows, cols), (rows, cols), (rows,), (count,))
    new_disp, adj, shear, grads = pl.pallas_call(
        functools.partial(kernel, ns, np_),
        out_shape=(
            jax.ShapeDtypeStruct((rows, cols), F32),
            jax.ShapeDtypeStruct((rows, cols), F32),
            jax.ShapeDtypeStruct((1, rows), F32),
            jax.ShapeDtypeStruct((1, count), F32),
        ),
        in_specs=[hbm, hbm, hbm, hbm, smem, hbm, smem, hbm, hbm, smem, vmem],
        out_specs=(hbm, hbm, vmem, vmem),
        scratch_shapes=[field] * 3
        + [ids] * 2
        + [pltpu.VMEM((cols, cols), F32), dma((7,)), dma((2,)), field]
        + [field] * 9
        + [pltpu.VMEM((2, rows, cols), F32)] * 3
        + [square] * 4
        + [grown] * 3
        + [
            pltpu.VMEM((1, rows, np_ * rows), F32),
            pltpu.VMEM((order, np_ * rows), F32),
            pltpu.VMEM((order, order), F32),
            pltpu.VMEM((2, 8, wide), F32),
            pltpu.VMEM((2, 2, 8, wide), F32),
            pltpu.VMEM((8, width), F32),
            pltpu.VMEM((np_, 8, width), F32),
            pltpu.VMEM((2, 8, width), F32),
            pltpu.VMEM((np_, order, order), F32),
            pltpu.VMEM((8, LANES), F32),
            pltpu.VMEM((np_, 8, LANES), F32),
            dma,
            dma,
            pltpu.VMEM((2, 1, LANES), F32),
            pltpu.VMEM((2, 4, LANES), F32),
            pltpu.VMEM((2, 2, cols // LANES, LANES), F32),
            pltpu.VMEM((2, np_, 4, LANES), F32),
            pltpu.VMEM((2, 2, np_, 1, LANES), F32),
            pltpu.VMEM((2, 2, cols // LANES, LANES), F32),
            pltpu.VMEM((2, 8, cols), F32),
            pltpu.VMEM((3, 1, LANES), F32),
            pltpu.VMEM((np_, 1, LANES), F32),
            pltpu.VMEM((ns, 1, LANES), F32),
            pltpu.VMEM((np_, 1, LANES), F32),
            pltpu.VMEM((count, LANES), F32),
            dma, dma, dma((2,)), dma((2,)), dma, dma, dma((2, 2)), dma((2, 2)),
            *[dma((2,))] * 6, dma((3,)), dma((3,)),
        ],
        compiler_params=pltpu.CompilerParams(
            collective_id=0, has_side_effects=True, vmem_limit_bytes=FULL
        ),
    )(load, disp, mass, wall_class, class_stiff, damper_map, damper_coef, band_tile, panel_store, owner, node_index)
    return pl.pallas_call(
        deliver,
        out_shape=tuple(jax.ShapeDtypeStruct(shape, F32) for shape in shapes),
        in_specs=[hbm] * 4,
        out_specs=(hbm,) * 4,
        scratch_shapes=[pltpu.VMEM(shape, F32) for shape in shapes] + [dma((2, 4))],
        compiler_params=pltpu.CompilerParams(vmem_limit_bytes=FULL),
    )(new_disp, adj, shear.reshape(rows), grads.reshape(count))


def solution(mesh):
    grid = P("storey", "plate")
    return jax.shard_map(
        on_device,
        mesh=mesh,
        in_specs=(grid, grid, grid, grid, P(), grid, P("storey"), grid, grid, P("storey"), grid),
        out_specs=(grid, grid, P("storey"), P("storey")),
        check_vma=False,
    )
```

```python
import functools
import math

import jax
import jax.numpy as jnp
from jax import lax
from jax.experimental import pallas as pl
from jax.experimental.pallas import tpu as pltpu
from jax.sharding import PartitionSpec as P

ITERS = 6
KF = 5.0 / 9.0
CM = 2.16
CD = 1.1
HIGH = lax.Precision.HIGHEST
MESH = pl.DeviceIdType.MESH
F32 = jnp.float32
BF16 = jnp.bfloat16
LANES = 128
FULL = 63 * 1024 * 1024


def iota(shape, dim):
    return lax.broadcasted_iota(jnp.int32, shape, dim)


def to_row(col):
    n = col.shape[0]
    return jnp.sum(jnp.where(iota((n, n), 0) == iota((n, n), 1), col, 0.0), axis=0, keepdims=True)


def to_col(row):
    n = row.shape[1]
    return jnp.sum(jnp.where(iota((n, n), 0) == iota((n, n), 1), row, 0.0), axis=1, keepdims=True)


def split(value):
    hi = value.astype(BF16)
    return hi, (value - hi.astype(F32)).astype(BF16)


def wait_bytes(ref, sem):
    pltpu.make_async_copy(ref, ref, sem).wait()


def kernel(
    ns, np_,
    load_in, disp_in, mass_in, wall_in, cstiff, dmap_in, coef, tile_in, panel, owner, nidx,
    out_disp, out_adj, out_shear, out_grads,
    load, disp, mass, wall, dmap, tile, in_sem, out_sem, found,
    stiff, diag, rdiag, cm, place, x, r, q, z,
    k_own, k_up, k_down,
    t_hi, t_lo, tt_hi, tt_lo,
    pan_own, pan_left, pan_right, pan_force, grown, used, info_out, info_in,
    spk, sslots, snb, pslots, epk, extras, x_send, x_recv,
    g1, gpk, rpk, slots, nbs, rows_in, edge_tile,
    apk, fslots, tslots, gslots, seg,
    s_send, s_recv, n_send, n_recv, p_send, p_recv, i_send, i_recv,
    r_send, r_recv, rn_send, rn_recv, e_send, e_recv, a_send, a_recv,
):
    rows, cols = load.shape
    nodes = nidx.shape[1]
    order = nodes * np_
    count = coef.shape[0]
    width = spk.shape[1]
    pieces = cols // LANES
    s = lax.axis_index("storey")
    b = lax.axis_index("plate")
    has = (s > 0, s < ns - 1)
    beside = (s - 1, s + 1)
    miss = (1 - jnp.minimum(s, 1), 1 - jnp.minimum(ns - 1 - s, 1))
    toward = (jnp.maximum(s - 1, 0), jnp.minimum(s + 1, ns - 1))
    lands = tuple((1 - way) * (1 - miss[way]) + way * miss[way] for way in range(2))
    same = tuple((b + miss[way]) % np_ for way in range(2))

    ways = ((disp_in, disp), (wall_in, wall), (mass_in, mass), (dmap_in, dmap), (tile_in, tile), (load_in, load))
    loads = [pltpu.make_async_copy(src, dst, in_sem.at[i]) for i, (src, dst) in enumerate(ways)]
    loads.append(pltpu.make_async_copy(panel, pslots.at[b], in_sem.at[len(ways)]))
    for copy in loads:
        copy.start()

    barrier = pltpu.get_barrier_semaphore()
    for d in range(1, np_):
        pl.semaphore_signal(barrier, inc=1, device_id=(s, (b + d) % np_), device_id_type=MESH)
    for d in range(1, ns):
        pl.semaphore_signal(barrier, inc=1, device_id=((s + d) % ns, b), device_id_type=MESH)
    for way in range(2):
        @pl.when(has[way])
        def _():
            for d in range(1, np_):
                pl.semaphore_signal(barrier, inc=1, device_id=(beside[way], (b + d) % np_), device_id_type=MESH)
    sides = jnp.minimum(s, 1) + jnp.minimum(ns - 1 - s, 1)
    pl.semaphore_wait(barrier, np_ - 1 + ns - 1 + sides * (np_ - 1))

    def push(src, dst, send, recv, where):
        pltpu.make_async_remote_copy(
            src_ref=src, dst_ref=dst, send_sem=send, recv_sem=recv, device_id=where, device_id_type=MESH
        ).start()

    def to_plates(src, dst, send, recv):
        for d in range(1, np_):
            push(src, dst, send, recv, (s, (b + d) % np_))

    to_plates(panel, pslots.at[b], p_send, p_recv)

    at_own = nidx[...].astype(F32)
    tiled = (iota((nodes, order), 1) % nodes == iota((nodes, order), 0)).astype(F32)
    spk[2:3, 0:order] = jnp.dot(at_own, tiled, precision=HIGH, preferred_element_type=F32)
    loads[0].wait()
    spk[0:1, 0:cols] = disp[0:1, :]
    spk[1:2, 0:cols] = disp[rows - 1 : rows, :]
    spk[3:4, 0:rows] = to_row(disp[:, 0:1])
    spk[4:5, 0:rows] = to_row(disp[:, cols - 1 : cols])
    to_plates(spk, sslots.at[b], s_send, s_recv)
    for way in range(2):
        @pl.when(has[way])
        def _():
            push(spk, snb.at[1 - way], n_send.at[way], n_recv.at[1 - way], (beside[way], b))

        @pl.when(jnp.logical_not(has[way]))
        def _():
            snb[way] = jnp.zeros(snb.shape[1:], F32)
            for i in range(2):
                info_in[i, way] = jnp.zeros(info_in.shape[2:], F32)

    loads[1].wait()
    level = jnp.zeros((rows, cols), F32)
    for c in range(cstiff.shape[0]):
        level = jnp.where(wall[...] == c, cstiff[c], level)
    stiff[...] = KF * level
    loads[2].wait()
    cm[...] = CM * mass[...]
    loads[3].wait()

    def lookup(i, carry):
        part = pl.ds(pl.multiple_of(i * 8, 8), 8)
        ids = dmap[part, :]
        value = jnp.zeros(ids.shape, F32)
        for d in range(count):
            value = jnp.where(ids == d, coef[d], value)
        total = 4.0 * stiff[part, :] + cm[part, :] + CD * value
        diag[part, :] = total
        rdiag[part, :] = 1.0 / total
        return carry

    lax.fori_loop(0, rows // 8, lookup, 0)
    loads[4].wait()
    t_hi[...], t_lo[...] = split(tile[...])
    for i, at in enumerate((0, cols - 1)):
        edge_tile[0, i : i + 1, :] = to_row(tile[:, at : at + 1])
        edge_tile[1, i : i + 1, :] = tile[at : at + 1, :]

    loads[5].wait()
    loads[6].wait()
    sslots[b] = spk[...]
    wait_bytes(sslots.at[pl.ds(0, np_ - 1)], s_recv)
    wait_bytes(pslots.at[pl.ds(0, np_ - 1)], p_recv)
    for way in range(2):
        @pl.when(has[way])
        def _():
            wait_bytes(snb.at[way], n_recv.at[way])
            wait_bytes(spk, n_send.at[way])
    wait_bytes(sslots.at[pl.ds(0, np_ - 1)], s_send)
    wait_bytes(pslots.at[pl.ds(0, np_ - 1)], p_send)

    root = owner[0]
    used_now = jnp.zeros((order, order), F32)
    for j in range(np_):
        used_now = jnp.where(root == j, pslots[j], used_now)
    used[...] = used_now
    lane_node = iota((1, order), 1) // nodes
    shift = cols.bit_length() - 1
    tall = (rows, order)
    left_slot = jnp.maximum(b - 1, 0)
    right_slot = jnp.minimum(b + 1, np_ - 1)

    def places():
        where_all = jnp.zeros((1, order), F32)
        for j in range(np_):
            where_all = jnp.where(lane_node == j, sslots[j, 2:3, 0:order], where_all)
        at = where_all.astype(jnp.int32)
        return jnp.right_shift(at, shift), jnp.bitwise_and(at, cols - 1)

    def expand_columns(mode):
        at_row, _ = places()
        at_row_col = to_col(at_row.astype(F32)).astype(jnp.int32)
        wide = (order, np_ * rows)
        spread = (
            (iota(wide, 1) % rows == at_row_col) & (iota(wide, 1) // rows == iota(wide, 0) // nodes)
        ).astype(F32).astype(BF16)
        hi, lo = split(used[...].T if mode else used[...])
        both = jnp.dot(jnp.concatenate([hi, lo], axis=0), spread, preferred_element_type=F32)
        grown[...] = both[:order] + both[order:]

    def pick(mask):
        hi, lo = split(grown[...])
        ones = mask.astype(F32).astype(BF16)
        return jnp.dot(ones, hi, preferred_element_type=F32) + jnp.dot(ones, lo, preferred_element_type=F32)

    def expand_own(mode):
        at_row, at_col = places()
        mask = (iota(tall, 0) == at_row) & (lane_node == b)
        if mode == 0:
            col_of = jnp.sum(jnp.where(mask, (at_col + 1).astype(F32), 0.0), axis=1, keepdims=True)
            place[...] = (iota((rows, cols), 1) == col_of.astype(jnp.int32) - 1).astype(F32)
        own = pick(mask)
        pan_own[mode] = own
        if mode:
            own = own * jnp.sum(place[...] * stiff[...], axis=1, keepdims=True)
        info_out[mode, 0:1, 0 : np_ * rows] = own[0:1, :]
        info_out[mode, 1:2, 0 : np_ * rows] = own[rows - 1 : rows, :]
        info_out[mode, 2:3, 0:cols] = place[0:1, :]
        info_out[mode, 3:4, 0:cols] = place[rows - 1 : rows, :]
        for way in range(2):
            @pl.when(has[way])
            def _():
                push(
                    info_out.at[mode], info_in.at[mode, 1 - way], i_send.at[mode, way],
                    i_recv.at[mode, 1 - way], (beside[way], b),
                )

    def wait_info(mode):
        for way in range(2):
            @pl.when(has[way])
            def _():
                wait_bytes(info_in.at[mode, way], i_recv.at[mode, way])
                wait_bytes(info_out.at[mode], i_send.at[mode, way])

    def expand_sides(mode):
        at_row, at_col = places()
        at_h = iota(tall, 0) == at_row
        left = at_h & (lane_node == b - 1) & (at_col == cols - 1)
        right = at_h & (lane_node == b + 1) & (at_col == 0)
        if mode:
            pan_left[mode] = pick(left) * to_col(extras[left_slot][1:2, 0:rows])
            pan_right[mode] = pick(right) * to_col(extras[right_slot][0:1, 0:rows])
        else:
            pan_left[mode] = pick(left)
            pan_right[mode] = pick(right)

    expand_columns(0)
    expand_own(0)

    eye = (iota((rows, rows), 0) == iota((rows, rows), 1)).astype(F32)
    lane = iota((rows, cols), 1)
    line = iota((rows, cols), 0)

    def sideways(v):
        return jnp.where(lane == 0, 0.0, pltpu.roll(v, 1, 1)) + jnp.where(
            lane == cols - 1, 0.0, pltpu.roll(v, cols - 1, 1)
        )

    def neighbours(v, top, bottom, left, right):
        above = jnp.where(line == 0, top, pltpu.roll(v, 1, 0))
        below = jnp.where(line == rows - 1, bottom, pltpu.roll(v, rows - 1, 0))
        west = jnp.where(lane == 0, left, pltpu.roll(v, 1, 1))
        east = jnp.where(lane == cols - 1, right, pltpu.roll(v, cols - 1, 1))
        return above + below + west + east

    def reach(mode):
        spot = place[...]
        held = stiff[...] * spot if mode else spot
        scale = (lambda v: v) if mode else (lambda v: stiff[...] * v)
        k_own[mode] = scale(sideways(held)) - diag[...] * spot
        k_up[mode] = jnp.where(line == 0, 0.0, scale(pltpu.roll(held, 1, 0)))
        k_down[mode] = jnp.where(line == rows - 1, 0.0, scale(pltpu.roll(held, rows - 1, 0)))

    def force_panel():
        at_row, _ = places()
        at_h = iota(tall, 0) == at_row
        mix = jnp.zeros(tall, F32)
        for j in range(np_):
            mix = jnp.where(at_h & (lane_node == j), to_col(extras[j, 2:3, 0:rows]), mix)
        pan_force[0] = jnp.dot(mix, grown[...], precision=HIGH, preferred_element_type=F32)

    def send_round(mode, par, edges):
        resid = r[...]
        scaled = resid * rdiag[...]
        g1[par] = to_row(jnp.sum(resid * place[...], axis=1, keepdims=True))
        gpk[par, 0:1, :] = g1[par]
        if edges:
            for i, at in enumerate((0, cols - 1)):
                value = x[:, at : at + 1] + jnp.sum(scaled * edge_tile[mode, i : i + 1, :], axis=1, keepdims=True)
                gpk[par, 1 + i : 2 + i, :] = to_row(value * stiff[:, at : at + 1] if mode else value)
        for way in range(2):
            for d in range(np_):
                if d:
                    plate, slot = (b + d) % np_, b
                else:
                    plate, slot = same[way], same[way]
                push(g1.at[par], nbs.at[par, lands[way], slot], rn_send.at[par], rn_recv.at[par], (toward[way], plate))
        to_plates(gpk.at[par], slots.at[par, b], r_send.at[par], r_recv.at[par])
        slots[par, b] = gpk[par]
        hi, lo = split(scaled)
        wh, wl = (tt_hi, tt_lo) if mode else (t_hi, t_lo)
        both = jnp.dot(jnp.concatenate([hi, lo], axis=0), wh[...], preferred_element_type=F32)
        band = both[:rows] + both[rows:] + jnp.dot(hi, wl[...], preferred_element_type=F32)
        total = x[...] + band
        z[...] = total
        if not edges:
            return
        first, last = total[0:1, :], total[rows - 1 : rows, :]
        if mode:
            first, last = first * stiff[0:1, :], last * stiff[rows - 1 : rows, :]
        for t in range(pieces):
            rpk[par, 0, t : t + 1, :] = first[:, t * LANES : (t + 1) * LANES]
            rpk[par, 1, t : t + 1, :] = last[:, t * LANES : (t + 1) * LANES]
        for way in range(2):
            push(rpk.at[par, way], rows_in.at[par, lands[way]], e_send.at[par], e_recv.at[par], (toward[way], same[way]))

    def wait_plates(par):
        wait_bytes(slots.at[par, pl.ds(0, np_ - 1)], r_recv.at[par])

    def wait_storeys(par, edges):
        wait_bytes(nbs.at[par], rn_recv.at[par])
        if edges:
            wait_bytes(rows_in.at[par], e_recv.at[par])
            wait_bytes(rows_in.at[par], e_send.at[par])
        wait_bytes(slots.at[par, pl.ds(0, np_ - 1)], r_send.at[par])
        wait_bytes(nbs.at[par], rn_send.at[par])

    def applied(mat, mode, par, extra=None):
        total = extra
        for j in range(np_):
            term = mat[mode, :, j * rows : (j + 1) * rows] * slots[par, j, 0:1, :]
            total = term if total is None else total + term
        return jnp.sum(total, axis=1, keepdims=True)

    def finish(mode, par):
        coarse = jnp.broadcast_to(applied(pan_own, mode, par), (rows, LANES))
        for t in range(pieces):
            part = slice(t * LANES, (t + 1) * LANES)
            x[:, part] = z[:, part] + coarse * place[:, part]
        return coarse

    def side_row(mode, par, way):
        pan_row = 1 - way
        total = jnp.zeros((1, rows), F32)
        for j in range(np_):
            total = total + info_in[mode, way, pan_row : pan_row + 1, j * rows : (j + 1) * rows] * nbs[par, way, j, 0:1, :]
        value = jnp.sum(total, axis=1, keepdims=True)
        got = jnp.concatenate([rows_in[par, way, t : t + 1, :] for t in range(pieces)], axis=1)
        got = jnp.where(has[way], got, 0.0)
        return got + value * info_in[mode, way, 2 + (1 - way) : 3 + (1 - way), 0:cols]

    def inner_resid(mode, base):
        v = z[...]
        zero = jnp.zeros((), F32)
        if mode:
            r[...] = base[...] - diag[...] * v + neighbours(stiff[...] * v, zero, zero, zero, zero)
        else:
            r[...] = base[...] - diag[...] * v + stiff[...] * neighbours(v, zero, zero, zero, zero)

    def outer_resid(mode, par, coarse):
        up, down = pltpu.roll(coarse, 1, 0), pltpu.roll(coarse, rows - 1, 0)
        west = jnp.where(b > 0, slots[par, left_slot, 2:3, :], 0.0)
        east = jnp.where(b < np_ - 1, slots[par, right_slot, 1:2, :], 0.0)
        west = applied(pan_left, mode, par, eye * west)
        east = applied(pan_right, mode, par, eye * east)
        thin = iota((rows, LANES), 1)
        for t in range(pieces):
            part = slice(t * LANES, (t + 1) * LANES)
            total = r[:, part] + coarse * k_own[mode, :, part]
            total = total + up * k_up[mode, :, part] + down * k_down[mode, :, part]
            if t == 0:
                total = total + jnp.where(thin == 0, west if mode else west * stiff[:, part], 0.0)
            if t == pieces - 1:
                total = total + jnp.where(thin == LANES - 1, east if mode else east * stiff[:, part], 0.0)
            r[:, part] = total

    def edge_resid(mode, par):
        top, bottom = side_row(mode, par, 0), side_row(mode, par, 1)
        if mode == 0:
            top, bottom = top * stiff[0:1, :], bottom * stiff[rows - 1 : rows, :]
        r[0:1, :] = r[0:1, :] + top
        r[rows - 1 : rows, :] = r[rows - 1 : rows, :] + bottom

    x[...] = disp[...]
    west = jnp.where(b > 0, to_col(sslots[left_slot][4:5, 0:rows]), 0.0)
    east = jnp.where(b < np_ - 1, to_col(sslots[right_slot][3:4, 0:rows]), 0.0)
    around = neighbours(disp[...], snb[0, 1:2, 0:cols], snb[1, 0:1, 0:cols], west, east)
    r[...] = load[...] - (diag[...] * disp[...] - stiff[...] * around)

    def primal(k, carry):
        par = lax.rem(k, 2)
        send_round(0, par, True)

        @pl.when(k == 0)
        def _():
            expand_sides(0)
            reach(0)
            epk[0:1, :] = to_row(stiff[:, 0:1])
            epk[1:2, :] = to_row(stiff[:, cols - 1 : cols])
            epk[2:3, :] = to_row(jnp.sum(place[...] * cm[...], axis=1, keepdims=True))
            to_plates(epk, extras.at[b], x_send, x_recv)
            extras[b] = epk[...]

        @pl.when(k == 1)
        def _():
            wait_bytes(extras.at[pl.ds(0, np_ - 1)], x_recv)
            wait_bytes(extras.at[pl.ds(0, np_ - 1)], x_send)
            force_panel()
            expand_columns(1)
            expand_own(1)

        @pl.when(k == 2)
        def _():
            expand_sides(1)
            reach(1)

        @pl.when(k == 3)
        def _():
            tt_hi[...], tt_lo[...] = split(tile[...].T)

        inner_resid(0, load)
        wait_plates(par)

        @pl.when(k == 0)
        def _():
            wait_info(0)

        outer_resid(0, par, finish(0, par))
        wait_storeys(par, True)
        edge_resid(0, par)
        return carry

    lax.fori_loop(0, ITERS - 1, primal, 0)
    par = (ITERS - 1) % 2
    send_round(0, par, False)
    apk[0, 0:1, :] = to_row(jnp.sum(cm[...] * z[...], axis=1, keepdims=True))
    to_plates(apk.at[0], fslots.at[b], a_send.at[0], a_recv.at[0])
    fslots[b] = apk[0]
    wait_info(1)
    wait_plates(par)
    wait_bytes(fslots.at[pl.ds(0, np_ - 1)], a_recv.at[0])
    wait_bytes(fslots.at[pl.ds(0, np_ - 1)], a_send.at[0])

    force = fslots[0, 0:1, :]
    for j in range(1, np_):
        force = force + fslots[j, 0:1, :]
    force = to_row(applied(pan_force, 0, par, eye * force))
    force = force * (8.0 / math.sqrt(cols * np_ * rows * ns))
    apk[1, 0:1, :] = force
    for d in range(1, ns):
        push(apk.at[1], tslots.at[s], a_send.at[1], a_recv.at[1], ((s + d) % ns, b))
    tslots[s] = apk[1]
    wait_storeys(par, False)
    finish(0, par)
    found[...] = x[...]
    give_disp = pltpu.make_async_copy(found, out_disp, out_sem.at[0])
    give_disp.start()
    wait_bytes(tslots.at[pl.ds(0, ns - 1)], a_recv.at[1])
    wait_bytes(tslots.at[pl.ds(0, ns - 1)], a_send.at[1])
    over = jnp.zeros((1, rows), F32)
    under = jnp.zeros((1, rows), F32)
    weight = (iota((1, rows), 1) + 1).astype(F32)
    for j in range(ns):
        line_j = tslots[j, 0:1, :]
        over = over + jnp.where(s < j, line_j, 0.0)
        under = under + line_j * (jnp.where(s > j, weight, 0.0) + (rows * jnp.minimum(s, j)).astype(F32))
    over = jnp.sum(over, axis=1, keepdims=True)
    under = jnp.sum(under, axis=1, keepdims=True)
    hh, ll = iota((rows, rows), 0), iota((rows, rows), 1)
    shear = jnp.sum(jnp.where(ll >= hh, force, 0.0), axis=1, keepdims=True) + over
    out_shear[...] = to_row(shear)
    local = jnp.sum(force * (jnp.minimum(hh, ll) + 1).astype(F32), axis=1, keepdims=True)
    step = (iota((rows, 1), 0) + 1).astype(F32)
    drift = (local + step * over + under) * (1.0 / (rows * ns))
    q[...] = cm[...] * drift
    r[...] = q[...]
    x[...] = jnp.zeros((rows, cols), F32)

    def adjoint(k, carry):
        par = lax.rem(k, 2)
        send_round(1, par, True)
        inner_resid(1, q)
        wait_plates(par)
        outer_resid(1, par, finish(1, par))
        wait_storeys(par, True)
        edge_resid(1, par)
        return carry

    lax.fori_loop(0, ITERS - 1, adjoint, 0)
    send_round(1, par, False)

    q[...] = z[...] * found[...]
    group = 8
    for first in range(0, count, group):
        def gather(i, accs):
            part = pl.ds(pl.multiple_of(i * 8, 8), 8)
            ids, vals = dmap[part, :], q[part, :]
            res = []
            for d in range(group):
                kept = jnp.where(ids == first + d, vals, 0.0)
                acc = accs[d]
                for t in range(pieces):
                    acc = acc + kept[:, t * LANES : (t + 1) * LANES]
                res.append(acc)
            return tuple(res)

        accs = lax.fori_loop(0, rows // 8, gather, tuple(jnp.zeros((8, LANES), F32) for _ in range(group)))
        for d in range(group):
            seg[first + d : first + d + 1, :] = jnp.sum(accs[d], axis=0, keepdims=True)
    sums = to_row(jnp.sum(seg[...], axis=1, keepdims=True))
    damper = jnp.sum(place[...] * dmap[...].astype(F32), axis=1, keepdims=True)
    held = jnp.sum(place[...] * found[...], axis=1, keepdims=True)
    hits = jnp.where(damper == iota((rows, count), 1).astype(F32), held, 0.0)
    wait_plates(par)
    coarse = finish(1, par)
    give_adj = pltpu.make_async_copy(x, out_adj, out_sem.at[1])
    give_adj.start()
    sums = sums + jnp.sum(hits * coarse[:, 0:count], axis=0, keepdims=True)
    apk[2, 0:1, 0:count] = sums
    to_plates(apk.at[2], gslots.at[b], a_send.at[2], a_recv.at[2])
    gslots[b] = apk[2]
    wait_storeys(par, False)
    wait_bytes(gslots.at[pl.ds(0, np_ - 1)], a_recv.at[2])
    wait_bytes(gslots.at[pl.ds(0, np_ - 1)], a_send.at[2])
    sums = gslots[0, 0:1, 0:count]
    for j in range(1, np_):
        sums = sums + gslots[j, 0:1, 0:count]
    out_grads[...] = sums * (-CD * 64.0 / math.sqrt(rows * cols * np_ / count))
    give_disp.wait()
    give_adj.wait()


def deliver(*refs):
    source, target, room, sems = refs[:4], refs[4:8], refs[8:12], refs[12]
    ins = [pltpu.make_async_copy(source[i], room[i], sems.at[0, i]) for i in range(4)]
    outs = [pltpu.make_async_copy(room[i], target[i], sems.at[1, i]) for i in range(4)]
    for copy in ins:
        copy.start()
    for i in range(4):
        ins[i].wait()
        outs[i].start()
    for copy in outs:
        copy.wait()


def on_device(load, disp, mass, wall_class, class_stiff, damper_map, damper_coef, band_tile, panel_store, owner, node_index):
    rows, cols = load.shape
    ns = lax.axis_size("storey")
    np_ = lax.axis_size("plate")
    nodes = node_index.shape[1]
    order = nodes * np_
    count = damper_coef.shape[0]
    width = max(cols, order, rows)
    wide = max(cols, np_ * rows)
    field = pltpu.VMEM((rows, cols), F32)
    square = pltpu.VMEM((cols, cols), BF16)
    grown = pltpu.VMEM((2, rows, np_ * rows), F32)
    dma = pltpu.SemaphoreType.DMA
    vmem = pl.BlockSpec(memory_space=pltpu.VMEM)
    smem = pl.BlockSpec(memory_space=pltpu.SMEM)
    hbm = pl.BlockSpec(memory_space=pltpu.HBM)
    ids = pltpu.VMEM((rows, cols), jnp.int32)
    shapes = ((rows, cols), (rows, cols), (rows,), (count,))
    new_disp, adj, shear, grads = pl.pallas_call(
        functools.partial(kernel, ns, np_),
        out_shape=(
            jax.ShapeDtypeStruct((rows, cols), F32),
            jax.ShapeDtypeStruct((rows, cols), F32),
            jax.ShapeDtypeStruct((1, rows), F32),
            jax.ShapeDtypeStruct((1, count), F32),
        ),
        in_specs=[hbm, hbm, hbm, hbm, smem, hbm, smem, hbm, hbm, smem, vmem],
        out_specs=(hbm, hbm, vmem, vmem),
        scratch_shapes=[field] * 3
        + [ids] * 2
        + [pltpu.VMEM((cols, cols), F32), dma((7,)), dma((2,)), field]
        + [field] * 9
        + [pltpu.VMEM((2, rows, cols), F32)] * 3
        + [square] * 4
        + [grown] * 3
        + [
            pltpu.VMEM((1, rows, np_ * rows), F32),
            pltpu.VMEM((order, np_ * rows), F32),
            pltpu.VMEM((order, order), F32),
            pltpu.VMEM((2, 8, wide), F32),
            pltpu.VMEM((2, 2, 8, wide), F32),
            pltpu.VMEM((8, width), F32),
            pltpu.VMEM((np_, 8, width), F32),
            pltpu.VMEM((2, 8, width), F32),
            pltpu.VMEM((np_, order, order), F32),
            pltpu.VMEM((8, LANES), F32),
            pltpu.VMEM((np_, 8, LANES), F32),
            dma,
            dma,
            pltpu.VMEM((2, 1, LANES), F32),
            pltpu.VMEM((2, 4, LANES), F32),
            pltpu.VMEM((2, 2, cols // LANES, LANES), F32),
            pltpu.VMEM((2, np_, 4, LANES), F32),
            pltpu.VMEM((2, 2, np_, 1, LANES), F32),
            pltpu.VMEM((2, 2, cols // LANES, LANES), F32),
            pltpu.VMEM((2, 8, cols), F32),
            pltpu.VMEM((3, 1, LANES), F32),
            pltpu.VMEM((np_, 1, LANES), F32),
            pltpu.VMEM((ns, 1, LANES), F32),
            pltpu.VMEM((np_, 1, LANES), F32),
            pltpu.VMEM((count, LANES), F32),
            dma, dma, dma((2,)), dma((2,)), dma, dma, dma((2, 2)), dma((2, 2)),
            *[dma((2,))] * 6, dma((3,)), dma((3,)),
        ],
        compiler_params=pltpu.CompilerParams(
            collective_id=0, has_side_effects=True, vmem_limit_bytes=FULL
        ),
    )(load, disp, mass, wall_class, class_stiff, damper_map, damper_coef, band_tile, panel_store, owner, node_index)
    return pl.pallas_call(
        deliver,
        out_shape=tuple(jax.ShapeDtypeStruct(shape, F32) for shape in shapes),
        in_specs=[hbm] * 4,
        out_specs=(hbm,) * 4,
        scratch_shapes=[pltpu.VMEM(shape, F32) for shape in shapes] + [dma((2, 4))],
        compiler_params=pltpu.CompilerParams(vmem_limit_bytes=FULL),
    )(new_disp, adj, shear.reshape(rows), grads.reshape(count))


def solution(mesh):
    grid = P("storey", "plate")
    return jax.shard_map(
        on_device,
        mesh=mesh,
        in_specs=(grid, grid, grid, grid, P(), grid, P("storey"), grid, grid, P("storey"), grid),
        out_specs=(grid, grid, P("storey"), P("storey")),
        check_vma=False,
    )
```

```python
import functools
import math

import jax
import jax.numpy as jnp
from jax import lax
from jax.experimental import pallas as pl
from jax.experimental.pallas import tpu as pltpu
from jax.sharding import PartitionSpec as P

ITERS = 6
KF = 5.0 / 9.0
CM = 2.16
CD = 1.1
HIGH = lax.Precision.HIGHEST
MESH = pl.DeviceIdType.MESH
F32 = jnp.float32
BF16 = jnp.bfloat16
LANES = 128
FULL = 63 * 1024 * 1024


def iota(shape, dim):
    return lax.broadcasted_iota(jnp.int32, shape, dim)


def to_row(col):
    n = col.shape[0]
    return jnp.sum(jnp.where(iota((n, n), 0) == iota((n, n), 1), col, 0.0), axis=0, keepdims=True)


def to_col(row):
    n = row.shape[1]
    return jnp.sum(jnp.where(iota((n, n), 0) == iota((n, n), 1), row, 0.0), axis=1, keepdims=True)


def split(value):
    hi = value.astype(BF16)
    return hi, (value - hi.astype(F32)).astype(BF16)


def wait_bytes(ref, sem):
    pltpu.make_async_copy(ref, ref, sem).wait()


def kernel(
    ns, np_,
    load_in, disp_in, mass_in, wall_in, cstiff, dmap_in, coef, tile_in, panel, owner, nidx,
    out_disp, out_adj, out_shear, out_grads,
    load, disp, mass, wall, dmap, tile, in_sem, out_sem, found,
    stiff, diag, rdiag, cm, place, x, r, q, z,
    k_own, k_up, k_down,
    t_hi, t_lo, tt_hi, tt_lo,
    pan_own, pan_left, pan_right, pan_force, grown, used, info_out, info_in,
    spk, sslots, snb, pslots, epk, extras, x_send, x_recv,
    g1, gpk, rpk, slots, nbs, rows_in, edge_tile,
    apk, fslots, tslots, gslots, seg,
    s_send, s_recv, n_send, n_recv, p_send, p_recv, i_send, i_recv,
    r_send, r_recv, rn_send, rn_recv, e_send, e_recv, a_send, a_recv,
):
    rows, cols = load.shape
    nodes = nidx.shape[1]
    order = nodes * np_
    count = coef.shape[0]
    width = spk.shape[1]
    pieces = cols // LANES
    s = lax.axis_index("storey")
    b = lax.axis_index("plate")
    has = (s > 0, s < ns - 1)
    beside = (s - 1, s + 1)
    miss = (1 - jnp.minimum(s, 1), 1 - jnp.minimum(ns - 1 - s, 1))
    toward = (jnp.maximum(s - 1, 0), jnp.minimum(s + 1, ns - 1))
    lands = tuple((1 - way) * (1 - miss[way]) + way * miss[way] for way in range(2))
    same = tuple((b + miss[way]) % np_ for way in range(2))

    ways = ((disp_in, disp), (wall_in, wall), (mass_in, mass), (dmap_in, dmap), (tile_in, tile), (load_in, load))
    loads = [pltpu.make_async_copy(src, dst, in_sem.at[i]) for i, (src, dst) in enumerate(ways)]
    loads.append(pltpu.make_async_copy(panel, pslots.at[b], in_sem.at[len(ways)]))
    for copy in loads:
        copy.start()

    barrier = pltpu.get_barrier_semaphore()
    for d in range(1, np_):
        pl.semaphore_signal(barrier, inc=1, device_id=(s, (b + d) % np_), device_id_type=MESH)
    for d in range(1, ns):
        pl.semaphore_signal(barrier, inc=1, device_id=((s + d) % ns, b), device_id_type=MESH)
    for way in range(2):
        @pl.when(has[way])
        def _():
            for d in range(1, np_):
                pl.semaphore_signal(barrier, inc=1, device_id=(beside[way], (b + d) % np_), device_id_type=MESH)
    sides = jnp.minimum(s, 1) + jnp.minimum(ns - 1 - s, 1)
    pl.semaphore_wait(barrier, np_ - 1 + ns - 1 + sides * (np_ - 1))

    def push(src, dst, send, recv, where):
        pltpu.make_async_remote_copy(
            src_ref=src, dst_ref=dst, send_sem=send, recv_sem=recv, device_id=where, device_id_type=MESH
        ).start()

    def to_plates(src, dst, send, recv):
        for d in range(1, np_):
            push(src, dst, send, recv, (s, (b + d) % np_))

    to_plates(panel, pslots.at[b], p_send, p_recv)

    at_own = nidx[...].astype(F32)
    tiled = (iota((nodes, order), 1) % nodes == iota((nodes, order), 0)).astype(F32)
    spk[2:3, 0:order] = jnp.dot(at_own, tiled, precision=HIGH, preferred_element_type=F32)
    loads[0].wait()
    spk[0:1, 0:cols] = disp[0:1, :]
    spk[1:2, 0:cols] = disp[rows - 1 : rows, :]
    spk[3:4, 0:rows] = to_row(disp[:, 0:1])
    spk[4:5, 0:rows] = to_row(disp[:, cols - 1 : cols])
    to_plates(spk, sslots.at[b], s_send, s_recv)
    for way in range(2):
        @pl.when(has[way])
        def _():
            push(spk, snb.at[1 - way], n_send.at[way], n_recv.at[1 - way], (beside[way], b))

        @pl.when(jnp.logical_not(has[way]))
        def _():
            snb[way] = jnp.zeros(snb.shape[1:], F32)
            for i in range(2):
                info_in[i, way] = jnp.zeros(info_in.shape[2:], F32)

    loads[1].wait()
    level = jnp.zeros((rows, cols), F32)
    for c in range(cstiff.shape[0]):
        level = jnp.where(wall[...] == c, cstiff[c], level)
    stiff[...] = KF * level
    loads[2].wait()
    cm[...] = CM * mass[...]
    loads[3].wait()

    def lookup(i, carry):
        part = pl.ds(pl.multiple_of(i * 8, 8), 8)
        ids = dmap[part, :]
        value = jnp.zeros(ids.shape, F32)
        for d in range(count):
            value = jnp.where(ids == d, coef[d], value)
        total = 4.0 * stiff[part, :] + cm[part, :] + CD * value
        diag[part, :] = total
        rdiag[part, :] = 1.0 / total
        return carry

    lax.fori_loop(0, rows // 8, lookup, 0)
    loads[4].wait()
    t_hi[...], t_lo[...] = split(tile[...])
    for i, at in enumerate((0, cols - 1)):
        edge_tile[0, i : i + 1, :] = to_row(tile[:, at : at + 1])
        edge_tile[1, i : i + 1, :] = tile[at : at + 1, :]

    loads[5].wait()
    loads[6].wait()
    sslots[b] = spk[...]
    wait_bytes(sslots.at[pl.ds(0, np_ - 1)], s_recv)
    wait_bytes(pslots.at[pl.ds(0, np_ - 1)], p_recv)
    for way in range(2):
        @pl.when(has[way])
        def _():
            wait_bytes(snb.at[way], n_recv.at[way])
            wait_bytes(spk, n_send.at[way])
    wait_bytes(sslots.at[pl.ds(0, np_ - 1)], s_send)
    wait_bytes(pslots.at[pl.ds(0, np_ - 1)], p_send)

    root = owner[0]
    used_now = jnp.zeros((order, order), F32)
    for j in range(np_):
        used_now = jnp.where(root == j, pslots[j], used_now)
    used[...] = used_now
    lane_node = iota((1, order), 1) // nodes
    shift = cols.bit_length() - 1
    tall = (rows, order)
    left_slot = jnp.maximum(b - 1, 0)
    right_slot = jnp.minimum(b + 1, np_ - 1)

    def places():
        where_all = jnp.zeros((1, order), F32)
        for j in range(np_):
            where_all = jnp.where(lane_node == j, sslots[j, 2:3, 0:order], where_all)
        at = where_all.astype(jnp.int32)
        return jnp.right_shift(at, shift), jnp.bitwise_and(at, cols - 1)

    def expand_columns(mode):
        at_row, _ = places()
        at_row_col = to_col(at_row.astype(F32)).astype(jnp.int32)
        wide = (order, np_ * rows)
        spread = (
            (iota(wide, 1) % rows == at_row_col) & (iota(wide, 1) // rows == iota(wide, 0) // nodes)
        ).astype(F32).astype(BF16)
        hi, lo = split(used[...].T if mode else used[...])
        both = jnp.dot(jnp.concatenate([hi, lo], axis=0), spread, preferred_element_type=F32)
        grown[...] = both[:order] + both[order:]

    def pick(mask):
        hi, lo = split(grown[...])
        ones = mask.astype(F32).astype(BF16)
        return jnp.dot(ones, hi, preferred_element_type=F32) + jnp.dot(ones, lo, preferred_element_type=F32)

    def expand_own(mode):
        at_row, at_col = places()
        mask = (iota(tall, 0) == at_row) & (lane_node == b)
        if mode == 0:
            col_of = jnp.sum(jnp.where(mask, (at_col + 1).astype(F32), 0.0), axis=1, keepdims=True)
            place[...] = (iota((rows, cols), 1) == col_of.astype(jnp.int32) - 1).astype(F32)
        own = pick(mask)
        pan_own[mode] = own
        if mode:
            own = own * jnp.sum(place[...] * stiff[...], axis=1, keepdims=True)
        info_out[mode, 0:1, 0 : np_ * rows] = own[0:1, :]
        info_out[mode, 1:2, 0 : np_ * rows] = own[rows - 1 : rows, :]
        info_out[mode, 2:3, 0:cols] = place[0:1, :]
        info_out[mode, 3:4, 0:cols] = place[rows - 1 : rows, :]
        for way in range(2):
            @pl.when(has[way])
            def _():
                push(
                    info_out.at[mode], info_in.at[mode, 1 - way], i_send.at[mode, way],
                    i_recv.at[mode, 1 - way], (beside[way], b),
                )

    def wait_info(mode):
        for way in range(2):
            @pl.when(has[way])
            def _():
                wait_bytes(info_in.at[mode, way], i_recv.at[mode, way])
                wait_bytes(info_out.at[mode], i_send.at[mode, way])

    def expand_sides(mode):
        at_row, at_col = places()
        at_h = iota(tall, 0) == at_row
        left = at_h & (lane_node == b - 1) & (at_col == cols - 1)
        right = at_h & (lane_node == b + 1) & (at_col == 0)
        if mode:
            pan_left[mode] = pick(left) * to_col(extras[left_slot][1:2, 0:rows])
            pan_right[mode] = pick(right) * to_col(extras[right_slot][0:1, 0:rows])
        else:
            pan_left[mode] = pick(left)
            pan_right[mode] = pick(right)

    expand_columns(0)
    expand_own(0)

    eye = (iota((rows, rows), 0) == iota((rows, rows), 1)).astype(F32)
    lane = iota((rows, cols), 1)
    line = iota((rows, cols), 0)

    def sideways(v):
        return jnp.where(lane == 0, 0.0, pltpu.roll(v, 1, 1)) + jnp.where(
            lane == cols - 1, 0.0, pltpu.roll(v, cols - 1, 1)
        )

    def neighbours(v, top, bottom, left, right):
        above = jnp.where(line == 0, top, pltpu.roll(v, 1, 0))
        below = jnp.where(line == rows - 1, bottom, pltpu.roll(v, rows - 1, 0))
        west = jnp.where(lane == 0, left, pltpu.roll(v, 1, 1))
        east = jnp.where(lane == cols - 1, right, pltpu.roll(v, cols - 1, 1))
        return above + below + west + east

    def reach(mode):
        spot = place[...]
        held = stiff[...] * spot if mode else spot
        scale = (lambda v: v) if mode else (lambda v: stiff[...] * v)
        k_own[mode] = scale(sideways(held)) - diag[...] * spot
        k_up[mode] = jnp.where(line == 0, 0.0, scale(pltpu.roll(held, 1, 0)))
        k_down[mode] = jnp.where(line == rows - 1, 0.0, scale(pltpu.roll(held, rows - 1, 0)))

    def force_panel():
        at_row, _ = places()
        at_h = iota(tall, 0) == at_row
        mix = jnp.zeros(tall, F32)
        for j in range(np_):
            mix = jnp.where(at_h & (lane_node == j), to_col(extras[j, 2:3, 0:rows]), mix)
        pan_force[0] = jnp.dot(mix, grown[...], precision=HIGH, preferred_element_type=F32)

    def send_round(mode, par, edges):
        resid = r[...]
        scaled = resid * rdiag[...]
        g1[par] = to_row(jnp.sum(resid * place[...], axis=1, keepdims=True))
        gpk[par, 0:1, :] = g1[par]
        if edges:
            for i, at in enumerate((0, cols - 1)):
                value = x[:, at : at + 1] + jnp.sum(scaled * edge_tile[mode, i : i + 1, :], axis=1, keepdims=True)
                gpk[par, 1 + i : 2 + i, :] = to_row(value * stiff[:, at : at + 1] if mode else value)
        to_plates(gpk.at[par], slots.at[par, b], r_send.at[par], r_recv.at[par])
        for way in range(2):
            for d in range(np_):
                if d:
                    plate, slot = (b + d) % np_, b
                else:
                    plate, slot = same[way], same[way]
                push(g1.at[par], nbs.at[par, lands[way], slot], rn_send.at[par], rn_recv.at[par], (toward[way], plate))
        slots[par, b] = gpk[par]
        hi, lo = split(scaled)
        wh, wl = (tt_hi, tt_lo) if mode else (t_hi, t_lo)
        both = jnp.dot(jnp.concatenate([hi, lo], axis=0), wh[...], preferred_element_type=F32)
        band = both[:rows] + both[rows:] + jnp.dot(hi, wl[...], preferred_element_type=F32)
        total = x[...] + band
        z[...] = total
        if not edges:
            return
        first, last = total[0:1, :], total[rows - 1 : rows, :]
        if mode:
            first, last = first * stiff[0:1, :], last * stiff[rows - 1 : rows, :]
        for t in range(pieces):
            rpk[par, 0, t : t + 1, :] = first[:, t * LANES : (t + 1) * LANES]
            rpk[par, 1, t : t + 1, :] = last[:, t * LANES : (t + 1) * LANES]
        for way in range(2):
            push(rpk.at[par, way], rows_in.at[par, lands[way]], e_send.at[par], e_recv.at[par], (toward[way], same[way]))

    def wait_plates(par):
        wait_bytes(slots.at[par, pl.ds(0, np_ - 1)], r_recv.at[par])

    def wait_storeys(par, edges):
        wait_bytes(nbs.at[par], rn_recv.at[par])
        if edges:
            wait_bytes(rows_in.at[par], e_recv.at[par])
            wait_bytes(rows_in.at[par], e_send.at[par])
        wait_bytes(slots.at[par, pl.ds(0, np_ - 1)], r_send.at[par])
        wait_bytes(nbs.at[par], rn_send.at[par])

    def applied(mat, mode, par, extra=None):
        total = extra
        for j in range(np_):
            term = mat[mode, :, j * rows : (j + 1) * rows] * slots[par, j, 0:1, :]
            total = term if total is None else total + term
        return jnp.sum(total, axis=1, keepdims=True)

    def finish(mode, par):
        coarse = jnp.broadcast_to(applied(pan_own, mode, par), (rows, LANES))
        for t in range(pieces):
            part = slice(t * LANES, (t + 1) * LANES)
            x[:, part] = z[:, part] + coarse * place[:, part]
        return coarse

    def side_row(mode, par, way):
        pan_row = 1 - way
        total = jnp.zeros((1, rows), F32)
        for j in range(np_):
            total = total + info_in[mode, way, pan_row : pan_row + 1, j * rows : (j + 1) * rows] * nbs[par, way, j, 0:1, :]
        value = jnp.sum(total, axis=1, keepdims=True)
        got = jnp.concatenate([rows_in[par, way, t : t + 1, :] for t in range(pieces)], axis=1)
        got = jnp.where(has[way], got, 0.0)
        return got + value * info_in[mode, way, 2 + (1 - way) : 3 + (1 - way), 0:cols]

    def inner_resid(mode, base):
        v = z[...]
        zero = jnp.zeros((), F32)
        if mode:
            r[...] = base[...] - diag[...] * v + neighbours(stiff[...] * v, zero, zero, zero, zero)
        else:
            r[...] = base[...] - diag[...] * v + stiff[...] * neighbours(v, zero, zero, zero, zero)

    def outer_resid(mode, par, coarse):
        up, down = pltpu.roll(coarse, 1, 0), pltpu.roll(coarse, rows - 1, 0)
        west = jnp.where(b > 0, slots[par, left_slot, 2:3, :], 0.0)
        east = jnp.where(b < np_ - 1, slots[par, right_slot, 1:2, :], 0.0)
        west = applied(pan_left, mode, par, eye * west)
        east = applied(pan_right, mode, par, eye * east)
        thin = iota((rows, LANES), 1)
        for t in range(pieces):
            part = slice(t * LANES, (t + 1) * LANES)
            total = r[:, part] + coarse * k_own[mode, :, part]
            total = total + up * k_up[mode, :, part] + down * k_down[mode, :, part]
            if t == 0:
                total = total + jnp.where(thin == 0, west if mode else west * stiff[:, part], 0.0)
            if t == pieces - 1:
                total = total + jnp.where(thin == LANES - 1, east if mode else east * stiff[:, part], 0.0)
            r[:, part] = total

    def edge_resid(mode, par):
        top, bottom = side_row(mode, par, 0), side_row(mode, par, 1)
        if mode == 0:
            top, bottom = top * stiff[0:1, :], bottom * stiff[rows - 1 : rows, :]
        r[0:1, :] = r[0:1, :] + top
        r[rows - 1 : rows, :] = r[rows - 1 : rows, :] + bottom

    x[...] = disp[...]
    west = jnp.where(b > 0, to_col(sslots[left_slot][4:5, 0:rows]), 0.0)
    east = jnp.where(b < np_ - 1, to_col(sslots[right_slot][3:4, 0:rows]), 0.0)
    around = neighbours(disp[...], snb[0, 1:2, 0:cols], snb[1, 0:1, 0:cols], west, east)
    r[...] = load[...] - (diag[...] * disp[...] - stiff[...] * around)

    def primal(k, carry):
        par = lax.rem(k, 2)
        send_round(0, par, True)

        @pl.when(k == 0)
        def _():
            expand_sides(0)
            reach(0)
            epk[0:1, :] = to_row(stiff[:, 0:1])
            epk[1:2, :] = to_row(stiff[:, cols - 1 : cols])
            epk[2:3, :] = to_row(jnp.sum(place[...] * cm[...], axis=1, keepdims=True))
            to_plates(epk, extras.at[b], x_send, x_recv)
            extras[b] = epk[...]

        @pl.when(k == 1)
        def _():
            wait_bytes(extras.at[pl.ds(0, np_ - 1)], x_recv)
            wait_bytes(extras.at[pl.ds(0, np_ - 1)], x_send)
            force_panel()
            expand_columns(1)
            expand_own(1)

        @pl.when(k == 2)
        def _():
            expand_sides(1)
            reach(1)

        @pl.when(k == 3)
        def _():
            tt_hi[...], tt_lo[...] = split(tile[...].T)

        inner_resid(0, load)
        wait_plates(par)

        @pl.when(k == 0)
        def _():
            wait_info(0)

        outer_resid(0, par, finish(0, par))
        wait_storeys(par, True)
        edge_resid(0, par)
        return carry

    lax.fori_loop(0, ITERS - 1, primal, 0)
    par = (ITERS - 1) % 2
    send_round(0, par, False)
    apk[0, 0:1, :] = to_row(jnp.sum(cm[...] * z[...], axis=1, keepdims=True))
    to_plates(apk.at[0], fslots.at[b], a_send.at[0], a_recv.at[0])
    fslots[b] = apk[0]
    wait_info(1)
    wait_plates(par)
    wait_bytes(fslots.at[pl.ds(0, np_ - 1)], a_recv.at[0])
    wait_bytes(fslots.at[pl.ds(0, np_ - 1)], a_send.at[0])

    force = fslots[0, 0:1, :]
    for j in range(1, np_):
        force = force + fslots[j, 0:1, :]
    force = to_row(applied(pan_force, 0, par, eye * force))
    force = force * (8.0 / math.sqrt(cols * np_ * rows * ns))
    apk[1, 0:1, :] = force
    for d in range(1, ns):
        push(apk.at[1], tslots.at[s], a_send.at[1], a_recv.at[1], ((s + d) % ns, b))
    tslots[s] = apk[1]
    wait_storeys(par, False)
    finish(0, par)
    found[...] = x[...]
    give_disp = pltpu.make_async_copy(found, out_disp, out_sem.at[0])
    give_disp.start()
    wait_bytes(tslots.at[pl.ds(0, ns - 1)], a_recv.at[1])
    wait_bytes(tslots.at[pl.ds(0, ns - 1)], a_send.at[1])
    over = jnp.zeros((1, rows), F32)
    under = jnp.zeros((1, rows), F32)
    weight = (iota((1, rows), 1) + 1).astype(F32)
    for j in range(ns):
        line_j = tslots[j, 0:1, :]
        over = over + jnp.where(s < j, line_j, 0.0)
        under = under + line_j * (jnp.where(s > j, weight, 0.0) + (rows * jnp.minimum(s, j)).astype(F32))
    over = jnp.sum(over, axis=1, keepdims=True)
    under = jnp.sum(under, axis=1, keepdims=True)
    hh, ll = iota((rows, rows), 0), iota((rows, rows), 1)
    shear = jnp.sum(jnp.where(ll >= hh, force, 0.0), axis=1, keepdims=True) + over
    out_shear[...] = to_row(shear)
    local = jnp.sum(force * (jnp.minimum(hh, ll) + 1).astype(F32), axis=1, keepdims=True)
    step = (iota((rows, 1), 0) + 1).astype(F32)
    drift = (local + step * over + under) * (1.0 / (rows * ns))
    q[...] = cm[...] * drift
    r[...] = q[...]
    x[...] = jnp.zeros((rows, cols), F32)

    def adjoint(k, carry):
        par = lax.rem(k, 2)
        send_round(1, par, True)
        inner_resid(1, q)
        wait_plates(par)
        outer_resid(1, par, finish(1, par))
        wait_storeys(par, True)
        edge_resid(1, par)
        return carry

    lax.fori_loop(0, ITERS - 1, adjoint, 0)
    send_round(1, par, False)

    q[...] = z[...] * found[...]
    group = 8
    for first in range(0, count, group):
        def gather(i, accs):
            part = pl.ds(pl.multiple_of(i * 8, 8), 8)
            ids, vals = dmap[part, :], q[part, :]
            res = []
            for d in range(group):
                kept = jnp.where(ids == first + d, vals, 0.0)
                acc = accs[d]
                for t in range(pieces):
                    acc = acc + kept[:, t * LANES : (t + 1) * LANES]
                res.append(acc)
            return tuple(res)

        accs = lax.fori_loop(0, rows // 8, gather, tuple(jnp.zeros((8, LANES), F32) for _ in range(group)))
        for d in range(group):
            seg[first + d : first + d + 1, :] = jnp.sum(accs[d], axis=0, keepdims=True)
    sums = to_row(jnp.sum(seg[...], axis=1, keepdims=True))
    damper = jnp.sum(place[...] * dmap[...].astype(F32), axis=1, keepdims=True)
    held = jnp.sum(place[...] * found[...], axis=1, keepdims=True)
    hits = jnp.where(damper == iota((rows, count), 1).astype(F32), held, 0.0)
    wait_plates(par)
    coarse = finish(1, par)
    give_adj = pltpu.make_async_copy(x, out_adj, out_sem.at[1])
    give_adj.start()
    sums = sums + jnp.sum(hits * coarse[:, 0:count], axis=0, keepdims=True)
    apk[2, 0:1, 0:count] = sums
    to_plates(apk.at[2], gslots.at[b], a_send.at[2], a_recv.at[2])
    gslots[b] = apk[2]
    wait_storeys(par, False)
    wait_bytes(gslots.at[pl.ds(0, np_ - 1)], a_recv.at[2])
    wait_bytes(gslots.at[pl.ds(0, np_ - 1)], a_send.at[2])
    sums = gslots[0, 0:1, 0:count]
    for j in range(1, np_):
        sums = sums + gslots[j, 0:1, 0:count]
    out_grads[...] = sums * (-CD * 64.0 / math.sqrt(rows * cols * np_ / count))
    give_disp.wait()
    give_adj.wait()


def deliver(*refs):
    source, target, room, sems = refs[:4], refs[4:8], refs[8:12], refs[12]
    ins = [pltpu.make_async_copy(source[i], room[i], sems.at[0, i]) for i in range(4)]
    outs = [pltpu.make_async_copy(room[i], target[i], sems.at[1, i]) for i in range(4)]
    for copy in ins:
        copy.start()
    for i in range(4):
        ins[i].wait()
        outs[i].start()
    for copy in outs:
        copy.wait()


def on_device(load, disp, mass, wall_class, class_stiff, damper_map, damper_coef, band_tile, panel_store, owner, node_index):
    rows, cols = load.shape
    ns = lax.axis_size("storey")
    np_ = lax.axis_size("plate")
    nodes = node_index.shape[1]
    order = nodes * np_
    count = damper_coef.shape[0]
    width = max(cols, order, rows)
    wide = max(cols, np_ * rows)
    field = pltpu.VMEM((rows, cols), F32)
    square = pltpu.VMEM((cols, cols), BF16)
    grown = pltpu.VMEM((2, rows, np_ * rows), F32)
    dma = pltpu.SemaphoreType.DMA
    vmem = pl.BlockSpec(memory_space=pltpu.VMEM)
    smem = pl.BlockSpec(memory_space=pltpu.SMEM)
    hbm = pl.BlockSpec(memory_space=pltpu.HBM)
    ids = pltpu.VMEM((rows, cols), jnp.int32)
    shapes = ((rows, cols), (rows, cols), (rows,), (count,))
    new_disp, adj, shear, grads = pl.pallas_call(
        functools.partial(kernel, ns, np_),
        out_shape=(
            jax.ShapeDtypeStruct((rows, cols), F32),
            jax.ShapeDtypeStruct((rows, cols), F32),
            jax.ShapeDtypeStruct((1, rows), F32),
            jax.ShapeDtypeStruct((1, count), F32),
        ),
        in_specs=[hbm, hbm, hbm, hbm, smem, hbm, smem, hbm, hbm, smem, vmem],
        out_specs=(hbm, hbm, vmem, vmem),
        scratch_shapes=[field] * 3
        + [ids] * 2
        + [pltpu.VMEM((cols, cols), F32), dma((7,)), dma((2,)), field]
        + [field] * 9
        + [pltpu.VMEM((2, rows, cols), F32)] * 3
        + [square] * 4
        + [grown] * 3
        + [
            pltpu.VMEM((1, rows, np_ * rows), F32),
            pltpu.VMEM((order, np_ * rows), F32),
            pltpu.VMEM((order, order), F32),
            pltpu.VMEM((2, 8, wide), F32),
            pltpu.VMEM((2, 2, 8, wide), F32),
            pltpu.VMEM((8, width), F32),
            pltpu.VMEM((np_, 8, width), F32),
            pltpu.VMEM((2, 8, width), F32),
            pltpu.VMEM((np_, order, order), F32),
            pltpu.VMEM((8, LANES), F32),
            pltpu.VMEM((np_, 8, LANES), F32),
            dma,
            dma,
            pltpu.VMEM((2, 1, LANES), F32),
            pltpu.VMEM((2, 4, LANES), F32),
            pltpu.VMEM((2, 2, cols // LANES, LANES), F32),
            pltpu.VMEM((2, np_, 4, LANES), F32),
            pltpu.VMEM((2, 2, np_, 1, LANES), F32),
            pltpu.VMEM((2, 2, cols // LANES, LANES), F32),
            pltpu.VMEM((2, 8, cols), F32),
            pltpu.VMEM((3, 1, LANES), F32),
            pltpu.VMEM((np_, 1, LANES), F32),
            pltpu.VMEM((ns, 1, LANES), F32),
            pltpu.VMEM((np_, 1, LANES), F32),
            pltpu.VMEM((count, LANES), F32),
            dma, dma, dma((2,)), dma((2,)), dma, dma, dma((2, 2)), dma((2, 2)),
            *[dma((2,))] * 6, dma((3,)), dma((3,)),
        ],
        compiler_params=pltpu.CompilerParams(
            collective_id=0, has_side_effects=True, vmem_limit_bytes=FULL
        ),
    )(load, disp, mass, wall_class, class_stiff, damper_map, damper_coef, band_tile, panel_store, owner, node_index)
    return pl.pallas_call(
        deliver,
        out_shape=tuple(jax.ShapeDtypeStruct(shape, F32) for shape in shapes),
        in_specs=[hbm] * 4,
        out_specs=(hbm,) * 4,
        scratch_shapes=[pltpu.VMEM(shape, F32) for shape in shapes] + [dma((2, 4))],
        compiler_params=pltpu.CompilerParams(vmem_limit_bytes=FULL),
    )(new_disp, adj, shear.reshape(rows), grads.reshape(count))


def solution(mesh):
    grid = P("storey", "plate")
    return jax.shard_map(
        on_device,
        mesh=mesh,
        in_specs=(grid, grid, grid, grid, P(), grid, P("storey"), grid, grid, P("storey"), grid),
        out_specs=(grid, grid, P("storey"), P("storey")),
        check_vma=False,
    )
```
